256 devices in a mesh: member: 8 (over y, core), lon: 16 (over z, x_lo), lat: 2 (over x_hi).
Axes of the slice: x: 4 (x_hi: 2, x_lo: 2; x = x_hi * 2 + x_lo), y: 4, z: 8, core: 2. Of those that a mesh axis runs over, the one named last changes fastest.
Arguments:
- member_state: float32 [8, 16, 256, 6144], P('member', None, 'lat', 'lon'), may hold values from -12 to 12
- column_depth: float32 [256, 6144], P('lat', 'lon'), may hold values from 0.5 to 2
- rotation: float32 [256, 6144], P('lat', 'lon'), may hold values from -0.2 to 0.2
- diffusivity: float32 [5, 256, 6144], P(None, 'lat', 'lon'), may hold values from 0.02 to 0.2
- ocean_mask: int32 [256, 6144], P('lat', 'lon'), may hold values from 0 to 1, as said below
- region_id: int32 [256, 6144], P('lat', 'lon'), may hold values from 0 to 15, as said below
- target_rms: float32 [16], replicated, may hold values from 0.2 to 1
Outputs:
- bred_state: float32 [8, 16, 256, 6144], P('member', None, 'lat', 'lon')
- growth_rms: float32 [8, 16], P('member')
The draws below stay inside these ranges and needn't reach their ends.
Inputs may be any that keep to these rules, and one draw needn't show every extreme that they name: `ocean_mask`: 1 marks an ocean cell. `region_id`: every region id holds ocean cells.
All inputs are finite; a program needn't handle non-finite values.
Results may differ from the reference program's by a relative error of at most 0.0003.
Values sent between devices are 32-bit elements; how exact they have to be, the bound alone decides.
No kernel may reach another device: no remote copies, remote signals or barrier semaphores. Data moves between devices by JAX's collectives and lax.ppermute only.
A program may use at most 64 MiB of HBM per device.

```python
import math
import jax
import jax.numpy as jnp
from jax import lax

LEV = 5
STEPS = 2
SECTORS = 8
MEMBERS = 8
CHANNELS = 16
REGIONS = 16
NLAT = 256
NLON = 6144


def draw_member_state(key, part):
    keys = jax.random.split(key, 2)
    shape = (MEMBERS, CHANNELS, NLAT, NLON)
    ramp = jnp.exp(math.log(3.0) * jnp.arange(NLON).astype(jnp.float32) / NLON)[None, None, None, :]
    rows = jnp.exp(jax.random.uniform(keys[0], (1, 1, NLAT, 1), jnp.float32, 0.0, math.log(3.3)))
    scale = 0.3 * rows * ramp
    return jax.random.truncated_normal(keys[1], -4.0, 4.0, shape, jnp.float32) * scale


def draw_ocean_mask(key, part):
    coins = jax.random.randint(key, (NLAT, NLON), 0, 4)
    rows = jnp.arange(NLAT)[:, None]
    ocean = jnp.where(coins > 0, 1, 0)
    edge = (rows == 0) | (rows == NLAT - 1)
    return jnp.where(edge, 1, ocean).astype(jnp.int32)


def draw_region_id(key, part):
    keys = jax.random.split(key, 2)
    offset = jax.random.randint(keys[0], (NLAT, 1), 0, SECTORS)
    columns = jnp.arange(NLON)[None, :]
    block_width = max(NLON // (4 * SECTORS), 1)
    sector = (columns // block_width + offset) % SECTORS
    bound = jax.random.randint(keys[1], (1, NLON), NLAT // 4, 3 * NLAT // 4 + 1)
    rows = jnp.arange(NLAT)[:, None]
    return (sector * 2 + jnp.where(rows >= bound, 1, 0)).astype(jnp.int32)


def block_scale(own_key, dims, cuts, low, top_value):
    level, own = 1.0, jax.random.fold_in(own_key, 6)
    for dim, shards_of in cuts:
        steps = jnp.exp(jax.random.uniform(jax.random.fold_in(own, dim), (shards_of,), jnp.float32, low / len(cuts), top_value / len(cuts)))
        level = level * jnp.repeat(steps, dims[dim] // shards_of).reshape([-1 if axis == dim else 1 for axis in range(len(dims))])
    return level


def setup_inputs(seed: int = 0) -> dict:
    key_list = jax.random.split(jax.random.key(seed), 8)
    return {
        "member_state": draw_member_state(jax.random.fold_in(key_list[7], 71), 0),
        "column_depth": jnp.clip(jnp.exp(math.log(2.0) - 1.3862944 * jax.random.uniform(key_list[1], (NLAT, NLON), jnp.float32) ** block_scale(key_list[1], (NLAT, NLON), ((0, 2), (1, 16)), -0.2, 0.2)), 0.5, 2.0),
        "rotation": jnp.clip(jax.random.uniform(key_list[2], (NLAT, NLON), jnp.float32, -0.2, 0.2) * block_scale(key_list[2], (NLAT, NLON), ((0, 2), (1, 16)), -0.4, 0.0), -0.2, 0.2),
        "diffusivity": jnp.clip(jnp.exp(math.log(0.2) - 2.3025851 * jax.random.uniform(key_list[3], (LEV, NLAT, NLON), jnp.float32) ** block_scale(key_list[3], (LEV, NLAT, NLON), ((1, 2), (2, 16)), -0.2, 0.2)), 0.02, 0.2),
        "ocean_mask": draw_ocean_mask(jax.random.fold_in(key_list[7], 71), 0),
        "region_id": draw_region_id(jax.random.fold_in(key_list[7], 71), 0),
        "target_rms": jnp.clip(jnp.exp(jax.random.uniform(key_list[6], (REGIONS,), jnp.float32, math.log(0.2), math.log(1.0))), 0.2, 1.0),
    }


divergence_gain = 0.25
pressure_gain = 0.25
buoyancy_gain = 0.1
advection_gain = 0.05
epsilon = 1e-06

def neighbours(field):
    east_side = jnp.roll(field, -1, axis=-1)
    west_side = jnp.roll(field, 1, axis=-1)
    zero_row = jnp.zeros_like(field[..., :1, :])
    north_side = jnp.concatenate([field[..., 1:, :], zero_row], axis=-2)
    south_side = jnp.concatenate([zero_row, field[..., :-1, :]], axis=-2)
    return (east_side, west_side, north_side, south_side)

def advance(state, column_depth, rotation, diffusivity, ocean_float):
    east_side, west_side, north_side, south_side = neighbours(state)
    zonal_diff = east_side - west_side
    merid_diff = north_side - south_side
    laplacian = east_side + west_side + north_side + south_side - 4.0 * state
    surface = state[:, 0]
    zonal_flow = state[:, 1:1 + LEV]
    merid_flow = state[:, 1 + LEV:1 + 2 * LEV]
    heat_field = state[:, 1 + 2 * LEV:]
    divergence = lax.optimization_barrier(jnp.mean(zonal_diff[:, 1:1 + LEV], axis=1)) + lax.optimization_barrier(jnp.mean(merid_diff[:, 1 + LEV:1 + 2 * LEV], axis=1))
    new_surface = ocean_float * (surface - divergence_gain * column_depth * divergence)
    s_east, s_west, s_north, s_south = neighbours(new_surface)
    slope_east = (s_east - s_west)[:, None]
    slope_north = (s_north - s_south)[:, None]
    heat_east = zonal_diff[:, 1 + 2 * LEV:]
    heat_north = merid_diff[:, 1 + 2 * LEV:]
    new_zonal = ocean_float * (zonal_flow + rotation * merid_flow - pressure_gain * slope_east - buoyancy_gain * heat_east + diffusivity * laplacian[:, 1:1 + LEV])
    new_merid = ocean_float * (merid_flow - rotation * zonal_flow - pressure_gain * slope_north - buoyancy_gain * heat_north + diffusivity * laplacian[:, 1 + LEV:1 + 2 * LEV])
    new_heat = ocean_float * (heat_field + diffusivity * laplacian[:, 1 + 2 * LEV:] - advection_gain * (new_zonal * heat_east + new_merid * heat_north))
    return jnp.concatenate([new_surface[:, None], new_zonal, new_merid, new_heat], axis=1)

def reference(member_state, column_depth, rotation, diffusivity, ocean_mask, region_id, target_rms):
    ocean_float = ocean_mask.astype(jnp.float32)
    state = member_state
    for step_index in range(STEPS):
        state = advance(state, column_depth, rotation, diffusivity, ocean_float)
    control = state[0:1]
    difference = state - control
    cell_sum = ocean_float * lax.optimization_barrier(jnp.sum(difference * difference, axis=1))
    labels = jnp.arange(REGIONS).astype(jnp.int32)
    onehot = (region_id[None] == labels[:, None, None]).astype(jnp.float32)
    squares = jnp.einsum('rji,mji->mr', onehot, cell_sum, precision=lax.Precision.HIGHEST)
    counts = jnp.einsum('rji,ji->r', onehot, ocean_float, precision=lax.Precision.HIGHEST)
    growth = jnp.sqrt(squares / (counts * CHANNELS) + epsilon)
    factor = target_rms[None] / growth
    cell_factor = jnp.einsum('mr,rji->mji', factor, onehot, precision=lax.Precision.HIGHEST)
    bred = control + cell_factor[:, None] * difference
    return (bred, growth)
```

```python
import functools
import jax
import jax.numpy as jnp
from jax import lax
from jax.experimental import pallas as pl
from jax.experimental.pallas import tpu as pltpu
from jax.sharding import PartitionSpec as P

LEV = 5
CH = 16
FIELDS = 24
REGIONS = 16
ROWS, COLS = 128, 384
ROWS_X, COLS_X = 136, 512
HALO = 4
EPSILON = 1e-06
VMEM = pl.BlockSpec(memory_space=pltpu.VMEM)
ANY = pl.BlockSpec(memory_space=pl.ANY)
SMEM = pl.BlockSpec(memory_space=pltpu.SMEM)
F32 = jnp.float32


def call(kernel, out, in_specs, out_specs, scratch=(), flops=1 << 22, nbytes=1 << 23):
    return pl.pallas_call(
        kernel,
        out_shape=out,
        in_specs=in_specs,
        out_specs=out_specs,
        scratch_shapes=list(scratch),
        compiler_params=pltpu.CompilerParams(vmem_limit_bytes=48 << 20),
        cost_estimate=pl.CostEstimate(flops=flops, bytes_accessed=nbytes, transcendentals=0),
    )


def iota(shape, dim):
    return lax.broadcasted_iota(jnp.int32, shape, dim)


def pack_kernel(lat, state, depth, rotation, diff, mask, west, east, rows, c_west, c_east):
    def field(k, r, c):
        if k < CH:
            return state[k, r, c]
        if k == CH:
            return depth[r, c]
        if k == CH + 1:
            return rotation[r, c]
        if k < CH + 2 + LEV:
            return diff[k - CH - 2, r, c]
        return mask[r, c].astype(F32)

    lane = iota((ROWS, 128), 1)
    full = slice(0, ROWS)
    w = jnp.zeros((ROWS, 128), F32)
    e = jnp.zeros((ROWS, 128), F32)
    for k in range(FIELDS):
        own = (lane >= HALO * k) & (lane < HALO * k + HALO)
        a = field(k, full, slice(0, 128))
        b = field(k, full, slice(COLS - 128, COLS))
        w = jnp.where(own, pltpu.roll(a, HALO * k, 1) if k else a, w)
        e = jnp.where(own, pltpu.roll(b, HALO * k + HALO, 1), e)
    west[...] = w
    east[...] = e
    upper = lat[0] == 0
    r0 = pl.multiple_of(jnp.where(upper, ROWS - 8, 0), 8)
    tile = pl.ds(r0, 8)
    c_west[...] = west[tile, :]
    c_east[...] = east[tile, :]
    sub = iota((8, COLS), 0)
    mine = (sub >= 4) == upper
    half = FIELDS // 2
    for k in range(half):
        x = field(k, tile, slice(0, COLS))
        y = field(k + half, tile, slice(0, COLS))
        rows[8 * k : 8 * k + 8, :] = jnp.where(mine, x, pltpu.roll(y, 4, 0))


def pack(lat, state, statics):
    shapes = [(ROWS, 128), (ROWS, 128), (FIELDS * 4, COLS), (8, 128), (8, 128)]
    return call(
        pack_kernel,
        [jax.ShapeDtypeStruct(s, F32) for s in shapes],
        [SMEM] + [VMEM] * 5,
        [VMEM] * 5,
    )(lat, state, *statics)


def exchange(west, east, rows, c_west, c_east):
    n = lax.axis_size("lon")
    up = [(i, (i + 1) % n) for i in range(n)]
    down = [((i + 1) % n, i) for i in range(n)]
    other = [(0, 1), (1, 0)]
    both = ("lon", "lat")
    up2 = [(2 * i + j, 2 * k + 1 - j) for i, k in up for j in range(2)]
    down2 = [(2 * i + j, 2 * k + 1 - j) for i, k in down for j in range(2)]
    return (
        lax.ppermute(east, "lon", up),
        lax.ppermute(west, "lon", down),
        lax.ppermute(rows, "lat", other),
        lax.ppermute(c_east, both, up2),
        lax.ppermute(c_west, both, down2),
    )


def fill_halo(x, count, half, lat, from_west, from_east, rows, c_west, c_east):
    def margin(k, w, e):
        lane = iota(w.shape, 1)
        s = (128 - HALO * k) % 128
        e = pltpu.roll(e, s, 1) if s else e
        return jnp.where(lane < 64, e, pltpu.roll(w, (124 - HALO * k) % 128, 1))

    sub = iota((8, COLS), 0)
    got = (sub < 4) == (lat[0] == 0)
    got_c = got[:, :128]
    w, e = from_west[...], from_east[...]
    cw, ce = c_west[...], c_east[...]
    for k in range(count):
        x[k, 0:ROWS, COLS:COLS_X] = margin(k, w, e)
        j = k % half
        tile = rows[8 * j : 8 * j + 8, :]
        if k >= half:
            tile = pltpu.roll(tile, 4, 0)
        x[k, ROWS:ROWS_X, 0:COLS] = jnp.where(got, tile, 0.0)
        x[k, ROWS:ROWS_X, COLS:COLS_X] = jnp.where(got_c, margin(k, cw, ce), 0.0)


TILES = ROWS_X // 8


def tile_at(t):
    return pl.ds(pl.multiple_of(t * 8, 8), 8)


def step(x, static, ub, vb, h2, store, tiles):
    sub = iota((8, COLS_X), 0)

    def around(t):
        return tile_at(jnp.where(t == 0, TILES - 1, t - 1)), tile_at(t), tile_at(jnp.where(t == TILES - 1, 0, t + 1))

    def north(cur, nxt):
        return pltpu.roll(jnp.where(sub == 0, nxt, cur), 7, 0)

    def south(cur, prv):
        return pltpu.roll(jnp.where(sub == 7, prv, cur), 1, 0)

    def east(cur):
        return pltpu.roll(cur, COLS_X - 1, 1)

    def west(cur):
        return pltpu.roll(cur, 1, 1)

    def sums(t, _):
        c = tile_at(t)
        u = x[1, c, :]
        v = x[1 + LEV, c, :]
        for l in range(1, LEV):
            u = u + x[1 + l, c, :]
            v = v + x[1 + LEV + l, c, :]
        ub[c, :] = east(u) - west(u)
        vb[c, :] = v
        return 0

    lax.fori_loop(0, TILES, sums, 0)

    def surface(t, _):
        p, c, n = around(t)
        v = vb[c, :]
        div = ub[c, :] + (north(v, vb[n, :]) - south(v, vb[p, :]))
        h2[c, :] = static[7, c, :] * (x[0, c, :] - (0.25 / LEV) * static[0, c, :] * div)
        return 0

    lax.fori_loop(0, TILES, surface, 0)

    def rest(t, _):
        p, c, n = around(t)
        oc = static[7, c, :]
        rot = static[1, c, :]
        h = h2[c, :]
        store(0, c, h)
        px = 0.25 * (east(h) - west(h))
        py = 0.25 * (north(h, h2[n, :]) - south(h, h2[p, :]))
        for l in range(LEV):
            k = static[2 + l, c, :]

            def near(ch):
                q = x[ch, c, :]
                return q, east(q), west(q), north(q, x[ch, n, :]), south(q, x[ch, p, :])

            q, e, w, a, b = near(1 + 2 * LEV + l)
            cx = e - w
            cy = a - b
            c0 = q + k * ((e + w) + (a + b) - 4.0 * q)
            u, e, w, a, b = near(1 + l)
            lap_u = (e + w) + (a + b) - 4.0 * u
            v, e, w, a, b = near(1 + LEV + l)
            lap_v = (e + w) + (a + b) - 4.0 * v
            u2 = oc * (u + rot * v - px - 0.1 * cx + k * lap_u)
            v2 = oc * (v - rot * u - py - 0.1 * cy + k * lap_v)
            store(1 + l, c, u2)
            store(1 + LEV + l, c, v2)
            store(1 + 2 * LEV + l, c, oc * (c0 - 0.05 * (u2 * cx + v2 * cy)))
        return 0

    lax.fori_loop(0, tiles, rest, 0)


def two_steps(x, static, y, ub, vb, h2, out):
    def keep(ch, c, value):
        y[ch, c, :] = value

    def give(ch, c, value):
        out[ch, c, :] = value[:, :COLS]

    step(x, static, ub, vb, h2, keep, TILES)
    step(y, static, ub, vb, h2, give, ROWS // 8)


STEP_SCRATCH = [
    pltpu.VMEM((CH, ROWS_X, COLS_X), F32),
    pltpu.VMEM((ROWS_X, COLS_X), F32),
    pltpu.VMEM((ROWS_X, COLS_X), F32),
    pltpu.VMEM((ROWS_X, COLS_X), F32),
]


def own_kernel(lat, state, depth, rotation, diff, mask, fw, fe, rows, cw, ce, out, x, y, ub, vb, h2, sem):
    main = (slice(0, ROWS), slice(0, COLS))
    copies = [
        pltpu.make_async_copy(state, x.at[(slice(0, CH),) + main], sem.at[0]),
        pltpu.make_async_copy(depth, x.at[(CH,) + main], sem.at[1]),
        pltpu.make_async_copy(rotation, x.at[(CH + 1,) + main], sem.at[2]),
        pltpu.make_async_copy(diff, x.at[(slice(CH + 2, CH + 2 + LEV),) + main], sem.at[3]),
    ]
    for copy in copies:
        copy.start()
    x[(FIELDS - 1,) + main] = mask[...].astype(F32)
    fill_halo(x, FIELDS, FIELDS // 2, lat, fw, fe, rows, cw, ce)
    for copy in copies:
        copy.wait()
    two_steps(x, x.at[CH:FIELDS], y, ub, vb, h2, out)


def own_steps(lat, state, statics, halos):
    return call(
        own_kernel,
        jax.ShapeDtypeStruct((CH, ROWS, COLS), F32),
        [SMEM] + [ANY] * 4 + [VMEM] * 6,
        VMEM,
        [pltpu.VMEM((FIELDS, ROWS_X, COLS_X), F32)] + STEP_SCRATCH + [pltpu.SemaphoreType.DMA((4,))],
        flops=1 << 28,
    )(lat, state, *statics, *halos)


def broadcast(state):
    m = lax.axis_index("member")
    a, b = state[: CH // 2], state[CH // 2 :]

    def send(value, pairs):
        return lax.ppermute(value, "member", pairs)

    first = m == 0
    p1 = send(a, [(0, 2)])
    m1 = send(b, [(0, 7)])
    u = jnp.where(first, b, p1)
    v = jnp.where(first, a, jnp.where(m == 2, p1, m1))
    p2 = send(u, [(0, 2), (2, 4)])
    m2 = send(v, [(0, 7), (7, 5)])
    e1 = send(v, [(0, 1), (2, 3), (7, 6)])
    e2 = send(jnp.where(first, b, jnp.where(m < 5, p2, m2)), [(0, 1), (2, 3), (4, 5), (5, 4), (7, 6)])

    def pick(options):
        value = options[-1]
        for i in range(len(options) - 1):
            value = jnp.where(m == i, options[i], value)
        return value

    top = pick([a, e1, p1, e1, p2, e2, e2, m2])
    low = pick([b, e2, p2, e2, e2, m2, e1, m1])
    return top, low


def sums_kernel(own, top, low, mask, region, out):
    half = CH // 2

    def body(t, carry):
        c = tile_at(t)
        acc = None
        for k in range(CH):
            ref = top[k, c, :] if k < half else low[k - half, c, :]
            d = own[k, c, :] - ref
            acc = d * d if acc is None else acc + d * d
        oc = mask[c, :].astype(F32)
        cell = oc * acc
        reg = region[c, :]
        new = []
        for r in range(REGIONS):
            hit = reg == r
            s = jnp.where(hit, cell, 0.0)
            n = jnp.where(hit, oc, 0.0)
            new.append(carry[2 * r] + (s[:, :128] + s[:, 128:256] + s[:, 256:]))
            new.append(carry[2 * r + 1] + (n[:, :128] + n[:, 128:256] + n[:, 256:]))
        return tuple(new)

    zero = jnp.zeros((8, 128), F32)
    total = lax.fori_loop(0, ROWS // 8, body, (zero,) * (2 * REGIONS))
    lane = iota((8, 128), 1)
    row = zero
    for r in range(REGIONS):
        for j in range(2):
            s = jnp.sum(jnp.sum(total[2 * r + j], axis=0, keepdims=True), axis=1, keepdims=True)
            row = jnp.where(lane == REGIONS * j + r, s, row)
    for i in range(32):
        out[i] = row


def local_sums(own, top, low, mask, region):
    return call(sums_kernel, jax.ShapeDtypeStruct((32, 8, 128), F32), [VMEM] * 5, VMEM)(
        own, top, low, mask, region
    )


def final_kernel(own, top, low, region, parts, target, out, growth):
    total = parts[0]
    for i in range(1, 32):
        total = total + parts[i]
    lane = iota((8, 128), 1)
    counts = jnp.where(lane < REGIONS, pltpu.roll(total, 128 - REGIONS, 1), 1.0)
    squares = jnp.where(lane < REGIONS, total, 1.0)
    g = jnp.sqrt(squares / (counts * CH) + EPSILON)
    growth[...] = g
    factor = target[...] / g

    half = CH // 2

    def body(t, _):
        c = tile_at(t)
        reg = region[c, :]
        f = [
            jnp.take_along_axis(factor, reg[:, 128 * j : 128 * j + 128], axis=1, mode="promise_in_bounds")
            for j in range(3)
        ]
        f = jnp.concatenate(f, axis=1)
        for k in range(CH):
            ref = top[k, c, :] if k < half else low[k - half, c, :]
            out[k, c, :] = ref + f * (own[k, c, :] - ref)
        return 0

    lax.fori_loop(0, ROWS // 8, body, 0)


def rescale(own, top, low, region, parts, target):
    target = jnp.broadcast_to(jnp.pad(target, (0, 128 - REGIONS), constant_values=1.0), (8, 128))
    return call(
        final_kernel,
        [jax.ShapeDtypeStruct((CH, ROWS, COLS), F32), jax.ShapeDtypeStruct((8, 128), F32)],
        [VMEM] * 6,
        [VMEM] * 2,
    )(own, top, low, region, parts, target)


def per_device(member_state, depth, rotation, diff, mask, region, target):
    state = member_state[0]
    statics = (depth, rotation, diff, mask)
    lat = lax.axis_index("lat").astype(jnp.int32).reshape(1)
    halos = exchange(*pack(lat, state, statics))
    own = own_steps(lat, state, statics, halos)
    top, low = broadcast(own)
    parts = local_sums(own, top, low, mask, region)
    parts = lax.all_to_all(parts, ("lon", "lat"), 0, 0)
    bred, growth = rescale(own, top, low, region, parts, target)
    return bred[None], growth[:1, :REGIONS]


def solution(mesh):
    return jax.shard_map(
        per_device,
        mesh=mesh,
        in_specs=(
            P("member", None, "lat", "lon"),
            P("lat", "lon"),
            P("lat", "lon"),
            P(None, "lat", "lon"),
            P("lat", "lon"),
            P("lat", "lon"),
            P(),
        ),
        out_specs=(P("member", None, "lat", "lon"), P("member", None)),
        check_vma=False,
    )
```

```python
import functools
import jax
import jax.numpy as jnp
from jax import lax
from jax.experimental import pallas as pl
from jax.experimental.pallas import tpu as pltpu
from jax.sharding import PartitionSpec as P

LEV = 5
CH = 16
FIELDS = 24
REGIONS = 16
ROWS, COLS = 128, 384
ROWS_X, COLS_X = 136, 512
HALF, HALF_X = 64, 72
HALO = 4
EPSILON = 1e-06
VMEM = pl.BlockSpec(memory_space=pltpu.VMEM)
ANY = pl.BlockSpec(memory_space=pl.ANY)
SMEM = pl.BlockSpec(memory_space=pltpu.SMEM)
F32 = jnp.float32


def call(kernel, out, in_specs, out_specs, scratch=(), flops=1 << 22, nbytes=1 << 23):
    return pl.pallas_call(
        kernel,
        out_shape=out,
        in_specs=in_specs,
        out_specs=out_specs,
        scratch_shapes=list(scratch),
        compiler_params=pltpu.CompilerParams(vmem_limit_bytes=48 << 20),
        cost_estimate=pl.CostEstimate(flops=flops, bytes_accessed=nbytes, transcendentals=0),
    )


def iota(shape, dim):
    return lax.broadcasted_iota(jnp.int32, shape, dim)


def row_slot(k):
    return (k % 8, k >= 8) if k < CH else (8 + (k - CH) % 4, k - CH >= 4)


def pack_kernel(lat, state, depth, rotation, diff, mask, west, east, rows, c_west, c_east, lo, hi, edge, sem):
    upper = lat[0] == 0
    r0 = pl.multiple_of(jnp.where(upper, ROWS - 8, 0), 8)
    tile = pl.ds(r0, 8)
    left, right, full = slice(0, 128), slice(COLS - 128, COLS), slice(0, ROWS)
    copies = []
    for i, (src, at) in enumerate(
        [(state, slice(0, CH)), (depth, CH), (rotation, CH + 1), (diff, slice(CH + 2, CH + 2 + LEV))]
    ):
        lead = (slice(None),) if src.shape[:-2] else ()
        for j, (dst, cut) in enumerate([(edge, (tile, slice(None))), (lo, (full, left)), (hi, (full, right))]):
            copies.append(pltpu.make_async_copy(src.at[lead + cut], dst.at[at], sem.at[3 * i + j]))
    for copy in copies:
        copy.start()
    last = FIELDS - 1
    lo[last] = mask[:, left].astype(F32)
    hi[last] = mask[:, right].astype(F32)
    edge[last] = mask[tile, :].astype(F32)
    for copy in copies:
        copy.wait()

    lane = iota((ROWS, 128), 1)
    w = jnp.zeros((ROWS, 128), F32)
    e = jnp.zeros((ROWS, 128), F32)
    for k in range(FIELDS):
        own = (lane >= HALO * k) & (lane < HALO * k + HALO)
        w = jnp.where(own, pltpu.roll(lo[k], HALO * k, 1) if k else lo[k], w)
        e = jnp.where(own, pltpu.roll(hi[k], HALO * k + HALO, 1), e)
    west[...] = w
    east[...] = e
    c_west[...] = west[tile, :]
    c_east[...] = east[tile, :]
    sub = iota((8, COLS), 0)
    mine = (sub >= 4) == upper
    for k in range(FIELDS):
        slot, flip = row_slot(k)
        if not flip:
            pair = k + (8 if k < CH else 4)
            rows[8 * slot : 8 * slot + 8, :] = jnp.where(mine, edge[k], pltpu.roll(edge[pair], 4, 0))


def pack(lat, state, statics):
    shapes = [(ROWS, 128), (ROWS, 128), (FIELDS * 4, COLS), (8, 128), (8, 128)]
    return call(
        pack_kernel,
        [jax.ShapeDtypeStruct(s, F32) for s in shapes],
        [SMEM] + [ANY] * 4 + [VMEM],
        [VMEM] * 5,
        [
            pltpu.VMEM((FIELDS, ROWS, 128), F32),
            pltpu.VMEM((FIELDS, ROWS, 128), F32),
            pltpu.VMEM((FIELDS, 8, COLS), F32),
            pltpu.SemaphoreType.DMA((12,)),
        ],
    )(lat, state, *statics)


def exchange(west, east, rows, c_west, c_east):
    n = lax.axis_size("lon")
    up = [(i, (i + 1) % n) for i in range(n)]
    down = [((i + 1) % n, i) for i in range(n)]
    other = [(0, 1), (1, 0)]
    both = ("lon", "lat")
    up2 = [(2 * i + j, 2 * k + 1 - j) for i, k in up for j in range(2)]
    down2 = [(2 * i + j, 2 * k + 1 - j) for i, k in down for j in range(2)]
    return (
        lax.ppermute(east, "lon", up),
        lax.ppermute(west, "lon", down),
        lax.ppermute(rows, "lat", other),
        lax.ppermute(c_east, both, up2),
        lax.ppermute(c_west, both, down2),
    )


def fill_halo(x, lat, from_west, from_east, rows, c_west, c_east):
    def margin(k, w, e):
        lane = iota(w.shape, 1)
        s = (128 - HALO * k) % 128
        e = pltpu.roll(e, s, 1) if s else e
        return jnp.where(lane < 64, e, pltpu.roll(w, (124 - HALO * k) % 128, 1))

    sub = iota((8, COLS), 0)
    got = (sub < 4) == (lat[0] == 0)
    got_c = got[:, :128]
    w, e = from_west[...], from_east[...]
    cw, ce = c_west[...], c_east[...]
    for k in range(FIELDS):
        x[k, 0:ROWS, COLS:COLS_X] = margin(k, w, e)
        j, flip = row_slot(k)
        tile = rows[8 * j : 8 * j + 8, :]
        if flip:
            tile = pltpu.roll(tile, 4, 0)
        x[k, ROWS:ROWS_X, 0:COLS] = jnp.where(got, tile, 0.0)
        x[k, ROWS:ROWS_X, COLS:COLS_X] = jnp.where(got_c, margin(k, cw, ce), 0.0)


def tile_at(t):
    return pl.ds(pl.multiple_of(t * 8, 8), 8)


def step(x, static, ub, vb, h2, store, count, tiles):
    sub = iota((8, COLS_X), 0)

    def around(t):
        return tile_at(jnp.where(t == 0, count - 1, t - 1)), tile_at(t), tile_at(jnp.where(t == count - 1, 0, t + 1))

    def north(cur, nxt):
        return pltpu.roll(jnp.where(sub == 0, nxt, cur), 7, 0)

    def south(cur, prv):
        return pltpu.roll(jnp.where(sub == 7, prv, cur), 1, 0)

    def east(cur):
        return pltpu.roll(cur, COLS_X - 1, 1)

    def west(cur):
        return pltpu.roll(cur, 1, 1)

    def sums(t, _):
        c = tile_at(t)
        u = x[1, c, :]
        v = x[1 + LEV, c, :]
        for l in range(1, LEV):
            u = u + x[1 + l, c, :]
            v = v + x[1 + LEV + l, c, :]
        ub[c, :] = east(u) - west(u)
        vb[c, :] = v
        return 0

    lax.fori_loop(0, count, sums, 0)

    def surface(t, _):
        p, c, n = around(t)
        v = vb[c, :]
        div = ub[c, :] + (north(v, vb[n, :]) - south(v, vb[p, :]))
        h2[c, :] = static[7, c, :] * (x[0, c, :] - (0.25 / LEV) * static[0, c, :] * div)
        return 0

    lax.fori_loop(0, count, surface, 0)

    def rest(t, _):
        p, c, n = around(t)
        oc = static[7, c, :]
        rot = static[1, c, :]
        h = h2[c, :]
        store(0, c, h)
        px = 0.25 * (east(h) - west(h))
        py = 0.25 * (north(h, h2[n, :]) - south(h, h2[p, :]))
        for l in range(LEV):
            k = static[2 + l, c, :]

            def near(ch):
                q = x[ch, c, :]
                return q, east(q), west(q), north(q, x[ch, n, :]), south(q, x[ch, p, :])

            q, e, w, a, b = near(1 + 2 * LEV + l)
            cx = e - w
            cy = a - b
            c0 = q + k * ((e + w) + (a + b) - 4.0 * q)
            u, e, w, a, b = near(1 + l)
            lap_u = (e + w) + (a + b) - 4.0 * u
            v, e, w, a, b = near(1 + LEV + l)
            lap_v = (e + w) + (a + b) - 4.0 * v
            u2 = oc * (u + rot * v - px - 0.1 * cx + k * lap_u)
            v2 = oc * (v - rot * u - py - 0.1 * cy + k * lap_v)
            store(1 + l, c, u2)
            store(1 + LEV + l, c, v2)
            store(1 + 2 * LEV + l, c, oc * (c0 - 0.05 * (u2 * cx + v2 * cy)))
        return 0

    lax.fori_loop(0, tiles, rest, 0)


def two_steps(x, static, y, ub, vb, h2, out):
    count = x.shape[1] // 8

    def keep(ch, c, value):
        y[ch, c, :] = value

    def give(ch, c, value):
        out[ch, c, :] = value[:, :COLS]

    step(x, static, ub, vb, h2, keep, count, count)
    step(y, static, ub, vb, h2, give, count, count - 1)


def step_scratch(rows):
    return [pltpu.VMEM((CH, rows, COLS_X), F32)] + [pltpu.VMEM((rows, COLS_X), F32)] * 3


def own_kernel(where, state, depth, rotation, diff, mask, fw, fe, rows, cw, ce, gate, out, part, x, y, ub, vb, h2, sem):
    main = (slice(0, ROWS), slice(0, COLS))
    copies = [
        pltpu.make_async_copy(state, x.at[(slice(0, CH),) + main], sem.at[0]),
        pltpu.make_async_copy(depth, x.at[(CH,) + main], sem.at[1]),
        pltpu.make_async_copy(rotation, x.at[(CH + 1,) + main], sem.at[2]),
        pltpu.make_async_copy(diff, x.at[(slice(CH + 2, CH + 2 + LEV),) + main], sem.at[3]),
    ]
    for copy in copies:
        copy.start()
    x[(FIELDS - 1,) + main] = mask[...].astype(F32)
    fill_halo(x, where, fw, fe, rows, cw, ce)
    for copy in copies:
        copy.wait()
    first = where[1] == 0
    tiles = HALF // 8
    sub = iota((8, COLS_X), 0)
    for j in range(CH, FIELDS):

        def body(t, _):
            part[j - CH, tile_at(t), :] = x[j, tile_at(t + jnp.where(first, 0, tiles)), :]
            return 0

        lax.fori_loop(0, tiles, body, 0)
        n = x[j, tile_at(jnp.where(first, tiles, 2 * tiles)), :]
        p = x[j, tile_at(jnp.where(first, 2 * tiles, tiles - 1)), :]
        part[j - CH, HALF:HALF_X, :] = jnp.where(sub < 4, n, p)
    two_steps(x, x.at[CH:FIELDS], y, ub, vb, h2, out)


def own_steps(where, state, statics, halos, gate):
    return call(
        own_kernel,
        [
            jax.ShapeDtypeStruct((CH, ROWS, COLS), F32),
            jax.ShapeDtypeStruct((FIELDS - CH, HALF_X, COLS_X), F32),
        ],
        [SMEM] + [ANY] * 4 + [VMEM] * 6 + [ANY],
        [VMEM] * 2,
        [pltpu.VMEM((FIELDS, ROWS_X, COLS_X), F32)] + step_scratch(ROWS_X) + [pltpu.SemaphoreType.DMA((4,))],
        flops=1 << 28,
    )(where, state, *statics, *halos, gate)


def control_halo_kernel(fw, fe, rows, cw, ce, out):
    out[0:64, :] = rows[0:64, :]

    def join(w, e):
        return jnp.where(iota(w.shape, 1) < 64, w, pltpu.roll(e, 64, 1))

    s = join(fw[...], fe[...])
    out[64:112, 0:128] = s[0:48]
    out[64:112, 128:256] = s[48:96]
    out[64:96, 256:384] = s[96:128]
    out[96:104, 256:384] = join(cw[...], ce[...])
    out[104:112, 256:384] = jnp.zeros((8, 128), F32)


def send(value, pairs):
    return lax.ppermute(value, "member", pairs)


def spread_halo_first(m, halos):
    own = call(control_halo_kernel, jax.ShapeDtypeStruct((112, COLS), F32), [VMEM] * 5, VMEM)(*halos)
    return jnp.where(m == 0, own, send(own, [(0, 1)]))


def spread_halo_rest(m, h):
    h = jnp.where(m < 2, h, send(h, [(0, 2), (1, 7)]))
    return jnp.where((m < 3) | (m == 7), h, send(h, [(0, 6), (1, 3), (2, 4), (7, 5)]))


def relay_kernel(where, top, low, p1, m1, gate, u, v, sem):
    m = where[2]

    def move(src, dst, i):
        copy = pltpu.make_async_copy(src, dst, sem.at[i])
        copy.start()
        copy.wait()

    @pl.when(m == 0)
    def _():
        one = pltpu.make_async_copy(low, u, sem.at[0])
        two = pltpu.make_async_copy(top, v, sem.at[1])
        one.start()
        two.start()
        one.wait()
        two.wait()

    @pl.when(m == 2)
    def _():
        move(p1, u, 0)

    @pl.when(m == 7)
    def _():
        move(m1, v, 1)


def spread_first(state):
    top, low = state[:, :HALF_X], state[:, ROWS - HALF_X :]
    return top, low, send(top, [(0, 2)]), send(low, [(0, 7)]), send(low, [(0, 1)])


def spread_rest(where, top, low, p1, m1, e0, gate):
    shape = jax.ShapeDtypeStruct((CH, HALF_X, COLS), F32)
    u, v = call(
        relay_kernel, [shape, shape], [SMEM] + [ANY] * 5, [ANY] * 2, [pltpu.SemaphoreType.DMA((2,))]
    )(where, top, low, p1, m1, gate)
    p2 = send(u, [(0, 3), (2, 4)])
    m2 = send(v, [(0, 6), (7, 5)])
    return (top, e0, p1, p2, m2, m1), u


HOLDER = ((0,), (1,), (2,), (3, 4), (5, 6), (7,))


def control_kernel(where, *refs):
    arrays, (halo, static, out, x, y, ub, vb, h2, near, strip, sem) = refs[:6], refs[6:]
    first = where[1] == 0
    m = where[2]
    for array, members in zip(arrays, HOLDER):
        for member in members:
            r0, r1 = (0, HALF) if member % 2 == 0 else (8, 0)

            @pl.when(m == member)
            def _(array=array, r0=r0, r1=r1):
                one = pltpu.make_async_copy(array.at[:, r0 : r0 + HALF, :], x.at[:, 0:HALF, 0:COLS], sem.at[0])
                two = pltpu.make_async_copy(array.at[:, r1 : r1 + 8, :], near, sem.at[1])
                one.start()
                two.start()
                one.wait()
                two.wait()

    strip[0:48, :] = halo[64:112, 0:128]
    strip[48:96, :] = halo[64:112, 128:256]
    strip[96:136, :] = halo[64:104, 256:384]

    def margin(k, s):
        lane = iota(s.shape, 1)
        return jnp.where(
            lane < 64, pltpu.roll(s, 64 - HALO * k, 1), pltpu.roll(s, 124 - HALO * k, 1)
        )

    sub = iota((8, COLS), 0)
    inner = (sub < 4) == first
    got = (sub < 4) == (where[0] == 0)
    s_main = strip[pl.ds(pl.multiple_of(jnp.where(first, 0, HALF), 8), HALF), :]
    s_near = strip[pl.ds(pl.multiple_of(jnp.where(first, HALF, HALF - 8), 8), 8), :]
    s_edge = jnp.where(inner[:, :128], s_near, jnp.where(got[:, :128], strip[ROWS:ROWS_X, :], 0.0))
    for k in range(CH):
        x[k, 0:HALF, COLS:COLS_X] = margin(k, s_main)
        x[k, HALF:HALF_X, COLS:COLS_X] = margin(k, s_edge)
        j, flip = row_slot(k)
        tile = halo[8 * j : 8 * j + 8, :]
        if flip:
            tile = pltpu.roll(tile, 4, 0)
        x[k, HALF:HALF_X, 0:COLS] = jnp.where(inner, near[k], jnp.where(got, tile, 0.0))
    two_steps(x, static, y, ub, vb, h2, out)


def control_steps(where, arrays, halo, static):
    return call(
        control_kernel,
        jax.ShapeDtypeStruct((CH, HALF, COLS), F32),
        [SMEM] + [ANY] * 6 + [VMEM] * 2,
        VMEM,
        [pltpu.VMEM((CH, HALF_X, COLS_X), F32)]
        + step_scratch(HALF_X)
        + [pltpu.VMEM((CH, 8, COLS), F32), pltpu.VMEM((ROWS_X, 128), F32), pltpu.SemaphoreType.DMA((2,))],
        flops=1 << 27,
    )(where, *arrays, halo, static)


def sums_kernel(other, where, own, control, mask, region, earlier, out):
    start = HALF // 8 * (where[1] ^ 1 if other else where[1])

    def body(t, carry):
        c, g = tile_at(t), tile_at(t + start)
        acc = None
        for k in range(CH):
            d = own[k, g, :] - control[k, c, :]
            acc = d * d if acc is None else acc + d * d
        oc = mask[g, :].astype(F32)
        cell = oc * acc
        reg = region[g, :]
        new = []
        for r in range(REGIONS):
            hit = reg == r
            s = jnp.where(hit, cell, 0.0)
            n = jnp.where(hit, oc, 0.0)
            new.append(carry[2 * r] + (s[:, :128] + s[:, 128:256] + s[:, 256:]))
            new.append(carry[2 * r + 1] + (n[:, :128] + n[:, 128:256] + n[:, 256:]))
        return tuple(new)

    zero = jnp.zeros((8, 128), F32)
    total = lax.fori_loop(0, HALF // 8, body, (zero,) * (2 * REGIONS))
    lane = iota((8, 128), 1)
    row = zero
    for r in range(REGIONS):
        for j in range(2):
            s = jnp.sum(jnp.sum(total[2 * r + j], axis=0, keepdims=True), axis=1, keepdims=True)
            row = jnp.where(lane == REGIONS * j + r, s, row)
    if other:
        row = row + earlier[...]
        for i in range(out.shape[0]):
            out[i] = row
    else:
        out[...] = row + earlier[...]


def half_sums(other, where, own, control, mask, region, earlier):
    shape = (32, 8, 128) if other else (8, 128)
    return call(
        functools.partial(sums_kernel, other), jax.ShapeDtypeStruct(shape, F32), [SMEM] + [VMEM] * 5, VMEM
    )(where, own, control, mask, region, earlier)


BLOCK = 4


def final_kernel(where, own, mine, theirs, region, parts, target, out, growth, cell):
    @pl.when(pl.program_id(0) == 0)
    def _():
        total = parts[0]
        for i in range(1, 32):
            total = total + parts[i]
        lane = iota((8, 128), 1)
        counts = jnp.where(lane < REGIONS, pltpu.roll(total, 128 - REGIONS, 1), 1.0)
        squares = jnp.where(lane < REGIONS, total, 1.0)
        g = jnp.sqrt(squares / (counts * CH) + EPSILON)
        growth[...] = g
        factor = target[...] / g

        def body(t, _):
            c = tile_at(t)
            for j in range(3):
                lanes = slice(128 * j, 128 * j + 128)
                reg = region[c, lanes]
                cell[c, lanes] = jnp.take_along_axis(factor, reg, axis=1, mode="promise_in_bounds")
            return 0

        lax.fori_loop(0, ROWS // 8, body, 0)

    start = HALF // 8 * where[1]
    for ref, s in ((mine, start), (theirs, HALF // 8 - start)):

        def body(t, _):
            c, g = tile_at(t), tile_at(t + s)
            f = cell[g, :]
            for k in range(BLOCK):
                q = ref[k, c, :]
                out[k, g, :] = q + f * (own[k, g, :] - q)
            return 0

        lax.fori_loop(0, HALF // 8, body, 0)


def rescale(where, own, mine, theirs, region, parts, target):
    target = jnp.broadcast_to(jnp.pad(target, (0, 128 - REGIONS), constant_values=1.0), (8, 128))

    def cut(rows):
        return pl.BlockSpec((BLOCK, rows, COLS), lambda i: (i, 0, 0))

    def whole(*shape):
        return pl.BlockSpec(shape, lambda i: (0,) * len(shape))

    return pl.pallas_call(
        final_kernel,
        grid=(CH // BLOCK,),
        out_shape=[jax.ShapeDtypeStruct((CH, ROWS, COLS), F32), jax.ShapeDtypeStruct((8, 128), F32)],
        in_specs=[SMEM, cut(ROWS), cut(HALF), cut(HALF), whole(ROWS, COLS), whole(32, 8, 128), whole(8, 128)],
        out_specs=[cut(ROWS), whole(8, 128)],
        scratch_shapes=[pltpu.VMEM((ROWS, COLS), F32)],
        compiler_params=pltpu.CompilerParams(vmem_limit_bytes=32 << 20),
        cost_estimate=pl.CostEstimate(flops=1 << 22, bytes_accessed=10 << 20, transcendentals=0),
    )(where, own, mine, theirs, region, parts, target)


def per_device(member_state, depth, rotation, diff, mask, region, target):
    state = member_state[0]
    statics = (depth, rotation, diff, mask)
    m = lax.axis_index("member")
    where = jnp.stack([lax.axis_index("lat"), m % 2, m]).astype(jnp.int32)
    first = spread_first(state)
    halos = exchange(*pack(where, state, statics))
    halo = spread_halo_first(m, halos)
    arrays, gate = spread_rest(where, *first, halo)
    halo = spread_halo_rest(m, halo)
    own, static = own_steps(where, state, statics, halos, gate)
    mine = control_steps(where, arrays, halo, static)
    theirs = send(mine, [(i, i ^ 1) for i in range(8)])
    parts = half_sums(False, where, own, mine, mask, region, jnp.zeros((8, 128), F32))
    parts = half_sums(True, where, own, theirs, mask, region, parts)
    parts = lax.all_to_all(parts, ("lon", "lat"), 0, 0)
    bred, growth = rescale(where, own, mine, theirs, region, parts, target)
    return bred[None], growth[:1, :REGIONS]


def solution(mesh):
    return jax.shard_map(
        per_device,
        mesh=mesh,
        in_specs=(
            P("member", None, "lat", "lon"),
            P("lat", "lon"),
            P("lat", "lon"),
            P(None, "lat", "lon"),
            P("lat", "lon"),
            P("lat", "lon"),
            P(),
        ),
        out_specs=(P("member", None, "lat", "lon"), P("member", None)),
        check_vma=False,
    )
```

```python
import functools
import jax
import jax.numpy as jnp
from jax import lax
from jax.experimental import pallas as pl
from jax.experimental.pallas import tpu as pltpu
from jax.sharding import PartitionSpec as P

LEV = 5
CH = 16
FIELDS = 24
REGIONS = 16
ROWS, COLS = 128, 384
ROWS_X, COLS_X = 136, 512
HALF, HALF_X = 64, 72
HALO = 4
EPSILON = 1e-06
VMEM = pl.BlockSpec(memory_space=pltpu.VMEM)
ANY = pl.BlockSpec(memory_space=pl.ANY)
SMEM = pl.BlockSpec(memory_space=pltpu.SMEM)
F32 = jnp.float32


def call(kernel, out, in_specs, out_specs, scratch=(), flops=1 << 22, nbytes=1 << 23):
    return pl.pallas_call(
        kernel,
        out_shape=out,
        in_specs=in_specs,
        out_specs=out_specs,
        scratch_shapes=list(scratch),
        compiler_params=pltpu.CompilerParams(vmem_limit_bytes=48 << 20),
        cost_estimate=pl.CostEstimate(flops=flops, bytes_accessed=nbytes, transcendentals=0),
    )


def iota(shape, dim):
    return lax.broadcasted_iota(jnp.int32, shape, dim)


def row_slot(k):
    return (k % 8, k >= 8) if k < CH else (8 + (k - CH) % 4, k - CH >= 4)


def pack_kernel(lat, state, depth, rotation, diff, mask, west, east, rows, c_west, c_east, lo, hi, edge, sem):
    upper = lat[0] == 0
    r0 = pl.multiple_of(jnp.where(upper, ROWS - 8, 0), 8)
    tile = pl.ds(r0, 8)
    left, right, full = slice(0, 128), slice(COLS - 128, COLS), slice(0, ROWS)
    copies = []
    for i, (src, at) in enumerate(
        [(state, slice(0, CH)), (depth, CH), (rotation, CH + 1), (diff, slice(CH + 2, CH + 2 + LEV))]
    ):
        lead = (slice(None),) if src.shape[:-2] else ()
        for j, (dst, cut) in enumerate([(edge, (tile, slice(None))), (lo, (full, left)), (hi, (full, right))]):
            copies.append(pltpu.make_async_copy(src.at[lead + cut], dst.at[at], sem.at[3 * i + j]))
    for copy in copies:
        copy.start()
    last = FIELDS - 1
    lo[last] = mask[:, left].astype(F32)
    hi[last] = mask[:, right].astype(F32)
    edge[last] = mask[tile, :].astype(F32)
    for copy in copies:
        copy.wait()

    lane = iota((ROWS, 128), 1)
    w = jnp.zeros((ROWS, 128), F32)
    e = jnp.zeros((ROWS, 128), F32)
    for k in range(FIELDS):
        own = (lane >= HALO * k) & (lane < HALO * k + HALO)
        w = jnp.where(own, pltpu.roll(lo[k], HALO * k, 1) if k else lo[k], w)
        e = jnp.where(own, pltpu.roll(hi[k], HALO * k + HALO, 1), e)
    west[...] = w
    east[...] = e
    c_west[...] = west[tile, :]
    c_east[...] = east[tile, :]
    sub = iota((8, COLS), 0)
    mine = (sub >= 4) == upper
    for k in range(FIELDS):
        slot, flip = row_slot(k)
        if not flip:
            pair = k + (8 if k < CH else 4)
            rows[8 * slot : 8 * slot + 8, :] = jnp.where(mine, edge[k], pltpu.roll(edge[pair], 4, 0))


def pack(lat, state, statics):
    shapes = [(ROWS, 128), (ROWS, 128), (FIELDS * 4, COLS), (8, 128), (8, 128)]
    return call(
        pack_kernel,
        [jax.ShapeDtypeStruct(s, F32) for s in shapes],
        [SMEM] + [ANY] * 4 + [VMEM],
        [VMEM] * 5,
        [
            pltpu.VMEM((FIELDS, ROWS, 128), F32),
            pltpu.VMEM((FIELDS, ROWS, 128), F32),
            pltpu.VMEM((FIELDS, 8, COLS), F32),
            pltpu.SemaphoreType.DMA((12,)),
        ],
    )(lat, state, *statics)


def exchange(west, east, rows, c_west, c_east):
    n = lax.axis_size("lon")
    up = [(i, (i + 1) % n) for i in range(n)]
    down = [((i + 1) % n, i) for i in range(n)]
    other = [(0, 1), (1, 0)]
    both = ("lon", "lat")
    up2 = [(2 * i + j, 2 * k + 1 - j) for i, k in up for j in range(2)]
    down2 = [(2 * i + j, 2 * k + 1 - j) for i, k in down for j in range(2)]
    return (
        lax.ppermute(east, "lon", up),
        lax.ppermute(west, "lon", down),
        lax.ppermute(rows, "lat", other),
        lax.ppermute(c_east, both, up2),
        lax.ppermute(c_west, both, down2),
    )


def fill_halo(x, lat, from_west, from_east, rows, c_west, c_east):
    def margin(k, w, e):
        lane = iota(w.shape, 1)
        s = (128 - HALO * k) % 128
        e = pltpu.roll(e, s, 1) if s else e
        return jnp.where(lane < 64, e, pltpu.roll(w, (124 - HALO * k) % 128, 1))

    sub = iota((8, COLS), 0)
    got = (sub < 4) == (lat[0] == 0)
    got_c = got[:, :128]
    w, e = from_west[...], from_east[...]
    cw, ce = c_west[...], c_east[...]
    for k in range(FIELDS):
        x[k, 0:ROWS, COLS:COLS_X] = margin(k, w, e)
        j, flip = row_slot(k)
        tile = rows[8 * j : 8 * j + 8, :]
        if flip:
            tile = pltpu.roll(tile, 4, 0)
        x[k, ROWS:ROWS_X, 0:COLS] = jnp.where(got, tile, 0.0)
        x[k, ROWS:ROWS_X, COLS:COLS_X] = jnp.where(got_c, margin(k, cw, ce), 0.0)


def tile_at(t):
    return pl.ds(pl.multiple_of(t * 8, 8), 8)


def step(x, static, ub, vb, h2, store, count, tiles):
    sub = iota((8, COLS_X), 0)

    def around(t):
        return tile_at(jnp.where(t == 0, count - 1, t - 1)), tile_at(t), tile_at(jnp.where(t == count - 1, 0, t + 1))

    def north(cur, nxt):
        return pltpu.roll(jnp.where(sub == 0, nxt, cur), 7, 0)

    def south(cur, prv):
        return pltpu.roll(jnp.where(sub == 7, prv, cur), 1, 0)

    def east(cur):
        return pltpu.roll(cur, COLS_X - 1, 1)

    def west(cur):
        return pltpu.roll(cur, 1, 1)

    def sums(t, _):
        c = tile_at(t)
        u = x[1, c, :]
        v = x[1 + LEV, c, :]
        for l in range(1, LEV):
            u = u + x[1 + l, c, :]
            v = v + x[1 + LEV + l, c, :]
        ub[c, :] = east(u) - west(u)
        vb[c, :] = v
        return 0

    lax.fori_loop(0, count, sums, 0)

    def surface(t, _):
        p, c, n = around(t)
        v = vb[c, :]
        div = ub[c, :] + (north(v, vb[n, :]) - south(v, vb[p, :]))
        h2[c, :] = static[7, c, :] * (x[0, c, :] - (0.25 / LEV) * static[0, c, :] * div)
        return 0

    lax.fori_loop(0, count, surface, 0)

    def rest(t, _):
        p, c, n = around(t)
        oc = static[7, c, :]
        rot = static[1, c, :]
        h = h2[c, :]
        store(0, c, h)
        px = 0.25 * (east(h) - west(h))
        py = 0.25 * (north(h, h2[n, :]) - south(h, h2[p, :]))
        for l in range(LEV):
            k = static[2 + l, c, :]

            def near(ch):
                q = x[ch, c, :]
                return q, east(q), west(q), north(q, x[ch, n, :]), south(q, x[ch, p, :])

            q, e, w, a, b = near(1 + 2 * LEV + l)
            cx = e - w
            cy = a - b
            c0 = q + k * ((e + w) + (a + b) - 4.0 * q)
            u, e, w, a, b = near(1 + l)
            lap_u = (e + w) + (a + b) - 4.0 * u
            v, e, w, a, b = near(1 + LEV + l)
            lap_v = (e + w) + (a + b) - 4.0 * v
            u2 = oc * (u + rot * v - px - 0.1 * cx + k * lap_u)
            v2 = oc * (v - rot * u - py - 0.1 * cy + k * lap_v)
            store(1 + l, c, u2)
            store(1 + LEV + l, c, v2)
            store(1 + 2 * LEV + l, c, oc * (c0 - 0.05 * (u2 * cx + v2 * cy)))
        return 0

    lax.fori_loop(0, tiles, rest, 0)


def two_steps(x, static, y, ub, vb, h2, out):
    count = x.shape[1] // 8

    def keep(ch, c, value):
        y[ch, c, :] = value

    def give(ch, c, value):
        out[ch, c, :] = value[:, :COLS]

    step(x, static, ub, vb, h2, keep, count, count)
    step(y, static, ub, vb, h2, give, count, count - 1)


def step_scratch(rows):
    return [pltpu.VMEM((CH, rows, COLS_X), F32)] + [pltpu.VMEM((rows, COLS_X), F32)] * 3


def own_kernel(where, state, depth, rotation, diff, mask, fw, fe, rows, cw, ce, gate, out, part, x, y, ub, vb, h2, sem):
    main = (slice(0, ROWS), slice(0, COLS))
    copies = [
        pltpu.make_async_copy(state, x.at[(slice(0, CH),) + main], sem.at[0]),
        pltpu.make_async_copy(depth, x.at[(CH,) + main], sem.at[1]),
        pltpu.make_async_copy(rotation, x.at[(CH + 1,) + main], sem.at[2]),
        pltpu.make_async_copy(diff, x.at[(slice(CH + 2, CH + 2 + LEV),) + main], sem.at[3]),
    ]
    for copy in copies:
        copy.start()
    x[(FIELDS - 1,) + main] = mask[...].astype(F32)
    fill_halo(x, where, fw, fe, rows, cw, ce)
    for copy in copies:
        copy.wait()
    first = where[1] == 0
    tiles = HALF // 8
    sub = iota((8, COLS_X), 0)
    for j in range(CH, FIELDS):

        def body(t, _):
            part[j - CH, tile_at(t), :] = x[j, tile_at(t + jnp.where(first, 0, tiles)), :]
            return 0

        lax.fori_loop(0, tiles, body, 0)
        n = x[j, tile_at(jnp.where(first, tiles, 2 * tiles)), :]
        p = x[j, tile_at(jnp.where(first, 2 * tiles, tiles - 1)), :]
        part[j - CH, HALF:HALF_X, :] = jnp.where(sub < 4, n, p)
    two_steps(x, x.at[CH:FIELDS], y, ub, vb, h2, out)


def own_steps(where, state, statics, halos, gate):
    return call(
        own_kernel,
        [
            jax.ShapeDtypeStruct((CH, ROWS, COLS), F32),
            jax.ShapeDtypeStruct((FIELDS - CH, HALF_X, COLS_X), F32),
        ],
        [SMEM] + [ANY] * 4 + [VMEM] * 6 + [ANY],
        [VMEM] * 2,
        [pltpu.VMEM((FIELDS, ROWS_X, COLS_X), F32)] + step_scratch(ROWS_X) + [pltpu.SemaphoreType.DMA((4,))],
        flops=1 << 28,
    )(where, state, *statics, *halos, gate)


def control_halo_kernel(fw, fe, rows, cw, ce, out):
    for k in range(8):
        out[k] = rows[8 * k : 8 * k + 8, :]
    for i in range(18):
        out[8 + i // 3, :, 128 * (i % 3) : 128 * (i % 3) + 128] = jnp.zeros((8, 128), F32)
    lane = iota((8, 128), 1)
    for i in range(17):
        r = slice(8 * i, 8 * i + 8)
        w, e = (fw[r, :], fe[r, :]) if i < 16 else (cw[...], ce[...])
        s = jnp.where(lane < 64, w, pltpu.roll(e, 64, 1))
        out[8 + i // 3, :, 128 * (i % 3) : 128 * (i % 3) + 128] = s
    out[14:16] = jnp.zeros((2, 8, COLS), F32)


def send(value, pairs):
    return lax.ppermute(value, "member", pairs)


def cut_kernel(where, state, top, low, sem):
    @pl.when(where[2] == 0)
    def _():
        one = pltpu.make_async_copy(state.at[:, 0:HALF_X, :], top, sem.at[0])
        two = pltpu.make_async_copy(state.at[:, ROWS - HALF_X : ROWS, :], low, sem.at[1])
        one.start()
        two.start()
        one.wait()
        two.wait()


def spread_first(where, state):
    shape = jax.ShapeDtypeStruct((CH, HALF_X, COLS), F32)
    top, low = call(cut_kernel, [shape, shape], [SMEM, ANY], [VMEM] * 2, [pltpu.SemaphoreType.DMA((2,))])(where, state)
    return top, low, send(top, [(0, 2)]), send(low, [(0, 7)]), send(low, [(0, 1)])


def spread_halo(m, halos):
    own = call(control_halo_kernel, jax.ShapeDtypeStruct((CH, 8, COLS), F32), [VMEM] * 5, VMEM)(*halos)
    h = jnp.where(m == 0, own, send(own, [(0, 1)]))
    return jnp.where(m < 2, h, send(h, [(0, 2), (1, 7)]))


def relay_kernel(where, top, low, p1, m1, halo, u, v, sem):
    m = where[2]

    def move(pairs):
        copies = []
        for i, (src, dst) in enumerate(pairs):
            copies.append(pltpu.make_async_copy(src, dst.at[:, 0:HALF_X, :], sem.at[2 * i]))
            copies.append(pltpu.make_async_copy(halo, dst.at[:, HALF_X : HALF_X + 8, :], sem.at[2 * i + 1]))
        for copy in copies:
            copy.start()
        for copy in copies:
            copy.wait()

    @pl.when(m == 0)
    def _():
        move([(low, u), (top, v)])

    @pl.when(m == 2)
    def _():
        move([(p1, u)])

    @pl.when(m == 7)
    def _():
        move([(m1, v)])


def spread_rest(where, top, low, p1, m1, e0, halo):
    shape = jax.ShapeDtypeStruct((CH, HALF_X + 8, COLS), F32)
    u, v = call(
        relay_kernel, [shape, shape], [SMEM] + [ANY] * 5, [VMEM] * 2, [pltpu.SemaphoreType.DMA((4,))]
    )(where, top, low, p1, m1, halo)
    p2 = send(u, [(0, 3), (2, 4)])
    m2 = send(v, [(0, 6), (7, 5)])
    return (top, e0, p1, p2, m2, m1), u


HOLDER = ((0,), (1,), (2,), (3, 4), (5, 6), (7,))


def control_kernel(where, *refs):
    arrays, (early, static, out, x, y, ub, vb, h2, near, halo, strip, sem) = refs[:6], refs[6:]
    first = where[1] == 0
    m = where[2]
    for array, members in zip(arrays, HOLDER):
        for member in members:
            r0, r1 = (0, HALF) if member % 2 == 0 else (8, 0)

            @pl.when(m == member)
            def _(array=array, r0=r0, r1=r1):
                one = pltpu.make_async_copy(array.at[:, r0 : r0 + HALF, :], x.at[:, 0:HALF, 0:COLS], sem.at[0])
                two = pltpu.make_async_copy(array.at[:, r1 : r1 + 8, :], near, sem.at[1])
                rides = array.shape[1] > HALF_X
                source = array.at[:, HALF_X : HALF_X + 8, :] if rides else early
                three = pltpu.make_async_copy(source, halo, sem.at[2])
                one.start()
                two.start()
                three.start()
                one.wait()
                two.wait()
                three.wait()

    for i in range(17):
        strip[8 * i : 8 * i + 8, :] = halo[8 + i // 3, :, 128 * (i % 3) : 128 * (i % 3) + 128]

    def margin(k, s):
        lane = iota(s.shape, 1)
        return jnp.where(
            lane < 64, pltpu.roll(s, 64 - HALO * k, 1), pltpu.roll(s, 124 - HALO * k, 1)
        )

    sub = iota((8, COLS), 0)
    inner = (sub < 4) == first
    got = (sub < 4) == (where[0] == 0)
    s_main = strip[pl.ds(pl.multiple_of(jnp.where(first, 0, HALF), 8), HALF), :]
    s_near = strip[pl.ds(pl.multiple_of(jnp.where(first, HALF, HALF - 8), 8), 8), :]
    s_edge = jnp.where(inner[:, :128], s_near, jnp.where(got[:, :128], strip[ROWS:ROWS_X, :], 0.0))
    for k in range(CH):
        x[k, 0:HALF, COLS:COLS_X] = margin(k, s_main)
        x[k, HALF:HALF_X, COLS:COLS_X] = margin(k, s_edge)
        j, flip = row_slot(k)
        tile = halo[j]
        if flip:
            tile = pltpu.roll(tile, 4, 0)
        x[k, HALF:HALF_X, 0:COLS] = jnp.where(inner, near[k], jnp.where(got, tile, 0.0))
    two_steps(x, static, y, ub, vb, h2, out)


def control_steps(where, arrays, halo, static):
    return call(
        control_kernel,
        jax.ShapeDtypeStruct((CH, HALF, COLS), F32),
        [SMEM] + [ANY] * 7 + [VMEM],
        VMEM,
        [pltpu.VMEM((CH, HALF_X, COLS_X), F32)]
        + step_scratch(HALF_X)
        + [pltpu.VMEM((CH, 8, COLS), F32)] * 2
        + [pltpu.VMEM((ROWS_X, 128), F32), pltpu.SemaphoreType.DMA((3,))],
        flops=1 << 27,
    )(where, *arrays, halo, static)


def sums_kernel(other, where, own, control, mask, region, earlier, out):
    start = HALF // 8 * (where[1] ^ 1 if other else where[1])

    def body(t, carry):
        c, g = tile_at(t), tile_at(t + start)
        acc = None
        for k in range(CH):
            d = own[k, g, :] - control[k, c, :]
            acc = d * d if acc is None else acc + d * d
        oc = mask[g, :].astype(F32)
        cell = oc * acc
        reg = region[g, :]
        new = []
        for r in range(REGIONS):
            hit = reg == r
            s = jnp.where(hit, cell, 0.0)
            n = jnp.where(hit, oc, 0.0)
            new.append(carry[2 * r] + (s[:, :128] + s[:, 128:256] + s[:, 256:]))
            new.append(carry[2 * r + 1] + (n[:, :128] + n[:, 128:256] + n[:, 256:]))
        return tuple(new)

    zero = jnp.zeros((8, 128), F32)
    total = lax.fori_loop(0, HALF // 8, body, (zero,) * (2 * REGIONS))
    lane = iota((8, 128), 1)
    row = zero
    for r in range(REGIONS):
        for j in range(2):
            s = jnp.sum(jnp.sum(total[2 * r + j], axis=0, keepdims=True), axis=1, keepdims=True)
            row = jnp.where(lane == REGIONS * j + r, s, row)
    if other:
        row = row + earlier[...]
        for i in range(out.shape[0]):
            out[i] = row
    else:
        out[...] = row + earlier[...]


def half_sums(other, where, own, control, mask, region, earlier):
    shape = (32, 8, 128) if other else (8, 128)
    return call(
        functools.partial(sums_kernel, other), jax.ShapeDtypeStruct(shape, F32), [SMEM] + [VMEM] * 5, VMEM
    )(where, own, control, mask, region, earlier)


BLOCK = 4


def final_kernel(where, own, mine, theirs, region, parts, target, out, growth, cell):
    @pl.when(pl.program_id(0) == 0)
    def _():
        total = parts[0]
        for i in range(1, 32):
            total = total + parts[i]
        lane = iota((8, 128), 1)
        counts = jnp.where(lane < REGIONS, pltpu.roll(total, 128 - REGIONS, 1), 1.0)
        squares = jnp.where(lane < REGIONS, total, 1.0)
        g = jnp.sqrt(squares / (counts * CH) + EPSILON)
        growth[...] = g
        factor = target[...] / g

        def body(t, _):
            c = tile_at(t)
            for j in range(3):
                lanes = slice(128 * j, 128 * j + 128)
                reg = region[c, lanes]
                cell[c, lanes] = jnp.take_along_axis(factor, reg, axis=1, mode="promise_in_bounds")
            return 0

        lax.fori_loop(0, ROWS // 8, body, 0)

    start = HALF // 8 * where[1]
    for ref, s in ((mine, start), (theirs, HALF // 8 - start)):

        def body(t, _):
            c, g = tile_at(t), tile_at(t + s)
            f = cell[g, :]
            for k in range(BLOCK):
                q = ref[k, c, :]
                out[k, g, :] = q + f * (own[k, g, :] - q)
            return 0

        lax.fori_loop(0, HALF // 8, body, 0)


def rescale(where, own, mine, theirs, region, parts, target):
    target = jnp.broadcast_to(jnp.pad(target, (0, 128 - REGIONS), constant_values=1.0), (8, 128))

    def cut(rows):
        return pl.BlockSpec((BLOCK, rows, COLS), lambda i: (i, 0, 0))

    def whole(*shape):
        return pl.BlockSpec(shape, lambda i: (0,) * len(shape))

    return pl.pallas_call(
        final_kernel,
        grid=(CH // BLOCK,),
        out_shape=[jax.ShapeDtypeStruct((CH, ROWS, COLS), F32), jax.ShapeDtypeStruct((8, 128), F32)],
        in_specs=[SMEM, cut(ROWS), cut(HALF), cut(HALF), whole(ROWS, COLS), whole(32, 8, 128), whole(8, 128)],
        out_specs=[cut(ROWS), whole(8, 128)],
        scratch_shapes=[pltpu.VMEM((ROWS, COLS), F32)],
        compiler_params=pltpu.CompilerParams(vmem_limit_bytes=32 << 20),
        cost_estimate=pl.CostEstimate(flops=1 << 22, bytes_accessed=10 << 20, transcendentals=0),
    )(where, own, mine, theirs, region, parts, target)


def per_device(member_state, depth, rotation, diff, mask, region, target):
    state = member_state[0]
    statics = (depth, rotation, diff, mask)
    m = lax.axis_index("member")
    where = jnp.stack([lax.axis_index("lat"), m % 2, m]).astype(jnp.int32)
    first = spread_first(where, state)
    halos = exchange(*pack(where, state, statics))
    halo = spread_halo(m, halos)
    arrays, gate = spread_rest(where, *first, halo)
    own, static = own_steps(where, state, statics, halos, gate)
    mine = control_steps(where, arrays, halo, static)
    theirs = send(mine, [(i, i ^ 1) for i in range(8)])
    parts = half_sums(False, where, own, mine, mask, region, jnp.zeros((8, 128), F32))
    parts = half_sums(True, where, own, theirs, mask, region, parts)
    parts = lax.all_to_all(parts, ("lon", "lat"), 0, 0)
    bred, growth = rescale(where, own, mine, theirs, region, parts, target)
    return bred[None], growth[:1, :REGIONS]


def solution(mesh):
    return jax.shard_map(
        per_device,
        mesh=mesh,
        in_specs=(
            P("member", None, "lat", "lon"),
            P("lat", "lon"),
            P("lat", "lon"),
            P(None, "lat", "lon"),
            P("lat", "lon"),
            P("lat", "lon"),
            P(),
        ),
        out_specs=(P("member", None, "lat", "lon"), P("member", None)),
        check_vma=False,
    )
```

```python
import functools
import jax
import jax.numpy as jnp
from jax import lax
from jax.experimental import pallas as pl
from jax.experimental.pallas import tpu as pltpu
from jax.sharding import PartitionSpec as P

LEV = 5
CH = 16
FIELDS = 24
REGIONS = 16
ROWS, COLS = 128, 384
ROWS_X, COLS_X = 136, 512
HALF, HALF_X = 64, 72
HALO = 4
EPSILON = 1e-06
VMEM = pl.BlockSpec(memory_space=pltpu.VMEM)
ANY = pl.BlockSpec(memory_space=pl.ANY)
SMEM = pl.BlockSpec(memory_space=pltpu.SMEM)
HBM = pl.BlockSpec(memory_space=pltpu.HBM)
F32 = jnp.float32


def call(kernel, out, in_specs, out_specs, scratch=(), flops=1 << 22, nbytes=1 << 23, mib=12):
    return pl.pallas_call(
        kernel,
        out_shape=out,
        in_specs=in_specs,
        out_specs=out_specs,
        scratch_shapes=list(scratch),
        compiler_params=pltpu.CompilerParams(vmem_limit_bytes=mib << 20),
        cost_estimate=pl.CostEstimate(flops=flops, bytes_accessed=nbytes, transcendentals=0),
    )


def iota(shape, dim):
    return lax.broadcasted_iota(jnp.int32, shape, dim)


def row_slot(k):
    return (k % 8, k >= 8) if k < CH else (8 + (k - CH) % 4, k - CH >= 4)


def pack_kernel(lat, state, depth, rotation, diff, mask, west, east, rows, c_west, c_east, lo, hi, edge, land, sem):
    upper = lat[0] == 0
    r0 = pl.multiple_of(jnp.where(upper, ROWS - 8, 0), 8)
    tile = pl.ds(r0, 8)
    left, right, full = slice(0, 128), slice(COLS - 128, COLS), slice(0, ROWS)
    copies = []
    for i, (src, at) in enumerate(
        [(state, slice(0, CH)), (depth, CH), (rotation, CH + 1), (diff, slice(CH + 2, CH + 2 + LEV))]
    ):
        lead = (slice(None),) if src.shape[:-2] else ()
        for j, (dst, cut) in enumerate([(edge, (tile, slice(None))), (lo, (full, left)), (hi, (full, right))]):
            copies.append(pltpu.make_async_copy(src.at[lead + cut], dst.at[at], sem.at[3 * i + j]))
    copies.append(pltpu.make_async_copy(mask, land, sem.at[12]))
    for copy in copies:
        copy.start()
    for copy in copies:
        copy.wait()
    last = FIELDS - 1
    lo[last] = land[:, left].astype(F32)
    hi[last] = land[:, right].astype(F32)
    edge[last] = land[tile, :].astype(F32)

    lane = iota((ROWS, 128), 1)
    w = jnp.zeros((ROWS, 128), F32)
    e = jnp.zeros((ROWS, 128), F32)
    for k in range(FIELDS):
        own = (lane >= HALO * k) & (lane < HALO * k + HALO)
        w = jnp.where(own, pltpu.roll(lo[k], HALO * k, 1) if k else lo[k], w)
        e = jnp.where(own, pltpu.roll(hi[k], HALO * k + HALO, 1), e)
    west[...] = w
    east[...] = e
    c_west[...] = west[tile, :]
    c_east[...] = east[tile, :]
    sub = iota((8, COLS), 0)
    mine = (sub >= 4) == upper
    for k in range(FIELDS):
        slot, flip = row_slot(k)
        if not flip:
            pair = k + (8 if k < CH else 4)
            rows[8 * slot : 8 * slot + 8, :] = jnp.where(mine, edge[k], pltpu.roll(edge[pair], 4, 0))


def pack(lat, state, statics):
    shapes = [(ROWS, 128), (ROWS, 128), (FIELDS * 4, COLS), (8, 128), (8, 128)]
    return call(
        pack_kernel,
        [jax.ShapeDtypeStruct(s, F32) for s in shapes],
        [SMEM] + [HBM] * 5,
        [VMEM] * 5,
        [
            pltpu.VMEM((FIELDS, ROWS, 128), F32),
            pltpu.VMEM((FIELDS, ROWS, 128), F32),
            pltpu.VMEM((FIELDS, 8, COLS), F32),
            pltpu.VMEM((ROWS, COLS), jnp.int32),
            pltpu.SemaphoreType.DMA((13,)),
        ],
        mib=62,
    )(lat, state, *statics)


def exchange(west, east, rows, c_west, c_east):
    n = lax.axis_size("lon")
    up = [(i, (i + 1) % n) for i in range(n)]
    down = [((i + 1) % n, i) for i in range(n)]
    other = [(0, 1), (1, 0)]
    both = ("lon", "lat")
    up2 = [(2 * i + j, 2 * k + 1 - j) for i, k in up for j in range(2)]
    down2 = [(2 * i + j, 2 * k + 1 - j) for i, k in down for j in range(2)]
    return (
        lax.ppermute(east, "lon", up),
        lax.ppermute(west, "lon", down),
        lax.ppermute(rows, "lat", other),
        lax.ppermute(c_east, both, up2),
        lax.ppermute(c_west, both, down2),
    )


def fill_halo(x, lat, from_west, from_east, rows, c_west, c_east):
    def margin(k, w, e):
        lane = iota(w.shape, 1)
        s = (128 - HALO * k) % 128
        e = pltpu.roll(e, s, 1) if s else e
        return jnp.where(lane < 64, e, pltpu.roll(w, (124 - HALO * k) % 128, 1))

    sub = iota((8, COLS), 0)
    got = (sub < 4) == (lat[0] == 0)
    got_c = got[:, :128]
    w, e = from_west[...], from_east[...]
    cw, ce = c_west[...], c_east[...]
    for k in range(FIELDS):
        x[k, 0:ROWS, COLS:COLS_X] = margin(k, w, e)
        j, flip = row_slot(k)
        tile = rows[8 * j : 8 * j + 8, :]
        if flip:
            tile = pltpu.roll(tile, 4, 0)
        x[k, ROWS:ROWS_X, 0:COLS] = jnp.where(got, tile, 0.0)
        x[k, ROWS:ROWS_X, COLS:COLS_X] = jnp.where(got_c, margin(k, cw, ce), 0.0)


def tile_at(t):
    return pl.ds(pl.multiple_of(t * 8, 8), 8)


def step(x, static, ub, vb, h2, store, count, tiles):
    sub = iota((8, COLS_X), 0)

    def around(t):
        return tile_at(jnp.where(t == 0, count - 1, t - 1)), tile_at(t), tile_at(jnp.where(t == count - 1, 0, t + 1))

    def north(cur, nxt):
        return pltpu.roll(jnp.where(sub == 0, nxt, cur), 7, 0)

    def south(cur, prv):
        return pltpu.roll(jnp.where(sub == 7, prv, cur), 1, 0)

    def east(cur):
        return pltpu.roll(cur, COLS_X - 1, 1)

    def west(cur):
        return pltpu.roll(cur, 1, 1)

    def sums(t, _):
        c = tile_at(t)
        u = x[1, c, :]
        v = x[1 + LEV, c, :]
        for l in range(1, LEV):
            u = u + x[1 + l, c, :]
            v = v + x[1 + LEV + l, c, :]
        ub[c, :] = east(u) - west(u)
        vb[c, :] = v
        return 0

    lax.fori_loop(0, count, sums, 0)

    def surface(t, _):
        p, c, n = around(t)
        v = vb[c, :]
        div = ub[c, :] + (north(v, vb[n, :]) - south(v, vb[p, :]))
        h2[c, :] = static[7, c, :] * (x[0, c, :] - (0.25 / LEV) * static[0, c, :] * div)
        return 0

    lax.fori_loop(0, count, surface, 0)

    def rest(t, _):
        p, c, n = around(t)
        oc = static[7, c, :]
        rot = static[1, c, :]
        h = h2[c, :]
        store(0, c, h)
        px = 0.25 * (east(h) - west(h))
        py = 0.25 * (north(h, h2[n, :]) - south(h, h2[p, :]))
        for l in range(LEV):
            k = static[2 + l, c, :]

            def near(ch):
                q = x[ch, c, :]
                return q, east(q), west(q), north(q, x[ch, n, :]), south(q, x[ch, p, :])

            q, e, w, a, b = near(1 + 2 * LEV + l)
            cx = e - w
            cy = a - b
            c0 = q + k * ((e + w) + (a + b) - 4.0 * q)
            u, e, w, a, b = near(1 + l)
            lap_u = (e + w) + (a + b) - 4.0 * u
            v, e, w, a, b = near(1 + LEV + l)
            lap_v = (e + w) + (a + b) - 4.0 * v
            u2 = oc * (u + rot * v - px - 0.1 * cx + k * lap_u)
            v2 = oc * (v - rot * u - py - 0.1 * cy + k * lap_v)
            store(1 + l, c, u2)
            store(1 + LEV + l, c, v2)
            store(1 + 2 * LEV + l, c, oc * (c0 - 0.05 * (u2 * cx + v2 * cy)))
        return 0

    lax.fori_loop(0, tiles, rest, 0)


def two_steps(x, static, y, ub, vb, h2, out):
    count = x.shape[1] // 8

    def keep(ch, c, value):
        y[ch, c, :] = value

    def give(ch, c, value):
        out[ch, c, :] = value[:, :COLS]

    step(x, static, ub, vb, h2, keep, count, count)
    step(y, static, ub, vb, h2, give, count, count - 1)


def step_scratch(rows):
    return [pltpu.VMEM((CH, rows, COLS_X), F32)] + [pltpu.VMEM((rows, COLS_X), F32)] * 3


def own_kernel(where, state, depth, rotation, diff, mask, fw, fe, rows, cw, ce, gate, out, part, x, land, y, ub, vb, h2, sem):
    main = (slice(0, ROWS), slice(0, COLS))
    copies = [
        pltpu.make_async_copy(state, x.at[(slice(0, CH),) + main], sem.at[0]),
        pltpu.make_async_copy(depth, x.at[(CH,) + main], sem.at[1]),
        pltpu.make_async_copy(rotation, x.at[(CH + 1,) + main], sem.at[2]),
        pltpu.make_async_copy(diff, x.at[(slice(CH + 2, CH + 2 + LEV),) + main], sem.at[3]),
    ]
    copies.append(pltpu.make_async_copy(mask, land, sem.at[4]))
    for copy in copies:
        copy.start()
    fill_halo(x, where, fw, fe, rows, cw, ce)
    for copy in copies:
        copy.wait()
    x[(FIELDS - 1,) + main] = land[...].astype(F32)
    first = where[1] == 0
    tiles = HALF // 8
    sub = iota((8, COLS_X), 0)
    for j in range(CH, FIELDS):

        def body(t, _):
            part[j - CH, tile_at(t), :] = x[j, tile_at(t + jnp.where(first, 0, tiles)), :]
            return 0

        lax.fori_loop(0, tiles, body, 0)
        n = x[j, tile_at(jnp.where(first, tiles, 2 * tiles)), :]
        p = x[j, tile_at(jnp.where(first, 2 * tiles, tiles - 1)), :]
        part[j - CH, HALF:HALF_X, :] = jnp.where(sub < 4, n, p)
    two_steps(x, x.at[CH:FIELDS], y, ub, vb, h2, out)


def own_steps(where, state, statics, halos, gate):
    return call(
        own_kernel,
        [
            jax.ShapeDtypeStruct((CH, ROWS, COLS), F32),
            jax.ShapeDtypeStruct((FIELDS - CH, HALF_X, COLS_X), F32),
        ],
        [SMEM] + [HBM] * 5 + [VMEM] * 5 + [HBM],
        [VMEM] * 2,
        [pltpu.VMEM((FIELDS, ROWS_X, COLS_X), F32), pltpu.VMEM((ROWS, COLS), jnp.int32)]
        + step_scratch(ROWS_X)
        + [pltpu.SemaphoreType.DMA((5,))],
        flops=1 << 28,
        mib=28,
    )(where, state, *statics, *halos, gate)


def control_halo_kernel(fw, fe, rows, cw, ce, out):
    for k in range(8):
        out[k] = rows[8 * k : 8 * k + 8, :]
    for i in range(18):
        out[8 + i // 3, :, 128 * (i % 3) : 128 * (i % 3) + 128] = jnp.zeros((8, 128), F32)
    lane = iota((8, 128), 1)
    for i in range(17):
        r = slice(8 * i, 8 * i + 8)
        w, e = (fw[r, :], fe[r, :]) if i < 16 else (cw[...], ce[...])
        s = jnp.where(lane < 64, w, pltpu.roll(e, 64, 1))
        out[8 + i // 3, :, 128 * (i % 3) : 128 * (i % 3) + 128] = s
    out[14:16] = jnp.zeros((2, 8, COLS), F32)


def send(value, pairs):
    return lax.ppermute(value, "member", pairs)


CHUNKS = 4


def staged(copies, buffer, sem):
    n = CH // CHUNKS
    both = []
    for i, (src, dst) in enumerate(copies):
        for j in range(CHUNKS):
            ch, s = slice(n * j, n * j + n), CHUNKS * i + j
            one = pltpu.make_async_copy(src.at[ch], buffer.at[i, ch], sem.at[2 * s])
            both.append((one, pltpu.make_async_copy(buffer.at[i, ch], dst.at[ch, 0:HALF_X, :], sem.at[2 * s + 1])))
            one.start()
    for one, two in both:
        one.wait()
        two.start()
    for one, two in both:
        two.wait()


STAGE = [pltpu.VMEM((2, CH, HALF_X, COLS), F32), pltpu.SemaphoreType.DMA((4 * CHUNKS,))]


def cut_kernel(where, state, top, low, buffer, sem):
    @pl.when(where[2] == 0)
    def _():
        staged(
            [(state.at[:, 0:HALF_X, :], top), (state.at[:, ROWS - HALF_X : ROWS, :], low)], buffer, sem
        )


def spread_first(where, state):
    shape = jax.ShapeDtypeStruct((CH, HALF_X, COLS), F32)
    top, low = call(cut_kernel, [shape, shape], [SMEM, HBM], [HBM] * 2, STAGE, mib=62)(where, state)
    return top, low, send(top, [(0, 2)]), send(low, [(0, 7)])


def relay_kernel(where, top, low, p1, m1, halo, u, v, buffer, sem, ride, ride_sem):
    m = where[2]

    def move(pairs):
        one = pltpu.make_async_copy(halo, ride, ride_sem.at[0])
        one.start()
        one.wait()
        more = [
            pltpu.make_async_copy(ride, dst.at[:, HALF_X : HALF_X + 8, :], ride_sem.at[1 + i])
            for i, (_, dst) in enumerate(pairs)
        ]
        for copy in more:
            copy.start()
        staged(pairs, buffer, sem)
        for copy in more:
            copy.wait()

    @pl.when(m == 0)
    def _():
        move([(low, u), (top, v)])

    @pl.when(m == 2)
    def _():
        move([(p1, u)])

    @pl.when(m == 7)
    def _():
        move([(m1, v)])


def spread_rest(where, top, low, p1, m1, halo):
    m = where[2]
    for_two, for_seven = send(halo, [(0, 2)]), send(halo, [(0, 7)])
    halo = jnp.where(m == 2, for_two, jnp.where(m == 7, for_seven, halo))
    shape = jax.ShapeDtypeStruct((CH, HALF_X + 8, COLS), F32)
    u, v = call(
        relay_kernel,
        [shape, shape],
        [SMEM] + [HBM] * 4 + [ANY],
        [HBM] * 2,
        STAGE + [pltpu.VMEM((CH, 8, COLS), F32), pltpu.SemaphoreType.DMA((3,))],
    )(where, top, low, p1, m1, halo)
    p2 = send(u, [(0, 3), (2, 4)])
    m2 = send(v, [(0, 6), (7, 5)])
    e0 = send(u, [(0, 1)])
    return (top, e0, p1, p2, m2, m1), halo, u


HOLDER = ((0,), (1,), (2,), (3, 4), (5, 6), (7,))


def control_kernel(where, *refs):
    arrays, (early, static, out, x, y, ub, vb, h2, near, halo, strip, sem) = refs[:6], refs[6:]
    first = where[1] == 0
    m = where[2]
    for array, members in zip(arrays, HOLDER):
        for member in members:
            r0, r1 = (0, HALF) if member % 2 == 0 else (8, 0)

            @pl.when(m == member)
            def _(array=array, r0=r0, r1=r1):
                one = pltpu.make_async_copy(array.at[:, r0 : r0 + HALF, :], x.at[:, 0:HALF, 0:COLS], sem.at[0])
                two = pltpu.make_async_copy(array.at[:, r1 : r1 + 8, :], near, sem.at[1])
                rides = array.shape[1] > HALF_X
                source = array.at[:, HALF_X : HALF_X + 8, :] if rides else early
                three = pltpu.make_async_copy(source, halo, sem.at[2])
                one.start()
                two.start()
                three.start()
                one.wait()
                two.wait()
                three.wait()

    for i in range(17):
        strip[8 * i : 8 * i + 8, :] = halo[8 + i // 3, :, 128 * (i % 3) : 128 * (i % 3) + 128]

    def margin(k, s):
        lane = iota(s.shape, 1)
        return jnp.where(
            lane < 64, pltpu.roll(s, 64 - HALO * k, 1), pltpu.roll(s, 124 - HALO * k, 1)
        )

    sub = iota((8, COLS), 0)
    inner = (sub < 4) == first
    got = (sub < 4) == (where[0] == 0)
    s_main = strip[pl.ds(pl.multiple_of(jnp.where(first, 0, HALF), 8), HALF), :]
    s_near = strip[pl.ds(pl.multiple_of(jnp.where(first, HALF, HALF - 8), 8), 8), :]
    s_edge = jnp.where(inner[:, :128], s_near, jnp.where(got[:, :128], strip[ROWS:ROWS_X, :], 0.0))
    for k in range(CH):
        x[k, 0:HALF, COLS:COLS_X] = margin(k, s_main)
        x[k, HALF:HALF_X, COLS:COLS_X] = margin(k, s_edge)
        j, flip = row_slot(k)
        tile = halo[j]
        if flip:
            tile = pltpu.roll(tile, 4, 0)
        x[k, HALF:HALF_X, 0:COLS] = jnp.where(inner, near[k], jnp.where(got, tile, 0.0))
    two_steps(x, static, y, ub, vb, h2, out)


def control_steps(where, arrays, halo, static):
    return call(
        control_kernel,
        jax.ShapeDtypeStruct((CH, HALF, COLS), F32),
        [SMEM] + [HBM] * 6 + [ANY, VMEM],
        VMEM,
        [pltpu.VMEM((CH, HALF_X, COLS_X), F32)]
        + step_scratch(HALF_X)
        + [pltpu.VMEM((CH, 8, COLS), F32)] * 2
        + [pltpu.VMEM((ROWS_X, 128), F32), pltpu.SemaphoreType.DMA((3,))],
        flops=1 << 27,
        mib=16,
    )(where, *arrays, halo, static)


def sums_kernel(other, where, own, control, mask, region, earlier, out, *copy):
    start = HALF // 8 * (where[1] ^ 1 if other else where[1])

    def body(t, carry):
        c, g = tile_at(t), tile_at(t + start)
        acc = None
        for k in range(CH):
            d = own[k, g, :] - control[k, c, :]
            acc = d * d if acc is None else acc + d * d
        oc = mask[g, :].astype(F32)
        cell = oc * acc
        reg = region[g, :]
        new = []
        for r in range(REGIONS):
            hit = reg == r
            s = jnp.where(hit, cell, 0.0)
            n = jnp.where(hit, oc, 0.0)
            new.append(carry[2 * r] + (s[:, :128] + s[:, 128:256] + s[:, 256:]))
            new.append(carry[2 * r + 1] + (n[:, :128] + n[:, 128:256] + n[:, 256:]))
        return tuple(new)

    zero = jnp.zeros((8, 128), F32)
    total = lax.fori_loop(0, HALF // 8, body, (zero,) * (2 * REGIONS))
    lane = iota((8, 128), 1)
    row = zero
    for r in range(REGIONS):
        for j in range(2):
            s = jnp.sum(jnp.sum(total[2 * r + j], axis=0, keepdims=True), axis=1, keepdims=True)
            row = jnp.where(lane == REGIONS * j + r, s, row)
    if other:
        row = row + earlier[...]
        copies, sem = copy
        for i in range(out.shape[0]):
            copies[i] = row
        move = pltpu.make_async_copy(copies, out, sem.at[0])
        move.start()
        move.wait()
    else:
        out[...] = row + earlier[...]


def half_sums(other, where, own, control, mask, region, earlier):
    shape = (32, 8, 128) if other else (8, 128)
    return call(
        functools.partial(sums_kernel, other),
        jax.ShapeDtypeStruct(shape, F32),
        [SMEM] + [VMEM] * 5,
        HBM if other else VMEM,
        [pltpu.VMEM(shape, F32), pltpu.SemaphoreType.DMA((1,))] if other else (),
        mib=4,
    )(where, own, control, mask, region, earlier)


BLOCK = 4


def final_kernel(where, own, mine, theirs, region, parts, target, out, growth, cell):
    @pl.when(pl.program_id(0) == 0)
    def _():
        total = parts[0]
        for i in range(1, 32):
            total = total + parts[i]
        lane = iota((8, 128), 1)
        counts = jnp.where(lane < REGIONS, pltpu.roll(total, 128 - REGIONS, 1), 1.0)
        squares = jnp.where(lane < REGIONS, total, 1.0)
        g = jnp.sqrt(squares / (counts * CH) + EPSILON)
        growth[...] = g[0:1, 0:REGIONS]
        factor = target[...] / g

        def body(t, _):
            c = tile_at(t)
            for j in range(3):
                lanes = slice(128 * j, 128 * j + 128)
                reg = region[c, lanes]
                cell[c, lanes] = jnp.take_along_axis(factor, reg, axis=1, mode="promise_in_bounds")
            return 0

        lax.fori_loop(0, ROWS // 8, body, 0)

    start = HALF // 8 * where[1]
    lead = pl.program_id(0) * BLOCK
    for ref, s in ((mine, start), (theirs, HALF // 8 - start)):

        def body(t, _):
            c, g = tile_at(t), tile_at(t + s)
            f = cell[g, :]
            for k in range(BLOCK):
                q = ref[lead + k, c, :]
                out[k, g, :] = q + f * (own[lead + k, g, :] - q)
            return 0

        lax.fori_loop(0, HALF // 8, body, 0)


def rescale(where, own, mine, theirs, region, parts, target):
    target = jnp.broadcast_to(jnp.pad(target, (0, 128 - REGIONS), constant_values=1.0), (8, 128))

    cut = pl.BlockSpec((BLOCK, ROWS, COLS), lambda i: (i, 0, 0))
    row = pl.BlockSpec((1, REGIONS), lambda i: (0, 0))
    return pl.pallas_call(
        final_kernel,
        grid=(CH // BLOCK,),
        out_shape=[jax.ShapeDtypeStruct((CH, ROWS, COLS), F32), jax.ShapeDtypeStruct((1, REGIONS), F32)],
        in_specs=[SMEM] + [VMEM] * 6,
        out_specs=[cut, row],
        scratch_shapes=[pltpu.VMEM((ROWS, COLS), F32)],
        compiler_params=pltpu.CompilerParams(vmem_limit_bytes=8 << 20),
        cost_estimate=pl.CostEstimate(flops=1 << 22, bytes_accessed=10 << 20, transcendentals=0),
    )(where, own, mine, theirs, region, parts, target)


def per_device(member_state, depth, rotation, diff, mask, region, target):
    state = member_state[0]
    statics = (depth, rotation, diff, mask)
    m = lax.axis_index("member")
    where = jnp.stack([lax.axis_index("lat"), m % 2, m]).astype(jnp.int32)
    first = spread_first(where, state)
    halos = exchange(*pack(where, state, statics))
    halo = call(control_halo_kernel, jax.ShapeDtypeStruct((CH, 8, COLS), F32), [VMEM] * 5, VMEM)(*halos)
    arrays, halo, gate = spread_rest(where, *first, halo)
    own, static = own_steps(where, state, statics, halos, gate)
    mine = control_steps(where, arrays, halo, static)
    theirs = send(mine, [(i, i ^ 1) for i in range(8)])
    parts = half_sums(False, where, own, mine, mask, region, jnp.zeros((8, 128), F32))
    parts = half_sums(True, where, own, theirs, mask, region, parts)
    parts = lax.all_to_all(parts, ("lon", "lat"), 0, 0)
    bred, growth = rescale(where, own, mine, theirs, region, parts, target)
    return bred[None], growth


def solution(mesh):
    return jax.shard_map(
        per_device,
        mesh=mesh,
        in_specs=(
            P("member", None, "lat", "lon"),
            P("lat", "lon"),
            P("lat", "lon"),
            P(None, "lat", "lon"),
            P("lat", "lon"),
            P("lat", "lon"),
            P(),
        ),
        out_specs=(P("member", None, "lat", "lon"), P("member", None)),
        check_vma=False,
    )
```

```python
import functools
import jax
import jax.numpy as jnp
from jax import lax
from jax.experimental import pallas as pl
from jax.experimental.pallas import tpu as pltpu
from jax.sharding import PartitionSpec as P

LEV = 5
CH = 16
FIELDS = 24
REGIONS = 16
ROWS, COLS = 128, 384
ROWS_X, COLS_X = 136, 512
HALF, HALF_X = 64, 72
HALO = 4
EPSILON = 1e-06
VMEM = pl.BlockSpec(memory_space=pltpu.VMEM)
ANY = pl.BlockSpec(memory_space=pl.ANY)
SMEM = pl.BlockSpec(memory_space=pltpu.SMEM)
HBM = pl.BlockSpec(memory_space=pltpu.HBM)
F32 = jnp.float32


def call(kernel, out, in_specs, out_specs, scratch=(), flops=1 << 22, nbytes=1 << 23, mib=12, aliases=None):
    return pl.pallas_call(
        kernel,
        out_shape=[jax.ShapeDtypeStruct(o.shape, o.dtype) for o in out] if isinstance(out, list) else out,
        in_specs=in_specs,
        out_specs=out_specs,
        scratch_shapes=list(scratch),
        input_output_aliases=aliases or {},
        compiler_params=pltpu.CompilerParams(vmem_limit_bytes=mib << 20),
        cost_estimate=pl.CostEstimate(flops=flops, bytes_accessed=nbytes, transcendentals=0),
    )


def iota(shape, dim):
    return lax.broadcasted_iota(jnp.int32, shape, dim)


def row_slot(k):
    return (k % 8, k >= 8) if k < CH else (8 + (k - CH) % 4, k - CH >= 4)


def pack_kernel(lat, state, depth, rotation, diff, mask, west, east, rows, c_west, c_east, lo, hi, edge, land, sem):
    upper = lat[0] == 0
    r0 = pl.multiple_of(jnp.where(upper, ROWS - 8, 0), 8)
    tile = pl.ds(r0, 8)
    left, right, full = slice(0, 128), slice(COLS - 128, COLS), slice(0, ROWS)
    copies = []
    for i, (src, at) in enumerate(
        [(state, slice(0, CH)), (depth, CH), (rotation, CH + 1), (diff, slice(CH + 2, CH + 2 + LEV))]
    ):
        lead = (slice(None),) if src.shape[:-2] else ()
        for j, (dst, cut) in enumerate([(edge, (tile, slice(None))), (lo, (full, left)), (hi, (full, right))]):
            copies.append(pltpu.make_async_copy(src.at[lead + cut], dst.at[at], sem.at[3 * i + j]))
    copies.append(pltpu.make_async_copy(mask, land, sem.at[12]))
    for copy in copies:
        copy.start()
    for copy in copies:
        copy.wait()
    last = FIELDS - 1
    lo[last] = land[:, left].astype(F32)
    hi[last] = land[:, right].astype(F32)
    edge[last] = land[tile, :].astype(F32)

    lane = iota((ROWS, 128), 1)
    w = jnp.zeros((ROWS, 128), F32)
    e = jnp.zeros((ROWS, 128), F32)
    for k in range(FIELDS):
        own = (lane >= HALO * k) & (lane < HALO * k + HALO)
        w = jnp.where(own, pltpu.roll(lo[k], HALO * k, 1) if k else lo[k], w)
        e = jnp.where(own, pltpu.roll(hi[k], HALO * k + HALO, 1), e)
    west[...] = w
    east[...] = e
    c_west[...] = west[tile, :]
    c_east[...] = east[tile, :]
    sub = iota((8, COLS), 0)
    mine = (sub >= 4) == upper
    for k in range(FIELDS):
        slot, flip = row_slot(k)
        if not flip:
            pair = k + (8 if k < CH else 4)
            rows[8 * slot : 8 * slot + 8, :] = jnp.where(mine, edge[k], pltpu.roll(edge[pair], 4, 0))


def pack(lat, state, statics):
    shapes = [(ROWS, 128), (ROWS, 128), (FIELDS * 4, COLS), (8, 128), (8, 128)]
    return call(
        pack_kernel,
        [jax.ShapeDtypeStruct(s, F32) for s in shapes],
        [SMEM] + [HBM] * 5,
        [VMEM] * 5,
        [
            pltpu.VMEM((FIELDS, ROWS, 128), F32),
            pltpu.VMEM((FIELDS, ROWS, 128), F32),
            pltpu.VMEM((FIELDS, 8, COLS), F32),
            pltpu.VMEM((ROWS, COLS), jnp.int32),
            pltpu.SemaphoreType.DMA((13,)),
        ],
        mib=62,
    )(lat, state, *statics)


def exchange(west, east, rows, c_west, c_east):
    n = lax.axis_size("lon")
    up = [(i, (i + 1) % n) for i in range(n)]
    down = [((i + 1) % n, i) for i in range(n)]
    other = [(0, 1), (1, 0)]
    both = ("lon", "lat")
    up2 = [(2 * i + j, 2 * k + 1 - j) for i, k in up for j in range(2)]
    down2 = [(2 * i + j, 2 * k + 1 - j) for i, k in down for j in range(2)]
    return (
        lax.ppermute(east, "lon", up),
        lax.ppermute(west, "lon", down),
        lax.ppermute(rows, "lat", other),
        lax.ppermute(c_east, both, up2),
        lax.ppermute(c_west, both, down2),
    )


def fill_halo(x, lat, from_west, from_east, rows, c_west, c_east):
    def margin(k, w, e):
        lane = iota(w.shape, 1)
        s = (128 - HALO * k) % 128
        e = pltpu.roll(e, s, 1) if s else e
        return jnp.where(lane < 64, e, pltpu.roll(w, (124 - HALO * k) % 128, 1))

    sub = iota((8, COLS), 0)
    got = (sub < 4) == (lat[0] == 0)
    got_c = got[:, :128]
    w, e = from_west[...], from_east[...]
    cw, ce = c_west[...], c_east[...]
    for k in range(FIELDS):
        x[k, 0:ROWS, COLS:COLS_X] = margin(k, w, e)
        j, flip = row_slot(k)
        tile = rows[8 * j : 8 * j + 8, :]
        if flip:
            tile = pltpu.roll(tile, 4, 0)
        x[k, ROWS:ROWS_X, 0:COLS] = jnp.where(got, tile, 0.0)
        x[k, ROWS:ROWS_X, COLS:COLS_X] = jnp.where(got_c, margin(k, cw, ce), 0.0)


def tile_at(t):
    return pl.ds(pl.multiple_of(t * 8, 8), 8)


def step(x, static, ub, vb, h2, store, count, tiles):
    sub = iota((8, COLS_X), 0)

    def around(t):
        return tile_at(jnp.where(t == 0, count - 1, t - 1)), tile_at(t), tile_at(jnp.where(t == count - 1, 0, t + 1))

    def north(cur, nxt):
        return pltpu.roll(jnp.where(sub == 0, nxt, cur), 7, 0)

    def south(cur, prv):
        return pltpu.roll(jnp.where(sub == 7, prv, cur), 1, 0)

    def east(cur):
        return pltpu.roll(cur, COLS_X - 1, 1)

    def west(cur):
        return pltpu.roll(cur, 1, 1)

    def sums(t, _):
        c = tile_at(t)
        u = x[1, c, :]
        v = x[1 + LEV, c, :]
        for l in range(1, LEV):
            u = u + x[1 + l, c, :]
            v = v + x[1 + LEV + l, c, :]
        ub[c, :] = east(u) - west(u)
        vb[c, :] = v
        return 0

    lax.fori_loop(0, count, sums, 0)

    def surface(t, _):
        p, c, n = around(t)
        v = vb[c, :]
        div = ub[c, :] + (north(v, vb[n, :]) - south(v, vb[p, :]))
        h2[c, :] = static[7, c, :] * (x[0, c, :] - (0.25 / LEV) * static[0, c, :] * div)
        return 0

    lax.fori_loop(0, count, surface, 0)

    def rest(t, _):
        p, c, n = around(t)
        oc = static[7, c, :]
        rot = static[1, c, :]
        h = h2[c, :]
        store(0, c, h)
        px = 0.25 * (east(h) - west(h))
        py = 0.25 * (north(h, h2[n, :]) - south(h, h2[p, :]))
        for l in range(LEV):
            k = static[2 + l, c, :]

            def near(ch):
                q = x[ch, c, :]
                return q, east(q), west(q), north(q, x[ch, n, :]), south(q, x[ch, p, :])

            q, e, w, a, b = near(1 + 2 * LEV + l)
            cx = e - w
            cy = a - b
            c0 = q + k * ((e + w) + (a + b) - 4.0 * q)
            u, e, w, a, b = near(1 + l)
            lap_u = (e + w) + (a + b) - 4.0 * u
            v, e, w, a, b = near(1 + LEV + l)
            lap_v = (e + w) + (a + b) - 4.0 * v
            u2 = oc * (u + rot * v - px - 0.1 * cx + k * lap_u)
            v2 = oc * (v - rot * u - py - 0.1 * cy + k * lap_v)
            store(1 + l, c, u2)
            store(1 + LEV + l, c, v2)
            store(1 + 2 * LEV + l, c, oc * (c0 - 0.05 * (u2 * cx + v2 * cy)))
        return 0

    lax.fori_loop(0, tiles, rest, 0)


def two_steps(x, static, y, ub, vb, h2, out):
    count = x.shape[1] // 8

    def keep(ch, c, value):
        y[ch, c, :] = value

    def give(ch, c, value):
        out[ch, c, :] = value[:, :COLS]

    step(x, static, ub, vb, h2, keep, count, count)
    step(y, static, ub, vb, h2, give, count, count - 1)


def step_scratch(rows):
    return [pltpu.VMEM((CH, rows, COLS_X), F32)] + [pltpu.VMEM((rows, COLS_X), F32)] * 3


def own_kernel(where, state, depth, rotation, diff, mask, fw, fe, rows, cw, ce, gate, out, part, x, land, y, ub, vb, h2, sem):
    main = (slice(0, ROWS), slice(0, COLS))
    copies = [
        pltpu.make_async_copy(state, x.at[(slice(0, CH),) + main], sem.at[0]),
        pltpu.make_async_copy(depth, x.at[(CH,) + main], sem.at[1]),
        pltpu.make_async_copy(rotation, x.at[(CH + 1,) + main], sem.at[2]),
        pltpu.make_async_copy(diff, x.at[(slice(CH + 2, CH + 2 + LEV),) + main], sem.at[3]),
    ]
    copies.append(pltpu.make_async_copy(mask, land, sem.at[4]))
    for copy in copies:
        copy.start()
    fill_halo(x, where, fw, fe, rows, cw, ce)
    for copy in copies:
        copy.wait()
    x[(FIELDS - 1,) + main] = land[...].astype(F32)
    first = where[1] == 0
    tiles = HALF // 8
    sub = iota((8, COLS_X), 0)
    for j in range(CH, FIELDS):

        def body(t, _):
            part[j - CH, tile_at(t), :] = x[j, tile_at(t + jnp.where(first, 0, tiles)), :]
            return 0

        lax.fori_loop(0, tiles, body, 0)
        n = x[j, tile_at(jnp.where(first, tiles, 2 * tiles)), :]
        p = x[j, tile_at(jnp.where(first, 2 * tiles, tiles - 1)), :]
        part[j - CH, HALF:HALF_X, :] = jnp.where(sub < 4, n, p)
    two_steps(x, x.at[CH:FIELDS], y, ub, vb, h2, out)


def own_steps(where, state, statics, halos, gate):
    return call(
        own_kernel,
        [
            jax.ShapeDtypeStruct((CH, ROWS, COLS), F32),
            jax.ShapeDtypeStruct((FIELDS - CH, HALF_X, COLS_X), F32),
        ],
        [SMEM] + [HBM] * 5 + [VMEM] * 5 + [HBM],
        [VMEM] * 2,
        [pltpu.VMEM((FIELDS, ROWS_X, COLS_X), F32), pltpu.VMEM((ROWS, COLS), jnp.int32)]
        + step_scratch(ROWS_X)
        + [pltpu.SemaphoreType.DMA((5,))],
        flops=1 << 28,
        mib=60,
    )(where, state, *statics, *halos, gate)


def control_halo_kernel(fw, fe, rows, cw, ce, out):
    for k in range(8):
        out[k] = rows[8 * k : 8 * k + 8, :]
    for i in range(18):
        out[8 + i // 3, :, 128 * (i % 3) : 128 * (i % 3) + 128] = jnp.zeros((8, 128), F32)
    lane = iota((8, 128), 1)
    for i in range(17):
        r = slice(8 * i, 8 * i + 8)
        w, e = (fw[r, :], fe[r, :]) if i < 16 else (cw[...], ce[...])
        s = jnp.where(lane < 64, w, pltpu.roll(e, 64, 1))
        out[8 + i // 3, :, 128 * (i % 3) : 128 * (i % 3) + 128] = s
    out[14:16] = jnp.zeros((2, 8, COLS), F32)


def send(value, pairs):
    return lax.ppermute(value, "member", pairs)


CHUNKS = 4


def staged(copies, buffer, sem):
    n = CH // CHUNKS
    both = []
    for i, (src, dst) in enumerate(copies):
        for j in range(CHUNKS):
            ch, s = slice(n * j, n * j + n), CHUNKS * i + j
            one = pltpu.make_async_copy(src.at[ch], buffer.at[i, ch], sem.at[2 * s])
            both.append((one, pltpu.make_async_copy(buffer.at[i, ch], dst.at[ch, 0:HALF_X, :], sem.at[2 * s + 1])))
            one.start()
    for one, two in both:
        one.wait()
        two.start()
    for one, two in both:
        two.wait()


STAGE = [pltpu.VMEM((2, CH, HALF_X, COLS), F32), pltpu.SemaphoreType.DMA((4 * CHUNKS,))]


def cut_kernel(where, state, low, top, buffer, sem):
    @pl.when(where[2] == 0)
    def _():
        staged(
            [(state.at[:, 0:HALF_X, :], top), (state.at[:, ROWS - HALF_X : ROWS, :], low)], buffer, sem
        )


def spread_first(where, state):
    shape = jax.ShapeDtypeStruct((CH, HALF_X, COLS), F32)
    low, top = call(cut_kernel, [shape, shape], [SMEM, HBM], [HBM] * 2, STAGE, mib=62)(where, state)
    return low, top, send(top, [(0, 2)]), send(low, [(0, 7)])


def relay_kernel(where, u, v, p1, m1, gate, u_out, v_out, buffer, sem):
    @pl.when(where[2] == 2)
    def _():
        staged([(p1, u_out)], buffer, sem)

    @pl.when(where[2] == 7)
    def _():
        staged([(m1, v_out)], buffer, sem)


def spread_rest(where, u, v, p1, m1, halo):
    m = where[2]
    for_two, for_seven = send(halo, [(0, 2)]), send(halo, [(0, 7)])
    known = jnp.where(m == 2, for_two, jnp.where(m == 7, for_seven, halo))
    u, v = call(
        relay_kernel, [u, v], [SMEM] + [HBM] * 4 + [ANY], [HBM] * 2, STAGE, mib=60, aliases={1: 0, 2: 1}
    )(where, u, v, p1, m1, known)
    p2 = send(u, [(0, 3), (2, 4)])
    m2 = send(v, [(0, 6), (7, 5)])
    e0 = send(u, [(0, 1)])
    on = send(known, [(0, 1), (2, 4), (7, 5)])
    across = send(known, [(2, 3), (7, 6)])
    return (v, e0, p1, p2, m2, m1), (known, on, across), u


HOLDER = ((0,), (1,), (2,), (3, 4), (5, 6), (7,))
HALO_HOLDER = (0, 1, 0, 2, 1, 1, 2, 0)


def control_kernel(where, *refs):
    arrays, halos, (static, out, x, y, ub, vb, h2, near, halo, strip, sem) = refs[:6], refs[6:9], refs[9:]
    first = where[1] == 0
    m = where[2]
    for array, members in zip(arrays, HOLDER):
        for member in members:
            r0, r1 = (0, HALF) if member % 2 == 0 else (8, 0)

            @pl.when(m == member)
            def _(array=array, r0=r0, r1=r1, source=halos[HALO_HOLDER[member]]):
                one = pltpu.make_async_copy(array.at[:, r0 : r0 + HALF, :], x.at[:, 0:HALF, 0:COLS], sem.at[0])
                two = pltpu.make_async_copy(array.at[:, r1 : r1 + 8, :], near, sem.at[1])
                three = pltpu.make_async_copy(source, halo, sem.at[2])
                one.start()
                two.start()
                three.start()
                one.wait()
                two.wait()
                three.wait()

    for i in range(17):
        strip[8 * i : 8 * i + 8, :] = halo[8 + i // 3, :, 128 * (i % 3) : 128 * (i % 3) + 128]

    def margin(k, s):
        lane = iota(s.shape, 1)
        return jnp.where(
            lane < 64, pltpu.roll(s, 64 - HALO * k, 1), pltpu.roll(s, 124 - HALO * k, 1)
        )

    sub = iota((8, COLS), 0)
    inner = (sub < 4) == first
    got = (sub < 4) == (where[0] == 0)
    s_main = strip[pl.ds(pl.multiple_of(jnp.where(first, 0, HALF), 8), HALF), :]
    s_near = strip[pl.ds(pl.multiple_of(jnp.where(first, HALF, HALF - 8), 8), 8), :]
    s_edge = jnp.where(inner[:, :128], s_near, jnp.where(got[:, :128], strip[ROWS:ROWS_X, :], 0.0))
    for k in range(CH):
        x[k, 0:HALF, COLS:COLS_X] = margin(k, s_main)
        x[k, HALF:HALF_X, COLS:COLS_X] = margin(k, s_edge)
        j, flip = row_slot(k)
        tile = halo[j]
        if flip:
            tile = pltpu.roll(tile, 4, 0)
        x[k, HALF:HALF_X, 0:COLS] = jnp.where(inner, near[k], jnp.where(got, tile, 0.0))
    two_steps(x, static, y, ub, vb, h2, out)


def control_steps(where, arrays, halos, static):
    return call(
        control_kernel,
        jax.ShapeDtypeStruct((CH, HALF, COLS), F32),
        [SMEM] + [HBM] * 6 + [ANY] * 3 + [VMEM],
        VMEM,
        [pltpu.VMEM((CH, HALF_X, COLS_X), F32)]
        + step_scratch(HALF_X)
        + [pltpu.VMEM((CH, 8, COLS), F32)] * 2
        + [pltpu.VMEM((ROWS_X, 128), F32), pltpu.SemaphoreType.DMA((3,))],
        flops=1 << 27,
        mib=60,
    )(where, *arrays, *halos, static)


def half_rows(where, other):
    return pl.multiple_of(HALF * (where[1] ^ 1 if other else where[1]), 8)


PARTS = 2


def sums_kernel(other, where, own, control, mask, region, earlier, out, a, b, land, reg_all, rows, sem):
    start = half_rows(where, other)
    n = HALF // PARTS
    copies = []
    for i in range(PARTS):
        at = slice(n * i, n * i + n)
        here = pl.ds(start + n * i, n)
        pairs = [
            (own.at[:, here, :], a.at[:, at, :]),
            (control.at[:, at, :], b.at[:, at, :]),
            (mask.at[here, :], land.at[at, :]),
            (region.at[here, :], reg_all.at[at, :]),
        ]
        copies.append([pltpu.make_async_copy(*pair, sem.at[4 * i + k]) for k, pair in enumerate(pairs)])
        for copy in copies[-1]:
            copy.start()

    def body(t, carry):
        c = tile_at(t)
        acc = None
        for k in range(CH):
            d = a[k, c, :] - b[k, c, :]
            acc = d * d if acc is None else acc + d * d
        oc = land[c, :].astype(F32)
        cell = oc * acc
        reg = reg_all[c, :]
        new = []
        for r in range(REGIONS):
            hit = reg == r
            s = jnp.where(hit, cell, 0.0)
            n = jnp.where(hit, oc, 0.0)
            new.append(carry[2 * r] + (s[:, :128] + s[:, 128:256] + s[:, 256:]))
            new.append(carry[2 * r + 1] + (n[:, :128] + n[:, 128:256] + n[:, 256:]))
        return tuple(new)

    zero = jnp.zeros((8, 128), F32)
    total = (zero,) * (2 * REGIONS)
    for i in range(PARTS):
        for copy in copies[i]:
            copy.wait()
        total = lax.fori_loop(n // 8 * i, n // 8 * (i + 1), body, total)
    lane = iota((8, 128), 1)
    row = zero
    for r in range(REGIONS):
        for j in range(2):
            s = jnp.sum(jnp.sum(total[2 * r + j], axis=0, keepdims=True), axis=1, keepdims=True)
            row = jnp.where(lane == REGIONS * j + r, s, row)
    row = row + earlier[...]
    if not other:
        out[...] = row
        return
    for i in range(out.shape[0]):
        rows[i] = row
    move = pltpu.make_async_copy(rows, out, sem.at[0])
    move.start()
    move.wait()


def half_sums(other, where, own, control, mask, region, earlier):
    shape = (32, 8, 128) if other else (8, 128)
    cells = pltpu.VMEM((HALF, COLS), jnp.int32)
    return call(
        functools.partial(sums_kernel, other),
        jax.ShapeDtypeStruct(shape, F32),
        [SMEM] + [HBM] * 4 + [VMEM],
        HBM if other else VMEM,
        [pltpu.VMEM((CH, HALF, COLS), F32)] * 2
        + [cells, cells, pltpu.VMEM((32, 8, 128), F32), pltpu.SemaphoreType.DMA((4 * PARTS,))],
        mib=56,
    )(where, own, control, mask, region, earlier)


BLOCK = 2


def final_kernel(where, own, mine, theirs, region, parts, target, out, growth, cell):
    @pl.when(pl.program_id(0) == 0)
    def _():
        total = parts[0]
        for i in range(1, 32):
            total = total + parts[i]
        lane = iota((8, 128), 1)
        counts = jnp.where(lane < REGIONS, pltpu.roll(total, 128 - REGIONS, 1), 1.0)
        squares = jnp.where(lane < REGIONS, total, 1.0)
        g = jnp.sqrt(squares / (counts * CH) + EPSILON)
        growth[...] = g[0:1, 0:REGIONS]
        factor = target[...] / g

        def body(t, _):
            c = tile_at(t)
            for j in range(3):
                lanes = slice(128 * j, 128 * j + 128)
                reg = region[c, lanes]
                cell[c, lanes] = jnp.take_along_axis(factor, reg, axis=1, mode="promise_in_bounds")
            return 0

        lax.fori_loop(0, ROWS // 8, body, 0)

    start = HALF // 8 * where[1]
    for ref, s in ((mine, start), (theirs, HALF // 8 - start)):

        def body(t, _):
            c, g = tile_at(t), tile_at(t + s)
            f = cell[g, :]
            for k in range(BLOCK):
                q = ref[k, c, :]
                out[k, g, :] = q + f * (own[k, g, :] - q)
            return 0

        lax.fori_loop(0, HALF // 8, body, 0)


def rescale(where, own, mine, theirs, region, parts, target):
    target = jnp.broadcast_to(jnp.pad(target, (0, 128 - REGIONS), constant_values=1.0), (8, 128))

    def cut(rows):
        return pl.BlockSpec((BLOCK, rows, COLS), lambda i: (i, 0, 0))

    row = pl.BlockSpec((1, REGIONS), lambda i: (0, 0))
    return pl.pallas_call(
        final_kernel,
        grid=(CH // BLOCK,),
        out_shape=[jax.ShapeDtypeStruct((CH, ROWS, COLS), F32), jax.ShapeDtypeStruct((1, REGIONS), F32)],
        in_specs=[SMEM, cut(ROWS), cut(HALF), cut(HALF)] + [VMEM] * 3,
        out_specs=[cut(ROWS), row],
        scratch_shapes=[pltpu.VMEM((ROWS, COLS), F32)],
        compiler_params=pltpu.CompilerParams(vmem_limit_bytes=62 << 20),
        cost_estimate=pl.CostEstimate(flops=1 << 22, bytes_accessed=10 << 20, transcendentals=0),
    )(where, own, mine, theirs, region, parts, target)


def per_device(member_state, depth, rotation, diff, mask, region, target):
    state = member_state[0]
    statics = (depth, rotation, diff, mask)
    m = lax.axis_index("member")
    where = jnp.stack([lax.axis_index("lat"), m % 2, m]).astype(jnp.int32)
    first = spread_first(where, state)
    halos = exchange(*pack(where, state, statics))
    halo = call(control_halo_kernel, jax.ShapeDtypeStruct((CH, 8, COLS), F32), [VMEM] * 5, VMEM)(*halos)
    arrays, control_halos, gate = spread_rest(where, *first, halo)
    own, static = own_steps(where, state, statics, halos, gate)
    mine = control_steps(where, arrays, control_halos, static)
    theirs = send(mine, [(i, i ^ 1) for i in range(8)])
    parts = half_sums(False, where, own, mine, mask, region, jnp.zeros((8, 128), F32))
    parts = half_sums(True, where, own, theirs, mask, region, parts)
    parts = lax.all_to_all(parts, ("lon", "lat"), 0, 0)
    bred, growth = rescale(where, own, mine, theirs, region, parts, target)
    return bred[None], growth


def solution(mesh):
    return jax.shard_map(
        per_device,
        mesh=mesh,
        in_specs=(
            P("member", None, "lat", "lon"),
            P("lat", "lon"),
            P("lat", "lon"),
            P(None, "lat", "lon"),
            P("lat", "lon"),
            P("lat", "lon"),
            P(),
        ),
        out_specs=(P("member", None, "lat", "lon"), P("member", None)),
        check_vma=False,
    )
```

```python
import functools
import jax
import jax.numpy as jnp
from jax import lax
from jax.experimental import pallas as pl
from jax.experimental.pallas import tpu as pltpu
from jax.sharding import PartitionSpec as P

LEV = 5
CH = 16
FIELDS = 24
REGIONS = 16
ROWS, COLS = 128, 384
ROWS_X, COLS_X = 136, 512
HALF, HALF_X = 64, 72
HALO = 4
EPSILON = 1e-06
VMEM = pl.BlockSpec(memory_space=pltpu.VMEM)
ANY = pl.BlockSpec(memory_space=pl.ANY)
SMEM = pl.BlockSpec(memory_space=pltpu.SMEM)
HBM = pl.BlockSpec(memory_space=pltpu.HBM)
F32 = jnp.float32


def call(kernel, out, in_specs, out_specs, scratch=(), flops=1 << 22, nbytes=1 << 23, mib=12):
    return pl.pallas_call(
        kernel,
        out_shape=out,
        in_specs=in_specs,
        out_specs=out_specs,
        scratch_shapes=list(scratch),
        compiler_params=pltpu.CompilerParams(vmem_limit_bytes=mib << 20),
        cost_estimate=pl.CostEstimate(flops=flops, bytes_accessed=nbytes, transcendentals=0),
    )


def iota(shape, dim):
    return lax.broadcasted_iota(jnp.int32, shape, dim)


def row_slot(k):
    return (k % 8, k >= 8) if k < CH else (8 + (k - CH) % 4, k - CH >= 4)


def sources(state, depth, rotation, diff, mask):
    return [(state, slice(0, CH)), (depth, CH), (rotation, CH + 1), (diff, slice(CH + 2, CH + 2 + LEV))]


def fetch(fields, mask, cuts, land, land_cut, sem):
    copies = [pltpu.make_async_copy(mask.at[land_cut], land, sem.at[0])]
    for src, at in fields:
        lead = (slice(None),) if src.shape[:-2] else ()
        for dst, cut in cuts:
            copies.append(pltpu.make_async_copy(src.at[lead + cut], dst.at[at], sem.at[len(copies)]))
    for copy in copies:
        copy.start()
    for copy in copies:
        copy.wait()


def rows_kernel(lat, state, depth, rotation, diff, mask, rows, edge, land, sem):
    upper = lat[0] == 0
    cut = (pl.ds(pl.multiple_of(jnp.where(upper, ROWS - 8, 0), 8), 8), slice(None))
    fetch(sources(state, depth, rotation, diff, mask), mask, [(edge, cut)], land, cut, sem)
    edge[FIELDS - 1] = land[...].astype(F32)
    mine = (iota((8, COLS), 0) >= 4) == upper
    for k in range(FIELDS):
        slot, flip = row_slot(k)
        if not flip:
            pair = k + (8 if k < CH else 4)
            rows[8 * slot : 8 * slot + 8, :] = jnp.where(mine, edge[k], pltpu.roll(edge[pair], 4, 0))


def put(k, a, b, w, e):
    lane = iota(w.shape, 1)
    own = (lane >= HALO * k) & (lane < HALO * k + HALO)
    w = jnp.where(own, pltpu.roll(a, HALO * k, 1) if k else a, w)
    return w, jnp.where(own, pltpu.roll(b, HALO * k + HALO, 1), e)


LEFT, RIGHT = slice(0, 128), slice(COLS - 128, COLS)


def strips_kernel(state, depth, rotation, diff, mask, west, east, lo, hi, land, sem):
    full = slice(None)
    cuts = [(lo, (full, LEFT)), (hi, (full, RIGHT))]
    fetch(sources(state, depth, rotation, diff, mask), mask, cuts, land, (full, full), sem)
    lo[FIELDS - 1] = land[:, LEFT].astype(F32)
    hi[FIELDS - 1] = land[:, RIGHT].astype(F32)
    w = e = jnp.zeros((ROWS, 128), F32)
    for k in range(FIELDS):
        w, e = put(k, lo[k], hi[k], w, e)
    west[...] = w
    east[...] = e


def corners_kernel(lat, rows, west, east, west_out, east_out):
    got = (iota((8, 128), 0) < 4) == (lat[0] == 0)
    w = e = jnp.zeros((8, 128), F32)
    for k in range(FIELDS):
        slot, flip = row_slot(k)
        a, b = rows[8 * slot : 8 * slot + 8, LEFT], rows[8 * slot : 8 * slot + 8, RIGHT]
        if flip:
            a, b = pltpu.roll(a, 4, 0), pltpu.roll(b, 4, 0)
        w, e = put(k, a, b, w, e)
    west_out[0:ROWS, :] = west[...]
    east_out[0:ROWS, :] = east[...]
    west_out[ROWS:ROWS_X, :] = jnp.where(got, w, 0.0)
    east_out[ROWS:ROWS_X, :] = jnp.where(got, e, 0.0)


def exchange(where, state, statics):
    n = lax.axis_size("lon")
    up = [(i, (i + 1) % n) for i in range(n)]
    down = [((i + 1) % n, i) for i in range(n)]

    def shape(*dims):
        return jax.ShapeDtypeStruct(dims, F32)

    rows = call(
        rows_kernel,
        shape(FIELDS * 4, COLS),
        [SMEM] + [HBM] * 5,
        VMEM,
        [pltpu.VMEM((FIELDS, 8, COLS), F32), pltpu.VMEM((8, COLS), jnp.int32), pltpu.SemaphoreType.DMA((5,))],
        mib=62,
    )(where, state, *statics)
    rows = lax.ppermute(rows, "lat", [(0, 1), (1, 0)])
    strip = pltpu.VMEM((FIELDS, ROWS, 128), F32)
    west, east = call(
        strips_kernel,
        [shape(ROWS, 128)] * 2,
        [HBM] * 5,
        [VMEM] * 2,
        [strip, strip, pltpu.VMEM((ROWS, COLS), jnp.int32), pltpu.SemaphoreType.DMA((9,))],
        mib=60,
    )(state, *statics)
    west, east = call(corners_kernel, [shape(ROWS_X, 128)] * 2, [SMEM] + [VMEM] * 3, [VMEM] * 2)(
        where, rows, west, east
    )
    return lax.ppermute(east, "lon", up), lax.ppermute(west, "lon", down), rows


def fill_halo(x, lat, from_west, from_east, rows):
    lane = iota((ROWS_X, 128), 1)
    got = (iota((8, COLS), 0) < 4) == (lat[0] == 0)
    w, e = from_west[...], from_east[...]
    for k in range(FIELDS):
        a = pltpu.roll(e, (128 - HALO * k) % 128, 1) if k else e
        x[k, :, COLS:COLS_X] = jnp.where(lane < 64, a, pltpu.roll(w, (124 - HALO * k) % 128, 1))
        j, flip = row_slot(k)
        tile = rows[8 * j : 8 * j + 8, :]
        if flip:
            tile = pltpu.roll(tile, 4, 0)
        x[k, ROWS:ROWS_X, 0:COLS] = jnp.where(got, tile, 0.0)


def tile_at(t):
    return pl.ds(pl.multiple_of(t * 8, 8), 8)


def step(x, static, ub, vb, h2, store, count, tiles):
    sub = iota((8, COLS_X), 0)

    def around(t):
        return tile_at(jnp.where(t == 0, count - 1, t - 1)), tile_at(t), tile_at(jnp.where(t == count - 1, 0, t + 1))

    def north(cur, nxt):
        return pltpu.roll(jnp.where(sub == 0, nxt, cur), 7, 0)

    def south(cur, prv):
        return pltpu.roll(jnp.where(sub == 7, prv, cur), 1, 0)

    def east(cur):
        return pltpu.roll(cur, COLS_X - 1, 1)

    def west(cur):
        return pltpu.roll(cur, 1, 1)

    def sums(t, _):
        c = tile_at(t)
        u = x[1, c, :]
        v = x[1 + LEV, c, :]
        for l in range(1, LEV):
            u = u + x[1 + l, c, :]
            v = v + x[1 + LEV + l, c, :]
        ub[c, :] = east(u) - west(u)
        vb[c, :] = v
        return 0

    lax.fori_loop(0, count, sums, 0)

    def surface(t, _):
        p, c, n = around(t)
        v = vb[c, :]
        div = ub[c, :] + (north(v, vb[n, :]) - south(v, vb[p, :]))
        h2[c, :] = static[7, c, :] * (x[0, c, :] - (0.25 / LEV) * static[0, c, :] * div)
        return 0

    lax.fori_loop(0, count, surface, 0)

    def rest(t, _):
        p, c, n = around(t)
        oc = static[7, c, :]
        rot = static[1, c, :]
        h = h2[c, :]
        store(0, c, h)
        px = 0.25 * (east(h) - west(h))
        py = 0.25 * (north(h, h2[n, :]) - south(h, h2[p, :]))
        for l in range(LEV):
            k = static[2 + l, c, :]

            def near(ch):
                q = x[ch, c, :]
                return q, east(q), west(q), north(q, x[ch, n, :]), south(q, x[ch, p, :])

            q, e, w, a, b = near(1 + 2 * LEV + l)
            cx = e - w
            cy = a - b
            c0 = q + k * ((e + w) + (a + b) - 4.0 * q)
            u, e, w, a, b = near(1 + l)
            lap_u = (e + w) + (a + b) - 4.0 * u
            v, e, w, a, b = near(1 + LEV + l)
            lap_v = (e + w) + (a + b) - 4.0 * v
            u2 = oc * (u + rot * v - px - 0.1 * cx + k * lap_u)
            v2 = oc * (v - rot * u - py - 0.1 * cy + k * lap_v)
            store(1 + l, c, u2)
            store(1 + LEV + l, c, v2)
            store(1 + 2 * LEV + l, c, oc * (c0 - 0.05 * (u2 * cx + v2 * cy)))
        return 0

    lax.fori_loop(0, tiles, rest, 0)


def two_steps(x, static, y, ub, vb, h2, out):
    count = x.shape[1] // 8

    def keep(ch, c, value):
        y[ch, c, :] = value

    def give(ch, c, value):
        out[ch, c, :] = value[:, :COLS]

    step(x, static, ub, vb, h2, keep, count, count)
    step(y, static, ub, vb, h2, give, count, count - 1)


def step_scratch(rows):
    return [pltpu.VMEM((CH, rows, COLS_X), F32)] + [pltpu.VMEM((rows, COLS_X), F32)] * 3


def own_kernel(where, state, depth, rotation, diff, mask, fw, fe, rows, gate, out, part, x, land, y, ub, vb, h2, sem):
    main = (slice(0, ROWS), slice(0, COLS))
    copies = [
        pltpu.make_async_copy(state, x.at[(slice(0, CH),) + main], sem.at[0]),
        pltpu.make_async_copy(depth, x.at[(CH,) + main], sem.at[1]),
        pltpu.make_async_copy(rotation, x.at[(CH + 1,) + main], sem.at[2]),
        pltpu.make_async_copy(diff, x.at[(slice(CH + 2, CH + 2 + LEV),) + main], sem.at[3]),
    ]
    copies.append(pltpu.make_async_copy(mask, land, sem.at[4]))
    for copy in copies:
        copy.start()
    fill_halo(x, where, fw, fe, rows)
    for copy in copies:
        copy.wait()
    x[(FIELDS - 1,) + main] = land[...].astype(F32)
    first = where[1] == 0
    tiles = HALF // 8
    sub = iota((8, COLS_X), 0)
    for j in range(CH, FIELDS):

        def body(t, _):
            part[j - CH, tile_at(t), :] = x[j, tile_at(t + jnp.where(first, 0, tiles)), :]
            return 0

        lax.fori_loop(0, tiles, body, 0)
        n = x[j, tile_at(jnp.where(first, tiles, 2 * tiles)), :]
        p = x[j, tile_at(jnp.where(first, 2 * tiles, tiles - 1)), :]
        part[j - CH, HALF:HALF_X, :] = jnp.where(sub < 4, n, p)
    two_steps(x, x.at[CH:FIELDS], y, ub, vb, h2, out)


def own_steps(where, state, statics, halos, gate):
    return call(
        own_kernel,
        [
            jax.ShapeDtypeStruct((CH, ROWS, COLS), F32),
            jax.ShapeDtypeStruct((FIELDS - CH, HALF_X, COLS_X), F32),
        ],
        [SMEM] + [HBM] * 5 + [VMEM] * 3 + [HBM],
        [VMEM] * 2,
        [pltpu.VMEM((FIELDS, ROWS_X, COLS_X), F32), pltpu.VMEM((ROWS, COLS), jnp.int32)]
        + step_scratch(ROWS_X)
        + [pltpu.SemaphoreType.DMA((5,))],
        flops=1 << 28,
        mib=28,
    )(where, state, *statics, *halos, gate)


def control_halo_kernel(fw, fe, rows, out):
    for k in range(8):
        out[k] = rows[8 * k : 8 * k + 8, :]
    for i in range(18):
        out[8 + i // 3, :, 128 * (i % 3) : 128 * (i % 3) + 128] = jnp.zeros((8, 128), F32)
    lane = iota((8, 128), 1)
    for i in range(17):
        r = slice(8 * i, 8 * i + 8)
        s = jnp.where(lane < 64, fw[r, :], pltpu.roll(fe[r, :], 64, 1))
        out[8 + i // 3, :, 128 * (i % 3) : 128 * (i % 3) + 128] = s
    out[14:16] = jnp.zeros((2, 8, COLS), F32)


def send(value, pairs):
    return lax.ppermute(value, "member", pairs)


CHUNKS = 4


def staged(copies, buffer, sem):
    n = CH // CHUNKS
    both = []
    for i, (src, dst) in enumerate(copies):
        for j in range(CHUNKS):
            ch, s = slice(n * j, n * j + n), CHUNKS * i + j
            one = pltpu.make_async_copy(src.at[ch], buffer.at[i, ch], sem.at[2 * s])
            both.append((one, pltpu.make_async_copy(buffer.at[i, ch], dst.at[ch, 0:HALF_X, :], sem.at[2 * s + 1])))
            one.start()
    for one, two in both:
        one.wait()
        two.start()
    for one, two in both:
        two.wait()


STAGE = [pltpu.VMEM((2, CH, HALF_X, COLS), F32), pltpu.SemaphoreType.DMA((4 * CHUNKS,))]


def cut_kernel(where, state, top, low, buffer, sem):
    @pl.when(where[2] == 0)
    def _():
        staged(
            [(state.at[:, 0:HALF_X, :], top), (state.at[:, ROWS - HALF_X : ROWS, :], low)], buffer, sem
        )


def spread_first(where, state):
    shape = jax.ShapeDtypeStruct((CH, HALF_X, COLS), F32)
    top, low = call(cut_kernel, [shape, shape], [SMEM, HBM], [HBM] * 2, STAGE, mib=62)(where, state)
    return top, low, send(top, [(0, 2)]), send(low, [(0, 7)])


def relay_kernel(where, top, low, p1, m1, halo, u, v, buffer, sem, ride, ride_sem):
    m = where[2]

    def move(pairs):
        one = pltpu.make_async_copy(halo, ride, ride_sem.at[0])
        one.start()
        one.wait()
        more = [
            pltpu.make_async_copy(ride, dst.at[:, HALF_X : HALF_X + 8, :], ride_sem.at[1 + i])
            for i, (_, dst) in enumerate(pairs)
        ]
        for copy in more:
            copy.start()
        staged(pairs, buffer, sem)
        for copy in more:
            copy.wait()

    @pl.when(m == 0)
    def _():
        move([(low, u), (top, v)])

    @pl.when(m == 2)
    def _():
        move([(p1, u)])

    @pl.when(m == 7)
    def _():
        move([(m1, v)])


def spread_rest(where, top, low, p1, m1, halo):
    m = where[2]
    for_two, for_seven = send(halo, [(0, 2)]), send(halo, [(0, 7)])
    halo = jnp.where(m == 2, for_two, jnp.where(m == 7, for_seven, halo))
    shape = jax.ShapeDtypeStruct((CH, HALF_X + 8, COLS), F32)
    u, v = call(
        relay_kernel,
        [shape, shape],
        [SMEM] + [HBM] * 4 + [ANY],
        [HBM] * 2,
        STAGE + [pltpu.VMEM((CH, 8, COLS), F32), pltpu.SemaphoreType.DMA((3,))],
    )(where, top, low, p1, m1, halo)
    p2 = send(u, [(0, 3), (2, 4)])
    m2 = send(v, [(0, 6), (7, 5)])
    e0 = send(u, [(0, 1)])
    return (top, e0, p1, p2, m2, m1), halo, u


HOLDER = ((0,), (1,), (2,), (3, 4), (5, 6), (7,))


def control_kernel(where, *refs):
    arrays, (early, static, out, x, y, ub, vb, h2, near, halo, strip, sem) = refs[:6], refs[6:]
    first = where[1] == 0
    m = where[2]
    for array, members in zip(arrays, HOLDER):
        for member in members:
            r0, r1 = (0, HALF) if member % 2 == 0 else (8, 0)

            @pl.when(m == member)
            def _(array=array, r0=r0, r1=r1):
                one = pltpu.make_async_copy(array.at[:, r0 : r0 + HALF, :], x.at[:, 0:HALF, 0:COLS], sem.at[0])
                two = pltpu.make_async_copy(array.at[:, r1 : r1 + 8, :], near, sem.at[1])
                rides = array.shape[1] > HALF_X
                source = array.at[:, HALF_X : HALF_X + 8, :] if rides else early
                three = pltpu.make_async_copy(source, halo, sem.at[2])
                one.start()
                two.start()
                three.start()
                one.wait()
                two.wait()
                three.wait()

    for i in range(17):
        strip[8 * i : 8 * i + 8, :] = halo[8 + i // 3, :, 128 * (i % 3) : 128 * (i % 3) + 128]

    def margin(k, s):
        lane = iota(s.shape, 1)
        return jnp.where(
            lane < 64, pltpu.roll(s, 64 - HALO * k, 1), pltpu.roll(s, 124 - HALO * k, 1)
        )

    sub = iota((8, COLS), 0)
    inner = (sub < 4) == first
    got = (sub < 4) == (where[0] == 0)
    s_main = strip[pl.ds(pl.multiple_of(jnp.where(first, 0, HALF), 8), HALF), :]
    s_near = strip[pl.ds(pl.multiple_of(jnp.where(first, HALF, HALF - 8), 8), 8), :]
    s_edge = jnp.where(inner[:, :128], s_near, jnp.where(got[:, :128], strip[ROWS:ROWS_X, :], 0.0))
    for k in range(CH):
        x[k, 0:HALF, COLS:COLS_X] = margin(k, s_main)
        x[k, HALF:HALF_X, COLS:COLS_X] = margin(k, s_edge)
        j, flip = row_slot(k)
        tile = halo[j]
        if flip:
            tile = pltpu.roll(tile, 4, 0)
        x[k, HALF:HALF_X, 0:COLS] = jnp.where(inner, near[k], jnp.where(got, tile, 0.0))
    two_steps(x, static, y, ub, vb, h2, out)


def control_steps(where, arrays, halo, static):
    return call(
        control_kernel,
        jax.ShapeDtypeStruct((CH, HALF, COLS), F32),
        [SMEM] + [HBM] * 6 + [ANY, VMEM],
        VMEM,
        [pltpu.VMEM((CH, HALF_X, COLS_X), F32)]
        + step_scratch(HALF_X)
        + [pltpu.VMEM((CH, 8, COLS), F32)] * 2
        + [pltpu.VMEM((ROWS_X, 128), F32), pltpu.SemaphoreType.DMA((3,))],
        flops=1 << 27,
        mib=16,
    )(where, *arrays, halo, static)


def sums_kernel(other, where, own, control, mask, region, earlier, out, *copy):
    start = HALF // 8 * (where[1] ^ 1 if other else where[1])

    def body(t, carry):
        c, g = tile_at(t), tile_at(t + start)
        acc = None
        for k in range(CH):
            d = own[k, g, :] - control[k, c, :]
            acc = d * d if acc is None else acc + d * d
        oc = mask[g, :].astype(F32)
        cell = oc * acc
        reg = region[g, :]
        new = []
        for r in range(REGIONS):
            hit = reg == r
            s = jnp.where(hit, cell, 0.0)
            n = jnp.where(hit, oc, 0.0)
            new.append(carry[2 * r] + (s[:, :128] + s[:, 128:256] + s[:, 256:]))
            new.append(carry[2 * r + 1] + (n[:, :128] + n[:, 128:256] + n[:, 256:]))
        return tuple(new)

    zero = jnp.zeros((8, 128), F32)
    total = lax.fori_loop(0, HALF // 8, body, (zero,) * (2 * REGIONS))
    lane = iota((8, 128), 1)
    row = zero
    for r in range(REGIONS):
        for j in range(2):
            s = jnp.sum(jnp.sum(total[2 * r + j], axis=0, keepdims=True), axis=1, keepdims=True)
            row = jnp.where(lane == REGIONS * j + r, s, row)
    if other:
        row = row + earlier[...]
        copies, sem = copy
        for i in range(out.shape[0]):
            copies[i] = row
        move = pltpu.make_async_copy(copies, out, sem.at[0])
        move.start()
        move.wait()
    else:
        out[...] = row + earlier[...]


def half_sums(other, where, own, control, mask, region, earlier):
    shape = (32, 8, 128) if other else (8, 128)
    return call(
        functools.partial(sums_kernel, other),
        jax.ShapeDtypeStruct(shape, F32),
        [SMEM] + [VMEM] * 5,
        HBM if other else VMEM,
        [pltpu.VMEM(shape, F32), pltpu.SemaphoreType.DMA((1,))] if other else (),
        mib=4,
    )(where, own, control, mask, region, earlier)


BLOCK = 4


def final_kernel(where, own, mine, theirs, region, parts, target, out, growth, cell):
    @pl.when(pl.program_id(0) == 0)
    def _():
        total = parts[0]
        for i in range(1, 32):
            total = total + parts[i]
        lane = iota((8, 128), 1)
        counts = jnp.where(lane < REGIONS, pltpu.roll(total, 128 - REGIONS, 1), 1.0)
        squares = jnp.where(lane < REGIONS, total, 1.0)
        g = jnp.sqrt(squares / (counts * CH) + EPSILON)
        growth[...] = g[0:1, 0:REGIONS]
        factor = target[...] / g

        def body(t, _):
            c = tile_at(t)
            for j in range(3):
                lanes = slice(128 * j, 128 * j + 128)
                reg = region[c, lanes]
                cell[c, lanes] = jnp.take_along_axis(factor, reg, axis=1, mode="promise_in_bounds")
            return 0

        lax.fori_loop(0, ROWS // 8, body, 0)

    start = HALF // 8 * where[1]
    lead = pl.program_id(0) * BLOCK
    for ref, s in ((mine, start), (theirs, HALF // 8 - start)):

        def body(t, _):
            c, g = tile_at(t), tile_at(t + s)
            f = cell[g, :]
            for k in range(BLOCK):
                q = ref[lead + k, c, :]
                out[k, g, :] = q + f * (own[lead + k, g, :] - q)
            return 0

        lax.fori_loop(0, HALF // 8, body, 0)


def rescale(where, own, mine, theirs, region, parts, target):
    target = jnp.broadcast_to(jnp.pad(target, (0, 128 - REGIONS), constant_values=1.0), (8, 128))

    cut = pl.BlockSpec((BLOCK, ROWS, COLS), lambda i: (i, 0, 0))
    row = pl.BlockSpec((1, REGIONS), lambda i: (0, 0))
    return pl.pallas_call(
        final_kernel,
        grid=(CH // BLOCK,),
        out_shape=[jax.ShapeDtypeStruct((CH, ROWS, COLS), F32), jax.ShapeDtypeStruct((1, REGIONS), F32)],
        in_specs=[SMEM] + [VMEM] * 6,
        out_specs=[cut, row],
        scratch_shapes=[pltpu.VMEM((ROWS, COLS), F32)],
        compiler_params=pltpu.CompilerParams(vmem_limit_bytes=8 << 20),
        cost_estimate=pl.CostEstimate(flops=1 << 22, bytes_accessed=10 << 20, transcendentals=0),
    )(where, own, mine, theirs, region, parts, target)


def per_device(member_state, depth, rotation, diff, mask, region, target):
    state = member_state[0]
    statics = (depth, rotation, diff, mask)
    m = lax.axis_index("member")
    where = jnp.stack([lax.axis_index("lat"), m % 2, m]).astype(jnp.int32)
    first = spread_first(where, state)
    halos = exchange(where, state, statics)
    halo = call(control_halo_kernel, jax.ShapeDtypeStruct((CH, 8, COLS), F32), [VMEM] * 3, VMEM)(*halos)
    arrays, halo, gate = spread_rest(where, *first, halo)
    own, static = own_steps(where, state, statics, halos, gate)
    mine = control_steps(where, arrays, halo, static)
    theirs = send(mine, [(i, i ^ 1) for i in range(8)])
    parts = half_sums(False, where, own, mine, mask, region, jnp.zeros((8, 128), F32))
    parts = half_sums(True, where, own, theirs, mask, region, parts)
    parts = lax.all_to_all(parts, ("lon", "lat"), 0, 0)
    bred, growth = rescale(where, own, mine, theirs, region, parts, target)
    return bred[None], growth


def solution(mesh):
    return jax.shard_map(
        per_device,
        mesh=mesh,
        in_specs=(
            P("member", None, "lat", "lon"),
            P("lat", "lon"),
            P("lat", "lon"),
            P(None, "lat", "lon"),
            P("lat", "lon"),
            P("lat", "lon"),
            P(),
        ),
        out_specs=(P("member", None, "lat", "lon"), P("member", None)),
        check_vma=False,
    )
```

```python
import functools
import jax
import jax.numpy as jnp
from jax import lax
from jax.experimental import pallas as pl
from jax.experimental.pallas import tpu as pltpu
from jax.sharding import PartitionSpec as P

LEV = 5
CH = 16
FIELDS = 24
REGIONS = 16
ROWS, COLS = 128, 384
ROWS_X, COLS_X = 136, 512
HALF, HALF_X = 64, 72
HALO = 4
EPSILON = 1e-06
VMEM = pl.BlockSpec(memory_space=pltpu.VMEM)
ANY = pl.BlockSpec(memory_space=pl.ANY)
SMEM = pl.BlockSpec(memory_space=pltpu.SMEM)
HBM = pl.BlockSpec(memory_space=pltpu.HBM)
F32 = jnp.float32


def call(kernel, out, in_specs, out_specs, scratch=(), flops=1 << 22, nbytes=1 << 23, mib=12, aliases=None):
    return pl.pallas_call(
        kernel,
        out_shape=out,
        in_specs=in_specs,
        out_specs=out_specs,
        scratch_shapes=list(scratch),
        input_output_aliases=aliases or {},
        compiler_params=pltpu.CompilerParams(vmem_limit_bytes=mib << 20),
        cost_estimate=pl.CostEstimate(flops=flops, bytes_accessed=nbytes, transcendentals=0),
    )


def iota(shape, dim):
    return lax.broadcasted_iota(jnp.int32, shape, dim)


def row_slot(k):
    return (k % 8, k >= 8) if k < CH else (8 + (k - CH) % 4, k - CH >= 4)


def sources(state, depth, rotation, diff, mask):
    return [(state, slice(0, CH)), (depth, CH), (rotation, CH + 1), (diff, slice(CH + 2, CH + 2 + LEV))]


def fetch(fields, mask, cuts, land, land_cut, sem):
    copies = [pltpu.make_async_copy(mask.at[land_cut], land, sem.at[0])]
    for src, at in fields:
        lead = (slice(None),) if src.shape[:-2] else ()
        for dst, cut in cuts:
            copies.append(pltpu.make_async_copy(src.at[lead + cut], dst.at[at], sem.at[len(copies)]))
    for copy in copies:
        copy.start()
    for copy in copies:
        copy.wait()


def rows_kernel(lat, state, depth, rotation, diff, mask, rows, edge, land, sem):
    upper = lat[0] == 0
    cut = (pl.ds(pl.multiple_of(jnp.where(upper, ROWS - 8, 0), 8), 8), slice(None))
    fetch(sources(state, depth, rotation, diff, mask), mask, [(edge, cut)], land, cut, sem)
    edge[FIELDS - 1] = land[...].astype(F32)
    mine = (iota((8, COLS), 0) >= 4) == upper
    for k in range(FIELDS):
        slot, flip = row_slot(k)
        if not flip:
            pair = k + (8 if k < CH else 4)
            rows[8 * slot : 8 * slot + 8, :] = jnp.where(mine, edge[k], pltpu.roll(edge[pair], 4, 0))


def put(k, a, b, w, e):
    lane = iota(w.shape, 1)
    own = (lane >= HALO * k) & (lane < HALO * k + HALO)
    w = jnp.where(own, pltpu.roll(a, HALO * k, 1) if k else a, w)
    return w, jnp.where(own, pltpu.roll(b, HALO * k + HALO, 1), e)


LEFT, RIGHT = slice(0, 128), slice(COLS - 128, COLS)


def strips_kernel(state, depth, rotation, diff, mask, west, east, lo, hi, land, sem):
    full = slice(None)
    cuts = [(lo, (full, LEFT)), (hi, (full, RIGHT))]
    fetch(sources(state, depth, rotation, diff, mask), mask, cuts, land, (full, full), sem)
    lo[FIELDS - 1] = land[:, LEFT].astype(F32)
    hi[FIELDS - 1] = land[:, RIGHT].astype(F32)
    w = e = jnp.zeros((ROWS, 128), F32)
    for k in range(FIELDS):
        w, e = put(k, lo[k], hi[k], w, e)
    west[...] = w
    east[...] = e


def corners_kernel(lat, rows, west, east, west_out, east_out):
    got = (iota((8, 128), 0) < 4) == (lat[0] == 0)
    w = e = jnp.zeros((8, 128), F32)
    for k in range(FIELDS):
        slot, flip = row_slot(k)
        a, b = rows[8 * slot : 8 * slot + 8, LEFT], rows[8 * slot : 8 * slot + 8, RIGHT]
        if flip:
            a, b = pltpu.roll(a, 4, 0), pltpu.roll(b, 4, 0)
        w, e = put(k, a, b, w, e)
    west_out[0:ROWS, :] = west[...]
    east_out[0:ROWS, :] = east[...]
    west_out[ROWS:ROWS_X, :] = jnp.where(got, w, 0.0)
    east_out[ROWS:ROWS_X, :] = jnp.where(got, e, 0.0)


def exchange(where, state, statics):
    n = lax.axis_size("lon")
    up = [(i, (i + 1) % n) for i in range(n)]
    down = [((i + 1) % n, i) for i in range(n)]

    def shape(*dims):
        return jax.ShapeDtypeStruct(dims, F32)

    rows = call(
        rows_kernel,
        shape(FIELDS * 4, COLS),
        [SMEM] + [HBM] * 5,
        VMEM,
        [pltpu.VMEM((FIELDS, 8, COLS), F32), pltpu.VMEM((8, COLS), jnp.int32), pltpu.SemaphoreType.DMA((5,))],
        mib=62,
    )(where, state, *statics)
    rows = lax.ppermute(rows, "lat", [(0, 1), (1, 0)])
    strip = pltpu.VMEM((FIELDS, ROWS, 128), F32)
    west, east = call(
        strips_kernel,
        [shape(ROWS, 128)] * 2,
        [HBM] * 5,
        [VMEM] * 2,
        [strip, strip, pltpu.VMEM((ROWS, COLS), jnp.int32), pltpu.SemaphoreType.DMA((9,))],
        mib=58,
    )(state, *statics)
    west, east = call(corners_kernel, [shape(ROWS_X, 128)] * 2, [SMEM] + [VMEM] * 3, [VMEM] * 2)(
        where, rows, west, east
    )
    return lax.ppermute(east, "lon", up), lax.ppermute(west, "lon", down), rows


def fill_halo(x, lat, from_west, from_east, rows):
    lane = iota((ROWS_X, 128), 1)
    got = (iota((8, COLS), 0) < 4) == (lat[0] == 0)
    w, e = from_west[...], from_east[...]
    for k in range(FIELDS):
        a = pltpu.roll(e, (128 - HALO * k) % 128, 1) if k else e
        x[k, :, COLS:COLS_X] = jnp.where(lane < 64, a, pltpu.roll(w, (124 - HALO * k) % 128, 1))
        j, flip = row_slot(k)
        tile = rows[8 * j : 8 * j + 8, :]
        if flip:
            tile = pltpu.roll(tile, 4, 0)
        x[k, ROWS:ROWS_X, 0:COLS] = jnp.where(got, tile, 0.0)


def tile_at(t):
    return pl.ds(pl.multiple_of(t * 8, 8), 8)


def step(x, static, ub, vb, h2, store, count, tiles):
    sub = iota((8, COLS_X), 0)

    def around(t):
        return tile_at(jnp.where(t == 0, count - 1, t - 1)), tile_at(t), tile_at(jnp.where(t == count - 1, 0, t + 1))

    def north(cur, nxt):
        return pltpu.roll(jnp.where(sub == 0, nxt, cur), 7, 0)

    def south(cur, prv):
        return pltpu.roll(jnp.where(sub == 7, prv, cur), 1, 0)

    def east(cur):
        return pltpu.roll(cur, COLS_X - 1, 1)

    def west(cur):
        return pltpu.roll(cur, 1, 1)

    def sums(t, _):
        c = tile_at(t)
        u = x[1, c, :]
        v = x[1 + LEV, c, :]
        for l in range(1, LEV):
            u = u + x[1 + l, c, :]
            v = v + x[1 + LEV + l, c, :]
        ub[c, :] = east(u) - west(u)
        vb[c, :] = v
        return 0

    lax.fori_loop(0, count, sums, 0)

    def surface(t, _):
        p, c, n = around(t)
        v = vb[c, :]
        div = ub[c, :] + (north(v, vb[n, :]) - south(v, vb[p, :]))
        h2[c, :] = static[7, c, :] * (x[0, c, :] - (0.25 / LEV) * static[0, c, :] * div)
        return 0

    lax.fori_loop(0, count, surface, 0)

    def rest(t, _):
        p, c, n = around(t)
        oc = static[7, c, :]
        rot = static[1, c, :]
        h = h2[c, :]
        store(0, c, h)
        px = 0.25 * (east(h) - west(h))
        py = 0.25 * (north(h, h2[n, :]) - south(h, h2[p, :]))
        for l in range(LEV):
            k = static[2 + l, c, :]

            def near(ch):
                q = x[ch, c, :]
                return q, east(q), west(q), north(q, x[ch, n, :]), south(q, x[ch, p, :])

            q, e, w, a, b = near(1 + 2 * LEV + l)
            cx = e - w
            cy = a - b
            c0 = q + k * ((e + w) + (a + b) - 4.0 * q)
            u, e, w, a, b = near(1 + l)
            lap_u = (e + w) + (a + b) - 4.0 * u
            v, e, w, a, b = near(1 + LEV + l)
            lap_v = (e + w) + (a + b) - 4.0 * v
            u2 = oc * (u + rot * v - px - 0.1 * cx + k * lap_u)
            v2 = oc * (v - rot * u - py - 0.1 * cy + k * lap_v)
            store(1 + l, c, u2)
            store(1 + LEV + l, c, v2)
            store(1 + 2 * LEV + l, c, oc * (c0 - 0.05 * (u2 * cx + v2 * cy)))
        return 0

    lax.fori_loop(0, tiles, rest, 0)


def two_steps(x, static, y, ub, vb, h2, out):
    count = x.shape[1] // 8

    def keep(ch, c, value):
        y[ch, c, :] = value

    def give(ch, c, value):
        out[ch, c, :] = value[:, :COLS]

    step(x, static, ub, vb, h2, keep, count, count)
    step(y, static, ub, vb, h2, give, count, count - 1)


def step_scratch(rows):
    return [pltpu.VMEM((CH, rows, COLS_X), F32)] + [pltpu.VMEM((rows, COLS_X), F32)] * 3


def own_kernel(where, state, depth, rotation, diff, mask, fw, fe, rows, gate, out, part, x, land, y, ub, vb, h2, sem):
    main = (slice(0, ROWS), slice(0, COLS))
    copies = [
        pltpu.make_async_copy(state, x.at[(slice(0, CH),) + main], sem.at[0]),
        pltpu.make_async_copy(depth, x.at[(CH,) + main], sem.at[1]),
        pltpu.make_async_copy(rotation, x.at[(CH + 1,) + main], sem.at[2]),
        pltpu.make_async_copy(diff, x.at[(slice(CH + 2, CH + 2 + LEV),) + main], sem.at[3]),
    ]
    copies.append(pltpu.make_async_copy(mask, land, sem.at[4]))
    for copy in copies:
        copy.start()
    fill_halo(x, where, fw, fe, rows)
    for copy in copies:
        copy.wait()
    x[(FIELDS - 1,) + main] = land[...].astype(F32)
    first = where[1] == 0
    tiles = HALF // 8
    sub = iota((8, COLS_X), 0)
    for j in range(CH, FIELDS):

        def body(t, _):
            part[j - CH, tile_at(t), :] = x[j, tile_at(t + jnp.where(first, 0, tiles)), :]
            return 0

        lax.fori_loop(0, tiles, body, 0)
        n = x[j, tile_at(jnp.where(first, tiles, 2 * tiles)), :]
        p = x[j, tile_at(jnp.where(first, 2 * tiles, tiles - 1)), :]
        part[j - CH, HALF:HALF_X, :] = jnp.where(sub < 4, n, p)
    two_steps(x, x.at[CH:FIELDS], y, ub, vb, h2, out)


def own_steps(where, state, statics, halos, gate):
    return call(
        own_kernel,
        [
            jax.ShapeDtypeStruct((CH, ROWS, COLS), F32),
            jax.ShapeDtypeStruct((FIELDS - CH, HALF_X, COLS_X), F32),
        ],
        [SMEM] + [HBM] * 5 + [VMEM] * 3 + [HBM],
        [VMEM] * 2,
        [pltpu.VMEM((FIELDS, ROWS_X, COLS_X), F32), pltpu.VMEM((ROWS, COLS), jnp.int32)]
        + step_scratch(ROWS_X)
        + [pltpu.SemaphoreType.DMA((5,))],
        flops=1 << 28,
        mib=28,
    )(where, state, *statics, *halos, gate)


def control_halo_kernel(fw, fe, rows, out):
    for k in range(8):
        out[k] = rows[8 * k : 8 * k + 8, :]
    for i in range(18):
        out[8 + i // 3, :, 128 * (i % 3) : 128 * (i % 3) + 128] = jnp.zeros((8, 128), F32)
    lane = iota((8, 128), 1)
    for i in range(17):
        r = slice(8 * i, 8 * i + 8)
        s = jnp.where(lane < 64, fw[r, :], pltpu.roll(fe[r, :], 64, 1))
        out[8 + i // 3, :, 128 * (i % 3) : 128 * (i % 3) + 128] = s
    out[14:16] = jnp.zeros((2, 8, COLS), F32)


def send(value, pairs):
    return lax.ppermute(value, "member", pairs)


CHUNKS = 4


def staged(copies, buffer, sem):
    n = CH // CHUNKS
    both = []
    for i, (src, dst) in enumerate(copies):
        for j in range(CHUNKS):
            ch, s = slice(n * j, n * j + n), CHUNKS * i + j
            one = pltpu.make_async_copy(src.at[ch], buffer.at[i, ch], sem.at[2 * s])
            both.append((one, pltpu.make_async_copy(buffer.at[i, ch], dst.at[ch, 0:HALF_X, :], sem.at[2 * s + 1])))
            one.start()
    for one, two in both:
        one.wait()
        two.start()
    for one, two in both:
        two.wait()


STAGE = [pltpu.VMEM((2, CH, HALF_X, COLS), F32), pltpu.SemaphoreType.DMA((4 * CHUNKS,))]


def cut_kernel(where, state, low, top, buffer, sem):
    @pl.when(where[2] == 0)
    def _():
        staged(
            [(state.at[:, 0:HALF_X, :], top), (state.at[:, ROWS - HALF_X : ROWS, :], low)], buffer, sem
        )


def spread_first(where, state):
    shape = jax.ShapeDtypeStruct((CH, HALF_X, COLS), F32)
    low, top = call(cut_kernel, [shape, shape], [SMEM, HBM], [HBM] * 2, STAGE, mib=62)(where, state)
    return low, top, send(top, [(0, 2)]), send(low, [(0, 7)])


def relay_kernel(where, u, v, p1, m1, gate, u_out, v_out, buffer, sem):
    @pl.when(where[2] == 2)
    def _():
        staged([(p1, u_out)], buffer, sem)

    @pl.when(where[2] == 7)
    def _():
        staged([(m1, v_out)], buffer, sem)


def spread_rest(where, u, v, p1, m1, halo):
    m = where[2]
    known = jnp.where(m == 1, send(halo, [(0, 1)]), halo)
    u, v = call(
        relay_kernel, [u, v], [SMEM] + [HBM] * 4 + [ANY], [HBM] * 2, STAGE, mib=58, aliases={1: 0, 2: 1}
    )(where, u, v, p1, m1, halo)
    p2 = send(u, [(0, 3), (2, 4)])
    m2 = send(v, [(0, 6), (7, 5)])
    e0 = send(u, [(0, 1)])
    return (v, e0, u, p2, m2), (known, send(known, [(0, 3), (1, 6)])), u


def spread_halo_rest(m, known, came):
    known = jnp.where((m == 3) | (m == 6), came, known)
    return known, send(known, [(0, 2), (1, 7), (3, 4), (6, 5)])


HOLDER = ((0, 7), (1,), (2,), (3, 4), (5, 6))
HALO_HOLDER = (0, 0, 1, 0, 1, 1, 0, 1)


def control_kernel(where, *refs):
    arrays, halos, (static, out, x, y, ub, vb, h2, near, halo, strip, sem) = refs[:5], refs[5:7], refs[7:]
    first = where[1] == 0
    m = where[2]
    for array, members in zip(arrays, HOLDER):
        for member in members:
            r0, r1 = (0, HALF) if member % 2 == 0 else (8, 0)

            @pl.when(m == member)
            def _(array=array, r0=r0, r1=r1, source=halos[HALO_HOLDER[member]]):
                one = pltpu.make_async_copy(array.at[:, r0 : r0 + HALF, :], x.at[:, 0:HALF, 0:COLS], sem.at[0])
                two = pltpu.make_async_copy(array.at[:, r1 : r1 + 8, :], near, sem.at[1])
                three = pltpu.make_async_copy(source, halo, sem.at[2])
                one.start()
                two.start()
                three.start()
                one.wait()
                two.wait()
                three.wait()

    for i in range(17):
        strip[8 * i : 8 * i + 8, :] = halo[8 + i // 3, :, 128 * (i % 3) : 128 * (i % 3) + 128]

    def margin(k, s):
        lane = iota(s.shape, 1)
        return jnp.where(
            lane < 64, pltpu.roll(s, 64 - HALO * k, 1), pltpu.roll(s, 124 - HALO * k, 1)
        )

    sub = iota((8, COLS), 0)
    inner = (sub < 4) == first
    got = (sub < 4) == (where[0] == 0)
    s_main = strip[pl.ds(pl.multiple_of(jnp.where(first, 0, HALF), 8), HALF), :]
    s_near = strip[pl.ds(pl.multiple_of(jnp.where(first, HALF, HALF - 8), 8), 8), :]
    s_edge = jnp.where(inner[:, :128], s_near, jnp.where(got[:, :128], strip[ROWS:ROWS_X, :], 0.0))
    for k in range(CH):
        x[k, 0:HALF, COLS:COLS_X] = margin(k, s_main)
        x[k, HALF:HALF_X, COLS:COLS_X] = margin(k, s_edge)
        j, flip = row_slot(k)
        tile = halo[j]
        if flip:
            tile = pltpu.roll(tile, 4, 0)
        x[k, HALF:HALF_X, 0:COLS] = jnp.where(inner, near[k], jnp.where(got, tile, 0.0))
    two_steps(x, static, y, ub, vb, h2, out)


def control_steps(where, arrays, halos, static):
    return call(
        control_kernel,
        jax.ShapeDtypeStruct((CH, HALF, COLS), F32),
        [SMEM] + [HBM] * 5 + [ANY] * 2 + [VMEM],
        VMEM,
        [pltpu.VMEM((CH, HALF_X, COLS_X), F32)]
        + step_scratch(HALF_X)
        + [pltpu.VMEM((CH, 8, COLS), F32)] * 2
        + [pltpu.VMEM((ROWS_X, 128), F32), pltpu.SemaphoreType.DMA((3,))],
        flops=1 << 27,
        mib=16,
    )(where, *arrays, *halos, static)


def sums_kernel(other, where, own, control, mask, region, earlier, out, *copy):
    start = HALF // 8 * (where[1] ^ 1 if other else where[1])

    def body(t, carry):
        c, g = tile_at(t), tile_at(t + start)
        acc = None
        for k in range(CH):
            d = own[k, g, :] - control[k, c, :]
            acc = d * d if acc is None else acc + d * d
        oc = mask[g, :].astype(F32)
        cell = oc * acc
        reg = region[g, :]
        new = []
        for r in range(REGIONS):
            hit = reg == r
            s = jnp.where(hit, cell, 0.0)
            n = jnp.where(hit, oc, 0.0)
            new.append(carry[2 * r] + (s[:, :128] + s[:, 128:256] + s[:, 256:]))
            new.append(carry[2 * r + 1] + (n[:, :128] + n[:, 128:256] + n[:, 256:]))
        return tuple(new)

    zero = jnp.zeros((8, 128), F32)
    total = lax.fori_loop(0, HALF // 8, body, (zero,) * (2 * REGIONS))
    lane = iota((8, 128), 1)
    row = zero
    for r in range(REGIONS):
        for j in range(2):
            s = jnp.sum(jnp.sum(total[2 * r + j], axis=0, keepdims=True), axis=1, keepdims=True)
            row = jnp.where(lane == REGIONS * j + r, s, row)
    if other:
        row = row + earlier[...]
        copies, sem = copy
        for i in range(out.shape[0]):
            copies[i] = row
        move = pltpu.make_async_copy(copies, out, sem.at[0])
        move.start()
        move.wait()
    else:
        out[...] = row + earlier[...]


def half_sums(other, where, own, control, mask, region, earlier):
    shape = (32, 8, 128) if other else (8, 128)
    return call(
        functools.partial(sums_kernel, other),
        jax.ShapeDtypeStruct(shape, F32),
        [SMEM] + [VMEM] * 5,
        HBM if other else VMEM,
        [pltpu.VMEM(shape, F32), pltpu.SemaphoreType.DMA((1,))] if other else (),
        mib=4,
    )(where, own, control, mask, region, earlier)


BLOCK = 4


def final_kernel(where, own, mine, theirs, region, parts, target, out, growth, cell):
    @pl.when(pl.program_id(0) == 0)
    def _():
        total = parts[0]
        for i in range(1, 32):
            total = total + parts[i]
        lane = iota((8, 128), 1)
        counts = jnp.where(lane < REGIONS, pltpu.roll(total, 128 - REGIONS, 1), 1.0)
        squares = jnp.where(lane < REGIONS, total, 1.0)
        g = jnp.sqrt(squares / (counts * CH) + EPSILON)
        growth[...] = g[0:1, 0:REGIONS]
        factor = target[...] / g

        def body(t, _):
            c = tile_at(t)
            for j in range(3):
                lanes = slice(128 * j, 128 * j + 128)
                reg = region[c, lanes]
                cell[c, lanes] = jnp.take_along_axis(factor, reg, axis=1, mode="promise_in_bounds")
            return 0

        lax.fori_loop(0, ROWS // 8, body, 0)

    start = HALF // 8 * where[1]
    lead = pl.program_id(0) * BLOCK
    for ref, s in ((mine, start), (theirs, HALF // 8 - start)):

        def body(t, _):
            c, g = tile_at(t), tile_at(t + s)
            f = cell[g, :]
            for k in range(BLOCK):
                q = ref[lead + k, c, :]
                out[k, g, :] = q + f * (own[lead + k, g, :] - q)
            return 0

        lax.fori_loop(0, HALF // 8, body, 0)


def rescale(where, own, mine, theirs, region, parts, target):
    target = jnp.broadcast_to(jnp.pad(target, (0, 128 - REGIONS), constant_values=1.0), (8, 128))

    cut = pl.BlockSpec((BLOCK, ROWS, COLS), lambda i: (i, 0, 0))
    row = pl.BlockSpec((1, REGIONS), lambda i: (0, 0))
    return pl.pallas_call(
        final_kernel,
        grid=(CH // BLOCK,),
        out_shape=[jax.ShapeDtypeStruct((CH, ROWS, COLS), F32), jax.ShapeDtypeStruct((1, REGIONS), F32)],
        in_specs=[SMEM] + [VMEM] * 6,
        out_specs=[cut, row],
        scratch_shapes=[pltpu.VMEM((ROWS, COLS), F32)],
        compiler_params=pltpu.CompilerParams(vmem_limit_bytes=8 << 20),
        cost_estimate=pl.CostEstimate(flops=1 << 22, bytes_accessed=10 << 20, transcendentals=0),
    )(where, own, mine, theirs, region, parts, target)


def per_device(member_state, depth, rotation, diff, mask, region, target):
    state = member_state[0]
    statics = (depth, rotation, diff, mask)
    m = lax.axis_index("member")
    where = jnp.stack([lax.axis_index("lat"), m % 2, m]).astype(jnp.int32)
    first = spread_first(where, state)
    halos = exchange(where, state, statics)
    halo = call(control_halo_kernel, jax.ShapeDtypeStruct((CH, 8, COLS), F32), [VMEM] * 3, VMEM)(*halos)
    arrays, control_halos, gate = spread_rest(where, *first, halo)
    own, static = own_steps(where, state, statics, halos, gate)
    came, static = lax.optimization_barrier((control_halos[1], static))
    control_halos = spread_halo_rest(m, control_halos[0], came)
    mine = control_steps(where, arrays, control_halos, static)
    theirs = send(mine, [(i, i ^ 1) for i in range(8)])
    parts = half_sums(False, where, own, mine, mask, region, jnp.zeros((8, 128), F32))
    parts = half_sums(True, where, own, theirs, mask, region, parts)
    parts = lax.all_to_all(parts, ("lon", "lat"), 0, 0)
    bred, growth = rescale(where, own, mine, theirs, region, parts, target)
    return bred[None], growth


def solution(mesh):
    return jax.shard_map(
        per_device,
        mesh=mesh,
        in_specs=(
            P("member", None, "lat", "lon"),
            P("lat", "lon"),
            P("lat", "lon"),
            P(None, "lat", "lon"),
            P("lat", "lon"),
            P("lat", "lon"),
            P(),
        ),
        out_specs=(P("member", None, "lat", "lon"), P("member", None)),
        check_vma=False,
    )
```

```python
import functools
import jax
import jax.numpy as jnp
from jax import lax
from jax.experimental import pallas as pl
from jax.experimental.pallas import tpu as pltpu
from jax.sharding import PartitionSpec as P

LEV = 5
CH = 16
FIELDS = 24
REGIONS = 16
ROWS, COLS = 128, 384
ROWS_X, COLS_X = 136, 512
HALF, HALF_X = 64, 72
HALO = 4
EPSILON = 1e-06
VMEM = pl.BlockSpec(memory_space=pltpu.VMEM)
ANY = pl.BlockSpec(memory_space=pl.ANY)
SMEM = pl.BlockSpec(memory_space=pltpu.SMEM)
HBM = pl.BlockSpec(memory_space=pltpu.HBM)
F32 = jnp.float32


def call(kernel, out, in_specs, out_specs, scratch=(), flops=1 << 22, nbytes=1 << 23, mib=12, aliases=None):
    return pl.pallas_call(
        kernel,
        out_shape=out,
        in_specs=in_specs,
        out_specs=out_specs,
        scratch_shapes=list(scratch),
        input_output_aliases=aliases or {},
        compiler_params=pltpu.CompilerParams(vmem_limit_bytes=mib << 20),
        cost_estimate=pl.CostEstimate(flops=flops, bytes_accessed=nbytes, transcendentals=0),
    )


def iota(shape, dim):
    return lax.broadcasted_iota(jnp.int32, shape, dim)


def row_slot(k):
    return (k % 8, k >= 8) if k < CH else (8 + (k - CH) % 4, k - CH >= 4)


def sources(state, depth, rotation, diff, mask):
    return [(state, slice(0, CH)), (depth, CH), (rotation, CH + 1), (diff, slice(CH + 2, CH + 2 + LEV))]


def fetch(fields, mask, cuts, land, land_cut, sem):
    copies = [pltpu.make_async_copy(mask.at[land_cut], land, sem.at[0])]
    for src, at in fields:
        lead = (slice(None),) if src.shape[:-2] else ()
        for dst, cut in cuts:
            copies.append(pltpu.make_async_copy(src.at[lead + cut], dst.at[at], sem.at[len(copies)]))
    for copy in copies:
        copy.start()
    for copy in copies:
        copy.wait()


def rows_kernel(lat, state, depth, rotation, diff, mask, rows, edge, land, sem):
    upper = lat[0] == 0
    cut = (pl.ds(pl.multiple_of(jnp.where(upper, ROWS - 8, 0), 8), 8), slice(None))
    fetch(sources(state, depth, rotation, diff, mask), mask, [(edge, cut)], land, cut, sem)
    edge[FIELDS - 1] = land[...].astype(F32)
    mine = (iota((8, COLS), 0) >= 4) == upper
    for k in range(FIELDS):
        slot, flip = row_slot(k)
        if not flip:
            pair = k + (8 if k < CH else 4)
            rows[8 * slot : 8 * slot + 8, :] = jnp.where(mine, edge[k], pltpu.roll(edge[pair], 4, 0))


def put(k, a, b, w, e):
    lane = iota(w.shape, 1)
    own = (lane >= HALO * k) & (lane < HALO * k + HALO)
    w = jnp.where(own, pltpu.roll(a, HALO * k, 1) if k else a, w)
    return w, jnp.where(own, pltpu.roll(b, HALO * k + HALO, 1), e)


LEFT, RIGHT = slice(0, 128), slice(COLS - 128, COLS)


def strips_kernel(state, depth, rotation, diff, mask, west, east, lo, hi, land, sem):
    full = slice(None)
    cuts = [(lo, (full, LEFT)), (hi, (full, RIGHT))]
    fetch(sources(state, depth, rotation, diff, mask), mask, cuts, land, (full, full), sem)
    lo[FIELDS - 1] = land[:, LEFT].astype(F32)
    hi[FIELDS - 1] = land[:, RIGHT].astype(F32)
    w = e = jnp.zeros((ROWS, 128), F32)
    for k in range(FIELDS):
        w, e = put(k, lo[k], hi[k], w, e)
    west[...] = w
    east[...] = e


def corners_kernel(lat, rows, west, east, west_out, east_out):
    got = (iota((8, 128), 0) < 4) == (lat[0] == 0)
    w = e = jnp.zeros((8, 128), F32)
    for k in range(FIELDS):
        slot, flip = row_slot(k)
        a, b = rows[8 * slot : 8 * slot + 8, LEFT], rows[8 * slot : 8 * slot + 8, RIGHT]
        if flip:
            a, b = pltpu.roll(a, 4, 0), pltpu.roll(b, 4, 0)
        w, e = put(k, a, b, w, e)
    west_out[0:ROWS, :] = west[...]
    east_out[0:ROWS, :] = east[...]
    west_out[ROWS:ROWS_X, :] = jnp.where(got, w, 0.0)
    east_out[ROWS:ROWS_X, :] = jnp.where(got, e, 0.0)


def exchange(where, state, statics):
    n = lax.axis_size("lon")
    up = [(i, (i + 1) % n) for i in range(n)]
    down = [((i + 1) % n, i) for i in range(n)]

    def shape(*dims):
        return jax.ShapeDtypeStruct(dims, F32)

    rows = call(
        rows_kernel,
        shape(FIELDS * 4, COLS),
        [SMEM] + [HBM] * 5,
        VMEM,
        [pltpu.VMEM((FIELDS, 8, COLS), F32), pltpu.VMEM((8, COLS), jnp.int32), pltpu.SemaphoreType.DMA((5,))],
        mib=62,
    )(where, state, *statics)
    rows = lax.ppermute(rows, "lat", [(0, 1), (1, 0)])
    strip = pltpu.VMEM((FIELDS, ROWS, 128), F32)
    west, east = call(
        strips_kernel,
        [shape(ROWS, 128)] * 2,
        [HBM] * 5,
        [VMEM] * 2,
        [strip, strip, pltpu.VMEM((ROWS, COLS), jnp.int32), pltpu.SemaphoreType.DMA((9,))],
        mib=58,
    )(state, *statics)
    west, east = call(corners_kernel, [shape(ROWS_X, 128)] * 2, [SMEM] + [VMEM] * 3, [VMEM] * 2)(
        where, rows, west, east
    )
    return lax.ppermute(east, "lon", up), lax.ppermute(west, "lon", down), rows


def fill_halo(x, lat, from_west, from_east, rows):
    lane = iota((ROWS_X, 128), 1)
    got = (iota((8, COLS), 0) < 4) == (lat[0] == 0)
    w, e = from_west[...], from_east[...]
    for k in range(FIELDS):
        a = pltpu.roll(e, (128 - HALO * k) % 128, 1) if k else e
        x[k, :, COLS:COLS_X] = jnp.where(lane < 64, a, pltpu.roll(w, (124 - HALO * k) % 128, 1))
        j, flip = row_slot(k)
        tile = rows[8 * j : 8 * j + 8, :]
        if flip:
            tile = pltpu.roll(tile, 4, 0)
        x[k, ROWS:ROWS_X, 0:COLS] = jnp.where(got, tile, 0.0)


def tile_at(t):
    return pl.ds(pl.multiple_of(t * 8, 8), 8)


def step(x, static, ub, vb, h2, store, count, tiles, ready):
    sub = iota((8, COLS_X), 0)

    def around(t):
        return tile_at(jnp.where(t == 0, count - 1, t - 1)), tile_at(t), tile_at(jnp.where(t == count - 1, 0, t + 1))

    def north(cur, nxt):
        return pltpu.roll(jnp.where(sub == 0, nxt, cur), 7, 0)

    def south(cur, prv):
        return pltpu.roll(jnp.where(sub == 7, prv, cur), 1, 0)

    def east(cur):
        return pltpu.roll(cur, COLS_X - 1, 1)

    def west(cur):
        return pltpu.roll(cur, 1, 1)

    def sums(t, _):
        c = tile_at(t)
        u = x[1, c, :]
        v = x[1 + LEV, c, :]
        for l in range(1, LEV):
            u = u + x[1 + l, c, :]
            v = v + x[1 + LEV + l, c, :]
        ub[c, :] = east(u) - west(u)
        vb[c, :] = v
        return 0

    ready(0)
    lax.fori_loop(0, count, sums, 0)

    def surface(t, _):
        p, c, n = around(t)
        v = vb[c, :]
        div = ub[c, :] + (north(v, vb[n, :]) - south(v, vb[p, :]))
        h2[c, :] = static[7, c, :] * (x[0, c, :] - (0.25 / LEV) * static[0, c, :] * div)
        return 0

    ready(1)
    lax.fori_loop(0, count, surface, 0)

    def rest(t, _):
        p, c, n = around(t)
        oc = static[7, c, :]
        rot = static[1, c, :]
        h = h2[c, :]
        store(0, c, h)
        px = 0.25 * (east(h) - west(h))
        py = 0.25 * (north(h, h2[n, :]) - south(h, h2[p, :]))
        for l in range(LEV):
            k = static[2 + l, c, :]

            def near(ch):
                q = x[ch, c, :]
                return q, east(q), west(q), north(q, x[ch, n, :]), south(q, x[ch, p, :])

            q, e, w, a, b = near(1 + 2 * LEV + l)
            cx = e - w
            cy = a - b
            c0 = q + k * ((e + w) + (a + b) - 4.0 * q)
            u, e, w, a, b = near(1 + l)
            lap_u = (e + w) + (a + b) - 4.0 * u
            v, e, w, a, b = near(1 + LEV + l)
            lap_v = (e + w) + (a + b) - 4.0 * v
            u2 = oc * (u + rot * v - px - 0.1 * cx + k * lap_u)
            v2 = oc * (v - rot * u - py - 0.1 * cy + k * lap_v)
            store(1 + l, c, u2)
            store(1 + LEV + l, c, v2)
            store(1 + 2 * LEV + l, c, oc * (c0 - 0.05 * (u2 * cx + v2 * cy)))
        return 0

    ready(2)
    lax.fori_loop(0, tiles, rest, 0)


def two_steps(x, static, y, ub, vb, h2, out, ready=lambda stage: None):
    count = x.shape[1] // 8

    def keep(ch, c, value):
        y[ch, c, :] = value

    def give(ch, c, value):
        out[ch, c, :] = value[:, :COLS]

    step(x, static, ub, vb, h2, keep, count, count, ready)
    step(y, static, ub, vb, h2, give, count, count - 1, lambda stage: None)


def step_scratch(rows):
    return [pltpu.VMEM((CH, rows, COLS_X), F32)] + [pltpu.VMEM((rows, COLS_X), F32)] * 3


def own_kernel(where, state, depth, rotation, diff, mask, fw, fe, rows, gate, out, part, x, land, y, ub, vb, h2, sem):
    main = (slice(0, ROWS), slice(0, COLS))

    def fetch_into(i, src, at):
        copy = pltpu.make_async_copy(src, x.at[(at,) + main], sem.at[i])
        copy.start()
        return copy

    flow, heat = slice(1, 1 + 2 * LEV), slice(1 + 2 * LEV, CH)
    now = [fetch_into(0, state.at[flow], flow)]
    soon = [fetch_into(1, state.at[0], 0), fetch_into(2, depth, CH)]
    soon.append(pltpu.make_async_copy(mask, land, sem.at[3]))
    soon[-1].start()
    late = [
        fetch_into(4, state.at[heat], heat),
        fetch_into(5, rotation, CH + 1),
        fetch_into(6, diff, slice(CH + 2, CH + 2 + LEV)),
    ]
    fill_halo(x, where, fw, fe, rows)

    def ready(stage):
        for copy in (now, soon, late)[stage]:
            copy.wait()
        if stage == 1:
            x[(FIELDS - 1,) + main] = land[...].astype(F32)

    two_steps(x, x.at[CH:FIELDS], y, ub, vb, h2, out, ready)
    first = where[1] == 0
    tiles = HALF // 8
    sub = iota((8, COLS_X), 0)

    def body(t, _):
        c, g = tile_at(t), tile_at(t + jnp.where(first, 0, tiles))
        for j in range(CH, FIELDS):
            part[j - CH, c, :] = x[j, g, :]
        return 0

    lax.fori_loop(0, tiles, body, 0)
    for j in range(CH, FIELDS):
        n = x[j, tile_at(jnp.where(first, tiles, 2 * tiles)), :]
        p = x[j, tile_at(jnp.where(first, 2 * tiles, tiles - 1)), :]
        part[j - CH, HALF:HALF_X, :] = jnp.where(sub < 4, n, p)


def own_steps(where, state, statics, halos, gate):
    return call(
        own_kernel,
        [
            jax.ShapeDtypeStruct((CH, ROWS, COLS), F32),
            jax.ShapeDtypeStruct((FIELDS - CH, HALF_X, COLS_X), F32),
        ],
        [SMEM] + [HBM] * 5 + [VMEM] * 3 + [HBM],
        [VMEM] * 2,
        [pltpu.VMEM((FIELDS, ROWS_X, COLS_X), F32), pltpu.VMEM((ROWS, COLS), jnp.int32)]
        + step_scratch(ROWS_X)
        + [pltpu.SemaphoreType.DMA((7,))],
        flops=1 << 28,
        mib=60,
    )(where, state, *statics, *halos, gate)


def control_halo_kernel(fw, fe, rows, out):
    for k in range(8):
        out[k] = rows[8 * k : 8 * k + 8, :]
    for i in range(18):
        out[8 + i // 3, :, 128 * (i % 3) : 128 * (i % 3) + 128] = jnp.zeros((8, 128), F32)
    lane = iota((8, 128), 1)
    for i in range(17):
        r = slice(8 * i, 8 * i + 8)
        s = jnp.where(lane < 64, fw[r, :], pltpu.roll(fe[r, :], 64, 1))
        out[8 + i // 3, :, 128 * (i % 3) : 128 * (i % 3) + 128] = s
    out[14:16] = jnp.zeros((2, 8, COLS), F32)


def send(value, pairs):
    return lax.ppermute(value, "member", pairs)


CHUNKS = 4


def staged(copies, buffer, sem):
    n = CH // CHUNKS
    both = []
    for i, (src, dst) in enumerate(copies):
        for j in range(CHUNKS):
            ch, s = slice(n * j, n * j + n), CHUNKS * i + j
            one = pltpu.make_async_copy(src.at[ch], buffer.at[i, ch], sem.at[2 * s])
            both.append((one, pltpu.make_async_copy(buffer.at[i, ch], dst.at[ch, 0:HALF_X, :], sem.at[2 * s + 1])))
            one.start()
    for one, two in both:
        one.wait()
        two.start()
    for one, two in both:
        two.wait()


STAGE = [pltpu.VMEM((2, CH, HALF_X, COLS), F32), pltpu.SemaphoreType.DMA((4 * CHUNKS,))]


def cut_kernel(where, state, low, top, buffer, sem):
    @pl.when(where[2] == 0)
    def _():
        staged(
            [(state.at[:, 0:HALF_X, :], top), (state.at[:, ROWS - HALF_X : ROWS, :], low)], buffer, sem
        )


def spread_first(where, state):
    shape = jax.ShapeDtypeStruct((CH, HALF_X, COLS), F32)
    low, top = call(cut_kernel, [shape, shape], [SMEM, HBM], [HBM] * 2, STAGE, mib=62)(where, state)
    return low, top, send(top, [(0, 2)]), send(low, [(0, 7)])


def relay_kernel(where, u, v, p1, m1, gate, u_out, v_out, buffer, sem):
    @pl.when(where[2] == 2)
    def _():
        staged([(p1, u_out)], buffer, sem)

    @pl.when(where[2] == 7)
    def _():
        staged([(m1, v_out)], buffer, sem)


def spread_rest(where, u, v, p1, m1, halo):
    u, v = call(
        relay_kernel, [u, v], [SMEM] + [HBM] * 4 + [ANY], [HBM] * 2, STAGE, mib=58, aliases={1: 0, 2: 1}
    )(where, u, v, p1, m1, halo)
    p2 = send(u, [(0, 3), (2, 4)])
    m2 = send(v, [(0, 6), (7, 5)])
    return (v, u, p2, m2), (halo, send(halo, [(0, 1)]), send(halo, [(0, 3)]), send(halo, [(0, 6)]))


def known_kernel(where, own, one, three, six, gate, out, sem):
    for member, ref in ((0, own), (1, one), (3, three), (6, six)):

        @pl.when(where[2] == member)
        def _(ref=ref):
            copy = pltpu.make_async_copy(ref, out, sem.at[0])
            copy.start()
            copy.wait()


def spread_halo_rest(where, halos, gate):
    known = call(
        known_kernel,
        jax.ShapeDtypeStruct((CH, 8, COLS), F32),
        [SMEM] + [ANY] * 5,
        VMEM,
        [pltpu.SemaphoreType.DMA((1,))],
        mib=8,
    )(where, *halos, gate)
    return known, send(known, [(0, 2), (1, 7), (3, 4), (6, 5)])


HOLDER = ((0, 7), (2,), (3, 4), (5, 6), (1,))
HALO_HOLDER = (0, 0, 1, 0, 1, 1, 0, 1)


def control_kernel(where, *refs):
    arrays, halos, (static, out, x, y, ub, vb, h2, near, halo, strip, sem) = refs[:5], refs[5:7], refs[7:]
    first = where[1] == 0
    m = where[2]
    for array, members in zip(arrays, HOLDER):
        for member in members:
            r0, r1 = (0, HALF) if member % 2 == 0 else (8, 0)

            @pl.when(m == member)
            def _(array=array, r0=r0, r1=r1, source=halos[HALO_HOLDER[member]]):
                one = pltpu.make_async_copy(array.at[:, r0 : r0 + HALF, :], x.at[:, 0:HALF, 0:COLS], sem.at[0])
                two = pltpu.make_async_copy(array.at[:, r1 : r1 + 8, :], near, sem.at[1])
                three = pltpu.make_async_copy(source, halo, sem.at[2])
                one.start()
                two.start()
                three.start()
                one.wait()
                two.wait()
                three.wait()

    for i in range(17):
        strip[8 * i : 8 * i + 8, :] = halo[8 + i // 3, :, 128 * (i % 3) : 128 * (i % 3) + 128]

    def margin(k, s):
        lane = iota(s.shape, 1)
        return jnp.where(
            lane < 64, pltpu.roll(s, 64 - HALO * k, 1), pltpu.roll(s, 124 - HALO * k, 1)
        )

    sub = iota((8, COLS), 0)
    inner = (sub < 4) == first
    got = (sub < 4) == (where[0] == 0)
    s_main = strip[pl.ds(pl.multiple_of(jnp.where(first, 0, HALF), 8), HALF), :]
    s_near = strip[pl.ds(pl.multiple_of(jnp.where(first, HALF, HALF - 8), 8), 8), :]
    s_edge = jnp.where(inner[:, :128], s_near, jnp.where(got[:, :128], strip[ROWS:ROWS_X, :], 0.0))
    for k in range(CH):
        x[k, 0:HALF, COLS:COLS_X] = margin(k, s_main)
        x[k, HALF:HALF_X, COLS:COLS_X] = margin(k, s_edge)
        j, flip = row_slot(k)
        tile = halo[j]
        if flip:
            tile = pltpu.roll(tile, 4, 0)
        x[k, HALF:HALF_X, 0:COLS] = jnp.where(inner, near[k], jnp.where(got, tile, 0.0))
    two_steps(x, static, y, ub, vb, h2, out)


def control_steps(where, arrays, halos, static):
    return call(
        control_kernel,
        jax.ShapeDtypeStruct((CH, HALF, COLS), F32),
        [SMEM] + [HBM] * 5 + [ANY] * 2 + [VMEM],
        VMEM,
        [pltpu.VMEM((CH, HALF_X, COLS_X), F32)]
        + step_scratch(HALF_X)
        + [pltpu.VMEM((CH, 8, COLS), F32)] * 2
        + [pltpu.VMEM((ROWS_X, 128), F32), pltpu.SemaphoreType.DMA((3,))],
        flops=1 << 27,
        mib=16,
    )(where, *arrays, *halos, static)


def sums_kernel(other, where, own, control, mask, region, earlier, out, *copy):
    start = HALF // 8 * (where[1] ^ 1 if other else where[1])

    def body(t, carry):
        c, g = tile_at(t), tile_at(t + start)
        acc = None
        for k in range(CH):
            d = own[k, g, :] - control[k, c, :]
            acc = d * d if acc is None else acc + d * d
        oc = mask[g, :].astype(F32)
        cell = oc * acc
        reg = region[g, :]
        new = []
        for r in range(REGIONS):
            hit = reg == r
            s = jnp.where(hit, cell, 0.0)
            n = jnp.where(hit, oc, 0.0)
            new.append(carry[2 * r] + (s[:, :128] + s[:, 128:256] + s[:, 256:]))
            new.append(carry[2 * r + 1] + (n[:, :128] + n[:, 128:256] + n[:, 256:]))
        return tuple(new)

    zero = jnp.zeros((8, 128), F32)
    total = lax.fori_loop(0, HALF // 8, body, (zero,) * (2 * REGIONS))
    lane = iota((8, 128), 1)
    row = zero
    for r in range(REGIONS):
        for j in range(2):
            s = jnp.sum(jnp.sum(total[2 * r + j], axis=0, keepdims=True), axis=1, keepdims=True)
            row = jnp.where(lane == REGIONS * j + r, s, row)
    if other:
        row = row + earlier[...]
        copies, sem = copy
        for i in range(out.shape[0]):
            copies[i] = row
        move = pltpu.make_async_copy(copies, out, sem.at[0])
        move.start()
        move.wait()
    else:
        out[...] = row + earlier[...]


def half_sums(other, where, own, control, mask, region, earlier):
    shape = (32, 8, 128) if other else (8, 128)
    return call(
        functools.partial(sums_kernel, other),
        jax.ShapeDtypeStruct(shape, F32),
        [SMEM] + [VMEM] * 5,
        HBM if other else VMEM,
        [pltpu.VMEM(shape, F32), pltpu.SemaphoreType.DMA((1,))] if other else (),
        mib=4,
    )(where, own, control, mask, region, earlier)


BLOCK = 4


def final_kernel(where, own, mine, theirs, region, parts, target, out, growth, cell):
    @pl.when(pl.program_id(0) == 0)
    def _():
        total = parts[0]
        for i in range(1, 32):
            total = total + parts[i]
        lane = iota((8, 128), 1)
        counts = jnp.where(lane < REGIONS, pltpu.roll(total, 128 - REGIONS, 1), 1.0)
        squares = jnp.where(lane < REGIONS, total, 1.0)
        g = jnp.sqrt(squares / (counts * CH) + EPSILON)
        growth[...] = g[0:1, 0:REGIONS]
        factor = target[...] / g

        def body(t, _):
            c = tile_at(t)
            for j in range(3):
                lanes = slice(128 * j, 128 * j + 128)
                reg = region[c, lanes]
                cell[c, lanes] = jnp.take_along_axis(factor, reg, axis=1, mode="promise_in_bounds")
            return 0

        lax.fori_loop(0, ROWS // 8, body, 0)

    start = HALF // 8 * where[1]
    lead = pl.program_id(0) * BLOCK
    for ref, s in ((mine, start), (theirs, HALF // 8 - start)):

        def body(t, _):
            c, g = tile_at(t), tile_at(t + s)
            f = cell[g, :]
            for k in range(BLOCK):
                q = ref[lead + k, c, :]
                out[k, g, :] = q + f * (own[lead + k, g, :] - q)
            return 0

        lax.fori_loop(0, HALF // 8, body, 0)


def rescale(where, own, mine, theirs, region, parts, target):
    target = jnp.broadcast_to(jnp.pad(target, (0, 128 - REGIONS), constant_values=1.0), (8, 128))

    cut = pl.BlockSpec((BLOCK, ROWS, COLS), lambda i: (i, 0, 0))
    row = pl.BlockSpec((1, REGIONS), lambda i: (0, 0))
    return pl.pallas_call(
        final_kernel,
        grid=(CH // BLOCK,),
        out_shape=[jax.ShapeDtypeStruct((CH, ROWS, COLS), F32), jax.ShapeDtypeStruct((1, REGIONS), F32)],
        in_specs=[SMEM] + [VMEM] * 6,
        out_specs=[cut, row],
        scratch_shapes=[pltpu.VMEM((ROWS, COLS), F32)],
        compiler_params=pltpu.CompilerParams(vmem_limit_bytes=8 << 20),
        cost_estimate=pl.CostEstimate(flops=1 << 22, bytes_accessed=10 << 20, transcendentals=0),
    )(where, own, mine, theirs, region, parts, target)


def per_device(member_state, depth, rotation, diff, mask, region, target):
    state = member_state[0]
    statics = (depth, rotation, diff, mask)
    m = lax.axis_index("member")
    where = jnp.stack([lax.axis_index("lat"), m % 2, m]).astype(jnp.int32)
    first = spread_first(where, state)
    halos = exchange(where, state, statics)
    halo = call(control_halo_kernel, jax.ShapeDtypeStruct((CH, 8, COLS), F32), [VMEM] * 3, VMEM)(*halos)
    arrays, control_halos = spread_rest(where, *first, halo)
    own, static = own_steps(where, state, statics, halos, arrays[1])
    control_halos = spread_halo_rest(where, control_halos, static)
    late, static = lax.optimization_barrier((arrays[1], static))
    arrays += (send(late, [(0, 1)]),)
    mine = control_steps(where, arrays, control_halos, static)
    theirs = send(mine, [(i, i ^ 1) for i in range(8)])
    parts = half_sums(False, where, own, mine, mask, region, jnp.zeros((8, 128), F32))
    parts = half_sums(True, where, own, theirs, mask, region, parts)
    parts = lax.all_to_all(parts, ("lon", "lat"), 0, 0)
    bred, growth = rescale(where, own, mine, theirs, region, parts, target)
    return bred[None], growth


def solution(mesh):
    return jax.shard_map(
        per_device,
        mesh=mesh,
        in_specs=(
            P("member", None, "lat", "lon"),
            P("lat", "lon"),
            P("lat", "lon"),
            P(None, "lat", "lon"),
            P("lat", "lon"),
            P("lat", "lon"),
            P(),
        ),
        out_specs=(P("member", None, "lat", "lon"), P("member", None)),
        check_vma=False,
    )
```

```python
import functools
import jax
import jax.numpy as jnp
from jax import lax
from jax.experimental import pallas as pl
from jax.experimental.pallas import tpu as pltpu
from jax.sharding import PartitionSpec as P

LEV = 5
CH = 16
FIELDS = 24
REGIONS = 16
ROWS, COLS = 128, 384
ROWS_X, COLS_X = 136, 512
HALF, HALF_X = 64, 72
HALO = 4
EPSILON = 1e-06
VMEM = pl.BlockSpec(memory_space=pltpu.VMEM)
ANY = pl.BlockSpec(memory_space=pl.ANY)
SMEM = pl.BlockSpec(memory_space=pltpu.SMEM)
HBM = pl.BlockSpec(memory_space=pltpu.HBM)
F32 = jnp.float32


def call(kernel, out, in_specs, out_specs, scratch=(), flops=1 << 22, nbytes=1 << 23, mib=12, aliases=None):
    return pl.pallas_call(
        kernel,
        out_shape=out,
        in_specs=in_specs,
        out_specs=out_specs,
        scratch_shapes=list(scratch),
        input_output_aliases=aliases or {},
        compiler_params=pltpu.CompilerParams(vmem_limit_bytes=mib << 20),
        cost_estimate=pl.CostEstimate(flops=flops, bytes_accessed=nbytes, transcendentals=0),
    )


def iota(shape, dim):
    return lax.broadcasted_iota(jnp.int32, shape, dim)


def row_slot(k):
    return (k % 8, k >= 8) if k < CH else (8 + (k - CH) % 4, k - CH >= 4)


def sources(state, depth, rotation, diff, mask):
    return [(state, slice(0, CH)), (depth, CH), (rotation, CH + 1), (diff, slice(CH + 2, CH + 2 + LEV))]


def fetch(fields, mask, cuts, land, land_cut, sem):
    copies = [pltpu.make_async_copy(mask.at[land_cut], land, sem.at[0])]
    for src, at in fields:
        lead = (slice(None),) if src.shape[:-2] else ()
        for dst, cut in cuts:
            copies.append(pltpu.make_async_copy(src.at[lead + cut], dst.at[at], sem.at[len(copies)]))
    for copy in copies:
        copy.start()
    for copy in copies:
        copy.wait()


def rows_kernel(lat, state, depth, rotation, diff, mask, rows, edge, land, sem):
    upper = lat[0] == 0
    cut = (pl.ds(pl.multiple_of(jnp.where(upper, ROWS - 8, 0), 8), 8), slice(None))
    fetch(sources(state, depth, rotation, diff, mask), mask, [(edge, cut)], land, cut, sem)
    edge[FIELDS - 1] = land[...].astype(F32)
    mine = (iota((8, COLS), 0) >= 4) == upper
    for k in range(FIELDS):
        slot, flip = row_slot(k)
        if not flip:
            pair = k + (8 if k < CH else 4)
            rows[8 * slot : 8 * slot + 8, :] = jnp.where(mine, edge[k], pltpu.roll(edge[pair], 4, 0))


def put(k, a, b, w, e):
    lane = iota(w.shape, 1)
    own = (lane >= HALO * k) & (lane < HALO * k + HALO)
    w = jnp.where(own, pltpu.roll(a, HALO * k, 1) if k else a, w)
    return w, jnp.where(own, pltpu.roll(b, HALO * k + HALO, 1), e)


LEFT, RIGHT = slice(0, 128), slice(COLS - 128, COLS)


def strips_kernel(state, depth, rotation, diff, mask, west, east, lo, hi, land, sem):
    full = slice(None)
    cuts = [(lo, (full, LEFT)), (hi, (full, RIGHT))]
    fetch(sources(state, depth, rotation, diff, mask), mask, cuts, land, (full, full), sem)
    lo[FIELDS - 1] = land[:, LEFT].astype(F32)
    hi[FIELDS - 1] = land[:, RIGHT].astype(F32)
    w = e = jnp.zeros((ROWS, 128), F32)
    for k in range(FIELDS):
        w, e = put(k, lo[k], hi[k], w, e)
    west[...] = w
    east[...] = e


def corners_kernel(lat, rows, west, east, west_out, east_out):
    got = (iota((8, 128), 0) < 4) == (lat[0] == 0)
    w = e = jnp.zeros((8, 128), F32)
    for k in range(FIELDS):
        slot, flip = row_slot(k)
        a, b = rows[8 * slot : 8 * slot + 8, LEFT], rows[8 * slot : 8 * slot + 8, RIGHT]
        if flip:
            a, b = pltpu.roll(a, 4, 0), pltpu.roll(b, 4, 0)
        w, e = put(k, a, b, w, e)
    west_out[0:ROWS, :] = west[...]
    east_out[0:ROWS, :] = east[...]
    west_out[ROWS:ROWS_X, :] = jnp.where(got, w, 0.0)
    east_out[ROWS:ROWS_X, :] = jnp.where(got, e, 0.0)


def exchange(where, state, statics):
    n = lax.axis_size("lon")
    up = [(i, (i + 1) % n) for i in range(n)]
    down = [((i + 1) % n, i) for i in range(n)]

    def shape(*dims):
        return jax.ShapeDtypeStruct(dims, F32)

    rows = call(
        rows_kernel,
        shape(FIELDS * 4, COLS),
        [SMEM] + [HBM] * 5,
        VMEM,
        [pltpu.VMEM((FIELDS, 8, COLS), F32), pltpu.VMEM((8, COLS), jnp.int32), pltpu.SemaphoreType.DMA((5,))],
        mib=62,
    )(where, state, *statics)
    rows = lax.ppermute(rows, "lat", [(0, 1), (1, 0)])
    strip = pltpu.VMEM((FIELDS, ROWS, 128), F32)
    west, east = call(
        strips_kernel,
        [shape(ROWS, 128)] * 2,
        [HBM] * 5,
        [VMEM] * 2,
        [strip, strip, pltpu.VMEM((ROWS, COLS), jnp.int32), pltpu.SemaphoreType.DMA((9,))],
        mib=58,
    )(state, *statics)
    west, east = call(corners_kernel, [shape(ROWS_X, 128)] * 2, [SMEM] + [VMEM] * 3, [VMEM] * 2)(
        where, rows, west, east
    )
    return lax.ppermute(east, "lon", up), lax.ppermute(west, "lon", down), rows


def fill_halo(x, lat, from_west, from_east, rows):
    lane = iota((ROWS_X, 128), 1)
    got = (iota((8, COLS), 0) < 4) == (lat[0] == 0)
    w, e = from_west[...], from_east[...]
    for k in range(FIELDS):
        a = pltpu.roll(e, (128 - HALO * k) % 128, 1) if k else e
        x[k, :, COLS:COLS_X] = jnp.where(lane < 64, a, pltpu.roll(w, (124 - HALO * k) % 128, 1))
        j, flip = row_slot(k)
        tile = rows[8 * j : 8 * j + 8, :]
        if flip:
            tile = pltpu.roll(tile, 4, 0)
        x[k, ROWS:ROWS_X, 0:COLS] = jnp.where(got, tile, 0.0)


def tile_at(t):
    return pl.ds(pl.multiple_of(t * 8, 8), 8)


def step(x, static, ub, vb, h2, store, count, tiles, ready):
    sub = iota((8, COLS_X), 0)

    def around(t):
        return tile_at(jnp.where(t == 0, count - 1, t - 1)), tile_at(t), tile_at(jnp.where(t == count - 1, 0, t + 1))

    def north(cur, nxt):
        return pltpu.roll(jnp.where(sub == 0, nxt, cur), 7, 0)

    def south(cur, prv):
        return pltpu.roll(jnp.where(sub == 7, prv, cur), 1, 0)

    def east(cur):
        return pltpu.roll(cur, COLS_X - 1, 1)

    def west(cur):
        return pltpu.roll(cur, 1, 1)

    def sums(t, _):
        c = tile_at(t)
        u = x[1, c, :]
        v = x[1 + LEV, c, :]
        for l in range(1, LEV):
            u = u + x[1 + l, c, :]
            v = v + x[1 + LEV + l, c, :]
        ub[c, :] = east(u) - west(u)
        vb[c, :] = v
        return 0

    ready(0)
    lax.fori_loop(0, count, sums, 0)

    def surface(t, _):
        p, c, n = around(t)
        v = vb[c, :]
        div = ub[c, :] + (north(v, vb[n, :]) - south(v, vb[p, :]))
        h2[c, :] = static[7, c, :] * (x[0, c, :] - (0.25 / LEV) * static[0, c, :] * div)
        return 0

    ready(1)
    lax.fori_loop(0, count, surface, 0)

    def rest(t, _):
        p, c, n = around(t)
        oc = static[7, c, :]
        rot = static[1, c, :]
        h = h2[c, :]
        store(0, c, h)
        px = 0.25 * (east(h) - west(h))
        py = 0.25 * (north(h, h2[n, :]) - south(h, h2[p, :]))
        for l in range(LEV):
            k = static[2 + l, c, :]

            def near(ch):
                q = x[ch, c, :]
                return q, east(q), west(q), north(q, x[ch, n, :]), south(q, x[ch, p, :])

            q, e, w, a, b = near(1 + 2 * LEV + l)
            cx = e - w
            cy = a - b
            c0 = q + k * ((e + w) + (a + b) - 4.0 * q)
            u, e, w, a, b = near(1 + l)
            lap_u = (e + w) + (a + b) - 4.0 * u
            v, e, w, a, b = near(1 + LEV + l)
            lap_v = (e + w) + (a + b) - 4.0 * v
            u2 = oc * (u + rot * v - px - 0.1 * cx + k * lap_u)
            v2 = oc * (v - rot * u - py - 0.1 * cy + k * lap_v)
            store(1 + l, c, u2)
            store(1 + LEV + l, c, v2)
            store(1 + 2 * LEV + l, c, oc * (c0 - 0.05 * (u2 * cx + v2 * cy)))
        return 0

    ready(2)
    lax.fori_loop(0, tiles, rest, 0)


def two_steps(x, static, y, ub, vb, h2, out, ready=lambda stage: None):
    count = x.shape[1] // 8

    def keep(ch, c, value):
        y[ch, c, :] = value

    def give(ch, c, value):
        out[ch, c, :] = value[:, :COLS]

    step(x, static, ub, vb, h2, keep, count, count, ready)
    step(y, static, ub, vb, h2, give, count, count - 1, lambda stage: None)


def step_scratch(rows):
    return [pltpu.VMEM((CH, rows, COLS_X), F32)] + [pltpu.VMEM((rows, COLS_X), F32)] * 3


def own_kernel(where, state, depth, rotation, diff, mask, fw, fe, rows, gate, out, part, x, land, y, ub, vb, h2, sem):
    main = (slice(0, ROWS), slice(0, COLS))

    def fetch_into(i, src, at):
        copy = pltpu.make_async_copy(src, x.at[(at,) + main], sem.at[i])
        copy.start()
        return copy

    flow, heat = slice(1, 1 + 2 * LEV), slice(1 + 2 * LEV, CH)
    now = [fetch_into(0, state.at[flow], flow)]
    soon = [fetch_into(1, state.at[0], 0), fetch_into(2, depth, CH)]
    soon.append(pltpu.make_async_copy(mask, land, sem.at[3]))
    soon[-1].start()
    late = [
        fetch_into(4, state.at[heat], heat),
        fetch_into(5, rotation, CH + 1),
        fetch_into(6, diff, slice(CH + 2, CH + 2 + LEV)),
    ]
    fill_halo(x, where, fw, fe, rows)

    def ready(stage):
        for copy in (now, soon, late)[stage]:
            copy.wait()
        if stage == 1:
            x[(FIELDS - 1,) + main] = land[...].astype(F32)

    two_steps(x, x.at[CH:FIELDS], y, ub, vb, h2, out, ready)
    first = where[1] == 0
    tiles = HALF // 8
    sub = iota((8, COLS_X), 0)

    def body(t, _):
        c, g = tile_at(t), tile_at(t + jnp.where(first, 0, tiles))
        for j in range(CH, FIELDS):
            part[j - CH, c, :] = x[j, g, :]
        return 0

    lax.fori_loop(0, tiles, body, 0)
    for j in range(CH, FIELDS):
        n = x[j, tile_at(jnp.where(first, tiles, 2 * tiles)), :]
        p = x[j, tile_at(jnp.where(first, 2 * tiles, tiles - 1)), :]
        part[j - CH, HALF:HALF_X, :] = jnp.where(sub < 4, n, p)


def own_steps(where, state, statics, halos, gate):
    return call(
        own_kernel,
        [
            jax.ShapeDtypeStruct((CH, ROWS, COLS), F32),
            jax.ShapeDtypeStruct((FIELDS - CH, HALF_X, COLS_X), F32),
        ],
        [SMEM] + [HBM] * 5 + [VMEM] * 3 + [HBM],
        [VMEM] * 2,
        [pltpu.VMEM((FIELDS, ROWS_X, COLS_X), F32), pltpu.VMEM((ROWS, COLS), jnp.int32)]
        + step_scratch(ROWS_X)
        + [pltpu.SemaphoreType.DMA((7,))],
        flops=1 << 28,
        mib=60,
    )(where, state, *statics, *halos, gate)


def control_halo_kernel(fw, fe, rows, out):
    for k in range(8):
        out[k] = rows[8 * k : 8 * k + 8, :]
    for i in range(18):
        out[8 + i // 3, :, 128 * (i % 3) : 128 * (i % 3) + 128] = jnp.zeros((8, 128), F32)
    lane = iota((8, 128), 1)
    for i in range(17):
        r = slice(8 * i, 8 * i + 8)
        s = jnp.where(lane < 64, fw[r, :], pltpu.roll(fe[r, :], 64, 1))
        out[8 + i // 3, :, 128 * (i % 3) : 128 * (i % 3) + 128] = s
    out[14:16] = jnp.zeros((2, 8, COLS), F32)


def send(value, pairs):
    return lax.ppermute(value, "member", pairs)


CHUNKS = 4


def staged(copies, buffer, sem):
    n = CH // CHUNKS
    both = []
    for i, (src, dst) in enumerate(copies):
        for j in range(CHUNKS):
            ch, s = slice(n * j, n * j + n), CHUNKS * i + j
            one = pltpu.make_async_copy(src.at[ch], buffer.at[i, ch], sem.at[2 * s])
            both.append((one, pltpu.make_async_copy(buffer.at[i, ch], dst.at[ch, 0:HALF_X, :], sem.at[2 * s + 1])))
            one.start()
    for one, two in both:
        one.wait()
        two.start()
    for one, two in both:
        two.wait()


STAGE = [pltpu.VMEM((2, CH, HALF_X, COLS), F32), pltpu.SemaphoreType.DMA((4 * CHUNKS,))]


def cut_kernel(where, state, low, top, buffer, sem):
    @pl.when(where[2] == 0)
    def _():
        staged(
            [(state.at[:, 0:HALF_X, :], top), (state.at[:, ROWS - HALF_X : ROWS, :], low)], buffer, sem
        )


def spread_first(where, state):
    shape = jax.ShapeDtypeStruct((CH, HALF_X, COLS), F32)
    low, top = call(cut_kernel, [shape, shape], [SMEM, HBM], [HBM] * 2, STAGE, mib=62)(where, state)
    return low, top, send(top, [(0, 2)]), send(low, [(0, 7)])


def relay_kernel(where, u, v, p1, m1, gate, u_out, v_out, buffer, sem):
    @pl.when(where[2] == 2)
    def _():
        staged([(p1, u_out)], buffer, sem)

    @pl.when(where[2] == 7)
    def _():
        staged([(m1, v_out), (m1, u_out)], buffer, sem)


def known_kernel(where, own, one, three, six, out, sem):
    for member, ref in ((0, own), (1, one), (3, three), (6, six)):

        @pl.when(where[2] == member)
        def _(ref=ref):
            copy = pltpu.make_async_copy(ref, out, sem.at[0])
            copy.start()
            copy.wait()


def spread_rest(where, u, v, p1, m1, halo):
    came = [send(halo, [(0, member)]) for member in (1, 3, 6)]
    known = call(
        known_kernel,
        jax.ShapeDtypeStruct((CH, 8, COLS), F32),
        [SMEM] + [ANY] * 4,
        VMEM,
        [pltpu.SemaphoreType.DMA((1,))],
        mib=8,
    )(where, halo, *came)
    u, v = call(
        relay_kernel, [u, v], [SMEM] + [HBM] * 4 + [ANY], [HBM] * 2, STAGE, mib=58, aliases={1: 0, 2: 1}
    )(where, u, v, p1, m1, known)
    p2 = send(u, [(0, 3), (2, 4), (7, 1)])
    m2 = send(v, [(0, 6), (7, 5)])
    return (v, u, p2, m2), (known, send(known, [(0, 2), (1, 7), (3, 4), (6, 5)]))


HOLDER = ((0, 7), (2,), (1, 3, 4), (5, 6))
HALO_HOLDER = (0, 0, 1, 0, 1, 1, 0, 1)


def control_kernel(where, *refs):
    arrays, halos, (static, out, x, y, ub, vb, h2, near, halo, strip, sem) = refs[:4], refs[4:6], refs[6:]
    first = where[1] == 0
    m = where[2]
    for array, members in zip(arrays, HOLDER):
        for member in members:
            r0, r1 = (0, HALF) if member % 2 == 0 else (8, 0)

            @pl.when(m == member)
            def _(array=array, r0=r0, r1=r1, source=halos[HALO_HOLDER[member]]):
                one = pltpu.make_async_copy(array.at[:, r0 : r0 + HALF, :], x.at[:, 0:HALF, 0:COLS], sem.at[0])
                two = pltpu.make_async_copy(array.at[:, r1 : r1 + 8, :], near, sem.at[1])
                three = pltpu.make_async_copy(source, halo, sem.at[2])
                one.start()
                two.start()
                three.start()
                one.wait()
                two.wait()
                three.wait()

    for i in range(17):
        strip[8 * i : 8 * i + 8, :] = halo[8 + i // 3, :, 128 * (i % 3) : 128 * (i % 3) + 128]

    def margin(k, s):
        lane = iota(s.shape, 1)
        return jnp.where(
            lane < 64, pltpu.roll(s, 64 - HALO * k, 1), pltpu.roll(s, 124 - HALO * k, 1)
        )

    sub = iota((8, COLS), 0)
    inner = (sub < 4) == first
    got = (sub < 4) == (where[0] == 0)
    s_main = strip[pl.ds(pl.multiple_of(jnp.where(first, 0, HALF), 8), HALF), :]
    s_near = strip[pl.ds(pl.multiple_of(jnp.where(first, HALF, HALF - 8), 8), 8), :]
    s_edge = jnp.where(inner[:, :128], s_near, jnp.where(got[:, :128], strip[ROWS:ROWS_X, :], 0.0))
    for k in range(CH):
        x[k, 0:HALF, COLS:COLS_X] = margin(k, s_main)
        x[k, HALF:HALF_X, COLS:COLS_X] = margin(k, s_edge)
        j, flip = row_slot(k)
        tile = halo[j]
        if flip:
            tile = pltpu.roll(tile, 4, 0)
        x[k, HALF:HALF_X, 0:COLS] = jnp.where(inner, near[k], jnp.where(got, tile, 0.0))
    two_steps(x, static, y, ub, vb, h2, out)


def control_steps(where, arrays, halos, static):
    return call(
        control_kernel,
        jax.ShapeDtypeStruct((CH, HALF, COLS), F32),
        [SMEM] + [HBM] * 4 + [ANY] * 2 + [VMEM],
        VMEM,
        [pltpu.VMEM((CH, HALF_X, COLS_X), F32)]
        + step_scratch(HALF_X)
        + [pltpu.VMEM((CH, 8, COLS), F32)] * 2
        + [pltpu.VMEM((ROWS_X, 128), F32), pltpu.SemaphoreType.DMA((3,))],
        flops=1 << 27,
        mib=16,
    )(where, *arrays, *halos, static)


def sums_kernel(other, where, own, control, mask, region, earlier, out, *copy):
    start = HALF // 8 * (where[1] ^ 1 if other else where[1])

    def body(t, carry):
        c, g = tile_at(t), tile_at(t + start)
        acc = None
        for k in range(CH):
            d = own[k, g, :] - control[k, c, :]
            acc = d * d if acc is None else acc + d * d
        oc = mask[g, :].astype(F32)
        cell = oc * acc
        reg = region[g, :]
        new = []
        for r in range(REGIONS):
            hit = reg == r
            s = jnp.where(hit, cell, 0.0)
            n = jnp.where(hit, oc, 0.0)
            new.append(carry[2 * r] + (s[:, :128] + s[:, 128:256] + s[:, 256:]))
            new.append(carry[2 * r + 1] + (n[:, :128] + n[:, 128:256] + n[:, 256:]))
        return tuple(new)

    zero = jnp.zeros((8, 128), F32)
    total = lax.fori_loop(0, HALF // 8, body, (zero,) * (2 * REGIONS))
    lane = iota((8, 128), 1)
    row = zero
    for r in range(REGIONS):
        for j in range(2):
            s = jnp.sum(jnp.sum(total[2 * r + j], axis=0, keepdims=True), axis=1, keepdims=True)
            row = jnp.where(lane == REGIONS * j + r, s, row)
    if other:
        row = row + earlier[...]
        copies, sem = copy
        for i in range(out.shape[0]):
            copies[i] = row
        move = pltpu.make_async_copy(copies, out, sem.at[0])
        move.start()
        move.wait()
    else:
        out[...] = row + earlier[...]


def half_sums(other, where, own, control, mask, region, earlier):
    shape = (32, 8, 128) if other else (8, 128)
    return call(
        functools.partial(sums_kernel, other),
        jax.ShapeDtypeStruct(shape, F32),
        [SMEM] + [VMEM] * 5,
        HBM if other else VMEM,
        [pltpu.VMEM(shape, F32), pltpu.SemaphoreType.DMA((1,))] if other else (),
        mib=4,
    )(where, own, control, mask, region, earlier)


BLOCK = 4


def final_kernel(where, own, mine, theirs, region, parts, target, out, growth, cell):
    @pl.when(pl.program_id(0) == 0)
    def _():
        total = parts[0]
        for i in range(1, 32):
            total = total + parts[i]
        lane = iota((8, 128), 1)
        counts = jnp.where(lane < REGIONS, pltpu.roll(total, 128 - REGIONS, 1), 1.0)
        squares = jnp.where(lane < REGIONS, total, 1.0)
        g = jnp.sqrt(squares / (counts * CH) + EPSILON)
        growth[...] = g[0:1, 0:REGIONS]
        factor = target[...] / g

        def body(t, _):
            c = tile_at(t)
            for j in range(3):
                lanes = slice(128 * j, 128 * j + 128)
                reg = region[c, lanes]
                cell[c, lanes] = jnp.take_along_axis(factor, reg, axis=1, mode="promise_in_bounds")
            return 0

        lax.fori_loop(0, ROWS // 8, body, 0)

    start = HALF // 8 * where[1]
    lead = pl.program_id(0) * BLOCK
    for ref, s in ((mine, start), (theirs, HALF // 8 - start)):

        def body(t, _):
            c, g = tile_at(t), tile_at(t + s)
            f = cell[g, :]
            for k in range(BLOCK):
                q = ref[lead + k, c, :]
                out[k, g, :] = q + f * (own[lead + k, g, :] - q)
            return 0

        lax.fori_loop(0, HALF // 8, body, 0)


def rescale(where, own, mine, theirs, region, parts, target):
    target = jnp.broadcast_to(jnp.pad(target, (0, 128 - REGIONS), constant_values=1.0), (8, 128))

    cut = pl.BlockSpec((BLOCK, ROWS, COLS), lambda i: (i, 0, 0))
    row = pl.BlockSpec((1, REGIONS), lambda i: (0, 0))
    return pl.pallas_call(
        final_kernel,
        grid=(CH // BLOCK,),
        out_shape=[jax.ShapeDtypeStruct((CH, ROWS, COLS), F32), jax.ShapeDtypeStruct((1, REGIONS), F32)],
        in_specs=[SMEM] + [VMEM] * 6,
        out_specs=[cut, row],
        scratch_shapes=[pltpu.VMEM((ROWS, COLS), F32)],
        compiler_params=pltpu.CompilerParams(vmem_limit_bytes=8 << 20),
        cost_estimate=pl.CostEstimate(flops=1 << 22, bytes_accessed=10 << 20, transcendentals=0),
    )(where, own, mine, theirs, region, parts, target)


def per_device(member_state, depth, rotation, diff, mask, region, target):
    state = member_state[0]
    statics = (depth, rotation, diff, mask)
    m = lax.axis_index("member")
    where = jnp.stack([lax.axis_index("lat"), m % 2, m]).astype(jnp.int32)
    first = spread_first(where, state)
    halos = exchange(where, state, statics)
    halo = call(control_halo_kernel, jax.ShapeDtypeStruct((CH, 8, COLS), F32), [VMEM] * 3, VMEM)(*halos)
    arrays, control_halos = spread_rest(where, *first, halo)
    own, static = own_steps(where, state, statics, halos, arrays[1])
    mine = control_steps(where, arrays, control_halos, static)
    theirs = send(mine, [(i, i ^ 1) for i in range(8)])
    parts = half_sums(False, where, own, mine, mask, region, jnp.zeros((8, 128), F32))
    parts = half_sums(True, where, own, theirs, mask, region, parts)
    parts = lax.all_to_all(parts, ("lon", "lat"), 0, 0)
    bred, growth = rescale(where, own, mine, theirs, region, parts, target)
    return bred[None], growth


def solution(mesh):
    return jax.shard_map(
        per_device,
        mesh=mesh,
        in_specs=(
            P("member", None, "lat", "lon"),
            P("lat", "lon"),
            P("lat", "lon"),
            P(None, "lat", "lon"),
            P("lat", "lon"),
            P("lat", "lon"),
            P(),
        ),
        out_specs=(P("member", None, "lat", "lon"), P("member", None)),
        check_vma=False,
    )
```

```python
import functools
import jax
import jax.numpy as jnp
from jax import lax
from jax.experimental import pallas as pl
from jax.experimental.pallas import tpu as pltpu
from jax.sharding import PartitionSpec as P

LEV = 5
CH = 16
FIELDS = 24
REGIONS = 16
ROWS, COLS = 128, 384
ROWS_X, COLS_X = 136, 512
HALF, HALF_X = 64, 72
HALO = 4
EPSILON = 1e-06
VMEM = pl.BlockSpec(memory_space=pltpu.VMEM)
ANY = pl.BlockSpec(memory_space=pl.ANY)
SMEM = pl.BlockSpec(memory_space=pltpu.SMEM)
HBM = pl.BlockSpec(memory_space=pltpu.HBM)
F32 = jnp.float32


def call(kernel, out, in_specs, out_specs, scratch=(), flops=1 << 22, nbytes=1 << 23, mib=12, aliases=None):
    return pl.pallas_call(
        kernel,
        out_shape=out,
        in_specs=in_specs,
        out_specs=out_specs,
        scratch_shapes=list(scratch),
        input_output_aliases=aliases or {},
        compiler_params=pltpu.CompilerParams(vmem_limit_bytes=mib << 20),
        cost_estimate=pl.CostEstimate(flops=flops, bytes_accessed=nbytes, transcendentals=0),
    )


def iota(shape, dim):
    return lax.broadcasted_iota(jnp.int32, shape, dim)


def row_slot(k):
    return (k % 8, k >= 8) if k < CH else (8 + (k - CH) % 4, k - CH >= 4)


def sources(state, depth, rotation, diff, mask):
    return [(state, slice(0, CH)), (depth, CH), (rotation, CH + 1), (diff, slice(CH + 2, CH + 2 + LEV))]


def fetch(fields, mask, cuts, land, land_cut, sem):
    copies = [pltpu.make_async_copy(mask.at[land_cut], land, sem.at[0])]
    for src, at in fields:
        lead = (slice(None),) if src.shape[:-2] else ()
        for dst, cut in cuts:
            copies.append(pltpu.make_async_copy(src.at[lead + cut], dst.at[at], sem.at[len(copies)]))
    for copy in copies:
        copy.start()
    for copy in copies:
        copy.wait()


def rows_kernel(lat, state, depth, rotation, diff, mask, rows, edge, land, sem):
    upper = lat[0] == 0
    cut = (pl.ds(pl.multiple_of(jnp.where(upper, ROWS - 8, 0), 8), 8), slice(None))
    fetch(sources(state, depth, rotation, diff, mask), mask, [(edge, cut)], land, cut, sem)
    edge[FIELDS - 1] = land[...].astype(F32)
    mine = (iota((8, COLS), 0) >= 4) == upper
    for k in range(FIELDS):
        slot, flip = row_slot(k)
        if not flip:
            pair = k + (8 if k < CH else 4)
            rows[8 * slot : 8 * slot + 8, :] = jnp.where(mine, edge[k], pltpu.roll(edge[pair], 4, 0))


def put(k, a, b, w, e):
    lane = iota(w.shape, 1)
    own = (lane >= HALO * k) & (lane < HALO * k + HALO)
    w = jnp.where(own, pltpu.roll(a, HALO * k, 1) if k else a, w)
    return w, jnp.where(own, pltpu.roll(b, HALO * k + HALO, 1), e)


LEFT, RIGHT = slice(0, 128), slice(COLS - 128, COLS)


def strips_kernel(state, depth, rotation, diff, mask, west, east, lo, hi, land, sem):
    full = slice(None)
    cuts = [(lo, (full, LEFT)), (hi, (full, RIGHT))]
    fetch(sources(state, depth, rotation, diff, mask), mask, cuts, land, (full, full), sem)
    lo[FIELDS - 1] = land[:, LEFT].astype(F32)
    hi[FIELDS - 1] = land[:, RIGHT].astype(F32)
    w = e = jnp.zeros((ROWS, 128), F32)
    for k in range(FIELDS):
        w, e = put(k, lo[k], hi[k], w, e)
    west[...] = w
    east[...] = e


def corners_kernel(lat, rows, west, east, west_out, east_out):
    got = (iota((8, 128), 0) < 4) == (lat[0] == 0)
    w = e = jnp.zeros((8, 128), F32)
    for k in range(FIELDS):
        slot, flip = row_slot(k)
        a, b = rows[8 * slot : 8 * slot + 8, LEFT], rows[8 * slot : 8 * slot + 8, RIGHT]
        if flip:
            a, b = pltpu.roll(a, 4, 0), pltpu.roll(b, 4, 0)
        w, e = put(k, a, b, w, e)
    west_out[0:ROWS, :] = west[...]
    east_out[0:ROWS, :] = east[...]
    west_out[ROWS:ROWS_X, :] = jnp.where(got, w, 0.0)
    east_out[ROWS:ROWS_X, :] = jnp.where(got, e, 0.0)


def exchange(where, state, statics):
    n = lax.axis_size("lon")
    up = [(i, (i + 1) % n) for i in range(n)]
    down = [((i + 1) % n, i) for i in range(n)]

    def shape(*dims):
        return jax.ShapeDtypeStruct(dims, F32)

    rows = call(
        rows_kernel,
        shape(FIELDS * 4, COLS),
        [SMEM] + [HBM] * 5,
        VMEM,
        [pltpu.VMEM((FIELDS, 8, COLS), F32), pltpu.VMEM((8, COLS), jnp.int32), pltpu.SemaphoreType.DMA((5,))],
        mib=62,
    )(where, state, *statics)
    rows = lax.ppermute(rows, "lat", [(0, 1), (1, 0)])
    strip = pltpu.VMEM((FIELDS, ROWS, 128), F32)
    west, east = call(
        strips_kernel,
        [shape(ROWS, 128)] * 2,
        [HBM] * 5,
        [VMEM] * 2,
        [strip, strip, pltpu.VMEM((ROWS, COLS), jnp.int32), pltpu.SemaphoreType.DMA((9,))],
        mib=58,
    )(state, *statics)
    west, east = call(corners_kernel, [shape(ROWS_X, 128)] * 2, [SMEM] + [VMEM] * 3, [VMEM] * 2)(
        where, rows, west, east
    )
    return lax.ppermute(east, "lon", up), lax.ppermute(west, "lon", down), rows


def fill_halo(x, lat, from_west, from_east, rows):
    lane = iota((ROWS_X, 128), 1)
    got = (iota((8, COLS), 0) < 4) == (lat[0] == 0)
    w, e = from_west[...], from_east[...]
    for k in range(FIELDS):
        a = pltpu.roll(e, (128 - HALO * k) % 128, 1) if k else e
        x[k, :, COLS:COLS_X] = jnp.where(lane < 64, a, pltpu.roll(w, (124 - HALO * k) % 128, 1))
        j, flip = row_slot(k)
        tile = rows[8 * j : 8 * j + 8, :]
        if flip:
            tile = pltpu.roll(tile, 4, 0)
        x[k, ROWS:ROWS_X, 0:COLS] = jnp.where(got, tile, 0.0)


def tile_at(t):
    return pl.ds(pl.multiple_of(t * 8, 8), 8)


def step(x, static, ub, vb, h2, store, count, tiles, ready):
    sub = iota((8, COLS_X), 0)

    def around(t):
        return tile_at(jnp.where(t == 0, count - 1, t - 1)), tile_at(t), tile_at(jnp.where(t == count - 1, 0, t + 1))

    def north(cur, nxt):
        return pltpu.roll(jnp.where(sub == 0, nxt, cur), 7, 0)

    def south(cur, prv):
        return pltpu.roll(jnp.where(sub == 7, prv, cur), 1, 0)

    def east(cur):
        return pltpu.roll(cur, COLS_X - 1, 1)

    def west(cur):
        return pltpu.roll(cur, 1, 1)

    def sums(t, _):
        c = tile_at(t)
        u = x[1, c, :]
        v = x[1 + LEV, c, :]
        for l in range(1, LEV):
            u = u + x[1 + l, c, :]
            v = v + x[1 + LEV + l, c, :]
        ub[c, :] = east(u) - west(u)
        vb[c, :] = v
        return 0

    ready(0)
    lax.fori_loop(0, count, sums, 0)

    def surface(t, _):
        p, c, n = around(t)
        v = vb[c, :]
        div = ub[c, :] + (north(v, vb[n, :]) - south(v, vb[p, :]))
        h2[c, :] = static[7, c, :] * (x[0, c, :] - (0.25 / LEV) * static[0, c, :] * div)
        return 0

    ready(1)
    lax.fori_loop(0, count, surface, 0)

    def rest(t, _):
        p, c, n = around(t)
        oc = static[7, c, :]
        rot = static[1, c, :]
        h = h2[c, :]
        store(0, c, h)
        px = 0.25 * (east(h) - west(h))
        py = 0.25 * (north(h, h2[n, :]) - south(h, h2[p, :]))
        for l in range(LEV):
            k = static[2 + l, c, :]

            def near(ch):
                q = x[ch, c, :]
                return q, east(q), west(q), north(q, x[ch, n, :]), south(q, x[ch, p, :])

            q, e, w, a, b = near(1 + 2 * LEV + l)
            cx = e - w
            cy = a - b
            c0 = q + k * ((e + w) + (a + b) - 4.0 * q)
            u, e, w, a, b = near(1 + l)
            lap_u = (e + w) + (a + b) - 4.0 * u
            v, e, w, a, b = near(1 + LEV + l)
            lap_v = (e + w) + (a + b) - 4.0 * v
            u2 = oc * (u + rot * v - px - 0.1 * cx + k * lap_u)
            v2 = oc * (v - rot * u - py - 0.1 * cy + k * lap_v)
            store(1 + l, c, u2)
            store(1 + LEV + l, c, v2)
            store(1 + 2 * LEV + l, c, oc * (c0 - 0.05 * (u2 * cx + v2 * cy)))
        return 0

    ready(2)
    lax.fori_loop(0, tiles, rest, 0)


def two_steps(x, static, y, ub, vb, h2, out, ready=lambda stage: None):
    count = x.shape[1] // 8

    def keep(ch, c, value):
        y[ch, c, :] = value

    def give(ch, c, value):
        out[ch, c, :] = value[:, :COLS]

    step(x, static, ub, vb, h2, keep, count, count, ready)
    step(y, static, ub, vb, h2, give, count, count - 1, lambda stage: None)


def step_scratch(rows):
    return [pltpu.VMEM((CH, rows, COLS_X), F32)] + [pltpu.VMEM((rows, COLS_X), F32)] * 3


def own_kernel(where, state, depth, rotation, diff, mask, fw, fe, rows, gate, out, part, x, land, y, ub, vb, h2, sem):
    main = (slice(0, ROWS), slice(0, COLS))

    def fetch_into(i, src, at):
        copy = pltpu.make_async_copy(src, x.at[(at,) + main], sem.at[i])
        copy.start()
        return copy

    flow, heat = slice(1, 1 + 2 * LEV), slice(1 + 2 * LEV, CH)
    now = [fetch_into(0, state.at[flow], flow)]
    soon = [fetch_into(1, state.at[0], 0), fetch_into(2, depth, CH)]
    soon.append(pltpu.make_async_copy(mask, land, sem.at[3]))
    soon[-1].start()
    late = [
        fetch_into(4, state.at[heat], heat),
        fetch_into(5, rotation, CH + 1),
        fetch_into(6, diff, slice(CH + 2, CH + 2 + LEV)),
    ]
    fill_halo(x, where, fw, fe, rows)

    def ready(stage):
        for copy in (now, soon, late)[stage]:
            copy.wait()
        if stage == 1:
            x[(FIELDS - 1,) + main] = land[...].astype(F32)

    two_steps(x, x.at[CH:FIELDS], y, ub, vb, h2, out, ready)
    first = where[1] == 0
    tiles = HALF // 8
    sub = iota((8, COLS_X), 0)

    def body(t, _):
        c, g = tile_at(t), tile_at(t + jnp.where(first, 0, tiles))
        for j in range(CH, FIELDS):
            part[j - CH, c, :] = x[j, g, :]
        return 0

    lax.fori_loop(0, tiles, body, 0)
    for j in range(CH, FIELDS):
        n = x[j, tile_at(jnp.where(first, tiles, 2 * tiles)), :]
        p = x[j, tile_at(jnp.where(first, 2 * tiles, tiles - 1)), :]
        part[j - CH, HALF:HALF_X, :] = jnp.where(sub < 4, n, p)


def own_steps(where, state, statics, halos, gate):
    return call(
        own_kernel,
        [
            jax.ShapeDtypeStruct((CH, ROWS, COLS), F32),
            jax.ShapeDtypeStruct((FIELDS - CH, HALF_X, COLS_X), F32),
        ],
        [SMEM] + [HBM] * 5 + [VMEM] * 3 + [HBM],
        [VMEM] * 2,
        [pltpu.VMEM((FIELDS, ROWS_X, COLS_X), F32), pltpu.VMEM((ROWS, COLS), jnp.int32)]
        + step_scratch(ROWS_X)
        + [pltpu.SemaphoreType.DMA((7,))],
        flops=1 << 28,
        mib=28,
    )(where, state, *statics, *halos, gate)


def control_halo_kernel(fw, fe, rows, out):
    for k in range(8):
        out[k] = rows[8 * k : 8 * k + 8, :]
    for i in range(18):
        out[8 + i // 3, :, 128 * (i % 3) : 128 * (i % 3) + 128] = jnp.zeros((8, 128), F32)
    lane = iota((8, 128), 1)
    for i in range(17):
        r = slice(8 * i, 8 * i + 8)
        s = jnp.where(lane < 64, fw[r, :], pltpu.roll(fe[r, :], 64, 1))
        out[8 + i // 3, :, 128 * (i % 3) : 128 * (i % 3) + 128] = s
    out[14:16] = jnp.zeros((2, 8, COLS), F32)


def send(value, pairs):
    return lax.ppermute(value, "member", pairs)


CHUNKS = 4


def staged(copies, buffer, sem):
    n = CH // CHUNKS
    both = []
    for i, (src, dst) in enumerate(copies):
        for j in range(CHUNKS):
            ch, s = slice(n * j, n * j + n), CHUNKS * i + j
            one = pltpu.make_async_copy(src.at[ch], buffer.at[i, ch], sem.at[2 * s])
            both.append((one, pltpu.make_async_copy(buffer.at[i, ch], dst.at[ch, 0:HALF_X, :], sem.at[2 * s + 1])))
            one.start()
    for one, two in both:
        one.wait()
        two.start()
    for one, two in both:
        two.wait()


STAGE = [pltpu.VMEM((2, CH, HALF_X, COLS), F32), pltpu.SemaphoreType.DMA((4 * CHUNKS,))]


def cut_kernel(where, state, low, top, buffer, sem):
    @pl.when(where[2] == 0)
    def _():
        staged(
            [(state.at[:, 0:HALF_X, :], top), (state.at[:, ROWS - HALF_X : ROWS, :], low)], buffer, sem
        )


def spread_first(where, state):
    shape = jax.ShapeDtypeStruct((CH, HALF_X, COLS), F32)
    low, top = call(cut_kernel, [shape, shape], [SMEM, HBM], [HBM] * 2, STAGE, mib=62)(where, state)
    return low, top, send(top, [(0, 2)]), send(low, [(0, 7)])


def relay_kernel(where, u, v, p1, m1, gate, u_out, v_out, buffer, sem):
    @pl.when(where[2] == 2)
    def _():
        staged([(p1, u_out)], buffer, sem)

    @pl.when(where[2] == 7)
    def _():
        staged([(m1, v_out), (m1, u_out)], buffer, sem)


def known_kernel(where, own, one, three, six, out, sem):
    for member, ref in ((0, own), (1, one), (3, three), (6, six)):

        @pl.when(where[2] == member)
        def _(ref=ref):
            copy = pltpu.make_async_copy(ref, out, sem.at[0])
            copy.start()
            copy.wait()


def spread_rest(where, u, v, p1, m1, halo):
    came = [send(halo, [(0, member)]) for member in (1, 3, 6)]
    known = call(
        known_kernel,
        jax.ShapeDtypeStruct((CH, 8, COLS), F32),
        [SMEM] + [ANY] * 4,
        VMEM,
        [pltpu.SemaphoreType.DMA((1,))],
        mib=8,
    )(where, halo, *came)
    u, v = call(
        relay_kernel, [u, v], [SMEM] + [HBM] * 4 + [ANY], [HBM] * 2, STAGE, mib=40, aliases={1: 0, 2: 1}
    )(where, u, v, p1, m1, known)
    p2 = send(u, [(0, 3), (2, 4), (7, 1)])
    m2 = send(v, [(0, 6), (7, 5)])
    return (v, u, p2, m2), (known, send(known, [(0, 2), (1, 7), (3, 4), (6, 5)]))


HOLDER = ((0, 7), (2,), (1, 3, 4), (5, 6))
HALO_HOLDER = (0, 0, 1, 0, 1, 1, 0, 1)


def control_kernel(where, *refs):
    arrays, halos, (static, out, x, y, ub, vb, h2, near, halo, strip, sem) = refs[:4], refs[4:6], refs[6:]
    first = where[1] == 0
    m = where[2]
    for array, members in zip(arrays, HOLDER):
        for member in members:
            r0, r1 = (0, HALF) if member % 2 == 0 else (8, 0)

            @pl.when(m == member)
            def _(array=array, r0=r0, r1=r1, source=halos[HALO_HOLDER[member]]):
                one = pltpu.make_async_copy(array.at[:, r0 : r0 + HALF, :], x.at[:, 0:HALF, 0:COLS], sem.at[0])
                two = pltpu.make_async_copy(array.at[:, r1 : r1 + 8, :], near, sem.at[1])
                three = pltpu.make_async_copy(source, halo, sem.at[2])
                one.start()
                two.start()
                three.start()
                one.wait()
                two.wait()
                three.wait()

    for i in range(17):
        strip[8 * i : 8 * i + 8, :] = halo[8 + i // 3, :, 128 * (i % 3) : 128 * (i % 3) + 128]

    def margin(k, s):
        lane = iota(s.shape, 1)
        return jnp.where(
            lane < 64, pltpu.roll(s, 64 - HALO * k, 1), pltpu.roll(s, 124 - HALO * k, 1)
        )

    sub = iota((8, COLS), 0)
    inner = (sub < 4) == first
    got = (sub < 4) == (where[0] == 0)
    s_main = strip[pl.ds(pl.multiple_of(jnp.where(first, 0, HALF), 8), HALF), :]
    s_near = strip[pl.ds(pl.multiple_of(jnp.where(first, HALF, HALF - 8), 8), 8), :]
    s_edge = jnp.where(inner[:, :128], s_near, jnp.where(got[:, :128], strip[ROWS:ROWS_X, :], 0.0))
    for k in range(CH):
        x[k, 0:HALF, COLS:COLS_X] = margin(k, s_main)
        x[k, HALF:HALF_X, COLS:COLS_X] = margin(k, s_edge)
        j, flip = row_slot(k)
        tile = halo[j]
        if flip:
            tile = pltpu.roll(tile, 4, 0)
        x[k, HALF:HALF_X, 0:COLS] = jnp.where(inner, near[k], jnp.where(got, tile, 0.0))
    two_steps(x, static, y, ub, vb, h2, out)


def control_steps(where, arrays, halos, static):
    return call(
        control_kernel,
        jax.ShapeDtypeStruct((CH, HALF, COLS), F32),
        [SMEM] + [HBM] * 4 + [ANY] * 2 + [VMEM],
        VMEM,
        [pltpu.VMEM((CH, HALF_X, COLS_X), F32)]
        + step_scratch(HALF_X)
        + [pltpu.VMEM((CH, 8, COLS), F32)] * 2
        + [pltpu.VMEM((ROWS_X, 128), F32), pltpu.SemaphoreType.DMA((3,))],
        flops=1 << 27,
        mib=16,
    )(where, *arrays, *halos, static)


def sums_kernel(other, where, own, control, mask, region, earlier, out, *copy):
    start = HALF // 8 * (where[1] ^ 1 if other else where[1])

    def body(t, carry):
        c, g = tile_at(t), tile_at(t + start)
        acc = None
        for k in range(CH):
            d = own[k, g, :] - control[k, c, :]
            acc = d * d if acc is None else acc + d * d
        oc = mask[g, :].astype(F32)
        cell = oc * acc
        reg = region[g, :]
        new = []
        for r in range(REGIONS):
            hit = reg == r
            s = jnp.where(hit, cell, 0.0)
            n = jnp.where(hit, oc, 0.0)
            new.append(carry[2 * r] + (s[:, :128] + s[:, 128:256] + s[:, 256:]))
            new.append(carry[2 * r + 1] + (n[:, :128] + n[:, 128:256] + n[:, 256:]))
        return tuple(new)

    zero = jnp.zeros((8, 128), F32)
    total = lax.fori_loop(0, HALF // 8, body, (zero,) * (2 * REGIONS))
    lane = iota((8, 128), 1)
    row = zero
    for r in range(REGIONS):
        for j in range(2):
            s = jnp.sum(jnp.sum(total[2 * r + j], axis=0, keepdims=True), axis=1, keepdims=True)
            row = jnp.where(lane == REGIONS * j + r, s, row)
    if other:
        row = row + earlier[...]
        copies, sem = copy
        for i in range(out.shape[0]):
            copies[i] = row
        move = pltpu.make_async_copy(copies, out, sem.at[0])
        move.start()
        move.wait()
    else:
        out[...] = row + earlier[...]


def half_sums(other, where, own, control, mask, region, earlier):
    shape = (32, 8, 128) if other else (8, 128)
    return call(
        functools.partial(sums_kernel, other),
        jax.ShapeDtypeStruct(shape, F32),
        [SMEM] + [VMEM] * 5,
        HBM if other else VMEM,
        [pltpu.VMEM(shape, F32), pltpu.SemaphoreType.DMA((1,))] if other else (),
        mib=4,
    )(where, own, control, mask, region, earlier)


BLOCK = 4


def final_kernel(where, own, mine, theirs, region, parts, target, out, growth, cell):
    @pl.when(pl.program_id(0) == 0)
    def _():
        total = parts[0]
        for i in range(1, 32):
            total = total + parts[i]
        lane = iota((8, 128), 1)
        counts = jnp.where(lane < REGIONS, pltpu.roll(total, 128 - REGIONS, 1), 1.0)
        squares = jnp.where(lane < REGIONS, total, 1.0)
        g = jnp.sqrt(squares / (counts * CH) + EPSILON)
        growth[...] = g[0:1, 0:REGIONS]
        factor = target[...] / g

        def body(t, _):
            c = tile_at(t)
            for j in range(3):
                lanes = slice(128 * j, 128 * j + 128)
                reg = region[c, lanes]
                cell[c, lanes] = jnp.take_along_axis(factor, reg, axis=1, mode="promise_in_bounds")
            return 0

        lax.fori_loop(0, ROWS // 8, body, 0)

    start = HALF // 8 * where[1]
    lead = pl.program_id(0) * BLOCK
    for ref, s in ((mine, start), (theirs, HALF // 8 - start)):

        def body(t, _):
            c, g = tile_at(t), tile_at(t + s)
            f = cell[g, :]
            for k in range(BLOCK):
                q = ref[lead + k, c, :]
                out[k, g, :] = q + f * (own[lead + k, g, :] - q)
            return 0

        lax.fori_loop(0, HALF // 8, body, 0)


def rescale(where, own, mine, theirs, region, parts, target):
    target = jnp.broadcast_to(jnp.pad(target, (0, 128 - REGIONS), constant_values=1.0), (8, 128))

    cut = pl.BlockSpec((BLOCK, ROWS, COLS), lambda i: (i, 0, 0))
    row = pl.BlockSpec((1, REGIONS), lambda i: (0, 0))
    return pl.pallas_call(
        final_kernel,
        grid=(CH // BLOCK,),
        out_shape=[jax.ShapeDtypeStruct((CH, ROWS, COLS), F32), jax.ShapeDtypeStruct((1, REGIONS), F32)],
        in_specs=[SMEM] + [VMEM] * 6,
        out_specs=[cut, row],
        scratch_shapes=[pltpu.VMEM((ROWS, COLS), F32)],
        compiler_params=pltpu.CompilerParams(vmem_limit_bytes=8 << 20),
        cost_estimate=pl.CostEstimate(flops=1 << 22, bytes_accessed=10 << 20, transcendentals=0),
    )(where, own, mine, theirs, region, parts, target)


def per_device(member_state, depth, rotation, diff, mask, region, target):
    state = member_state[0]
    statics = (depth, rotation, diff, mask)
    m = lax.axis_index("member")
    where = jnp.stack([lax.axis_index("lat"), m % 2, m]).astype(jnp.int32)
    first = spread_first(where, state)
    halos = exchange(where, state, statics)
    halo = call(control_halo_kernel, jax.ShapeDtypeStruct((CH, 8, COLS), F32), [VMEM] * 3, VMEM)(*halos)
    arrays, control_halos = spread_rest(where, *first, halo)
    own, static = own_steps(where, state, statics, halos, arrays[1])
    mine = control_steps(where, arrays, control_halos, static)
    theirs = send(mine, [(i, i ^ 1) for i in range(8)])
    parts = half_sums(False, where, own, mine, mask, region, jnp.zeros((8, 128), F32))
    parts = half_sums(True, where, own, theirs, mask, region, parts)
    parts = lax.all_to_all(parts, ("lon", "lat"), 0, 0)
    bred, growth = rescale(where, own, mine, theirs, region, parts, target)
    return bred[None], growth


def solution(mesh):
    return jax.shard_map(
        per_device,
        mesh=mesh,
        in_specs=(
            P("member", None, "lat", "lon"),
            P("lat", "lon"),
            P("lat", "lon"),
            P(None, "lat", "lon"),
            P("lat", "lon"),
            P("lat", "lon"),
            P(),
        ),
        out_specs=(P("member", None, "lat", "lon"), P("member", None)),
        check_vma=False,
    )
```

```python
import functools
import jax
import jax.numpy as jnp
from jax import lax
from jax.experimental import pallas as pl
from jax.experimental.pallas import tpu as pltpu
from jax.sharding import PartitionSpec as P

LEV = 5
CH = 16
FIELDS = 24
REGIONS = 16
ROWS, COLS = 128, 384
ROWS_X, COLS_X = 136, 512
HALF, HALF_X = 64, 72
HALO = 4
EPSILON = 1e-06
VMEM = pl.BlockSpec(memory_space=pltpu.VMEM)
ANY = pl.BlockSpec(memory_space=pl.ANY)
SMEM = pl.BlockSpec(memory_space=pltpu.SMEM)
HBM = pl.BlockSpec(memory_space=pltpu.HBM)
F32 = jnp.float32


def call(kernel, out, in_specs, out_specs, scratch=(), flops=1 << 22, nbytes=1 << 23, mib=12, aliases=None):
    return pl.pallas_call(
        kernel,
        out_shape=out,
        in_specs=in_specs,
        out_specs=out_specs,
        scratch_shapes=list(scratch),
        input_output_aliases=aliases or {},
        compiler_params=pltpu.CompilerParams(vmem_limit_bytes=mib << 20),
        cost_estimate=pl.CostEstimate(flops=flops, bytes_accessed=nbytes, transcendentals=0),
    )


def iota(shape, dim):
    return lax.broadcasted_iota(jnp.int32, shape, dim)


def row_slot(k):
    return (k % 8, k >= 8) if k < CH else (8 + (k - CH) % 4, k - CH >= 4)


def sources(state, depth, rotation, diff, mask):
    return [(state, slice(0, CH)), (depth, CH), (rotation, CH + 1), (diff, slice(CH + 2, CH + 2 + LEV))]


def fetch(fields, mask, cuts, land, land_cut, sem):
    copies = [pltpu.make_async_copy(mask.at[land_cut], land, sem.at[0])]
    for src, at in fields:
        lead = (slice(None),) if src.shape[:-2] else ()
        for dst, cut in cuts:
            copies.append(pltpu.make_async_copy(src.at[lead + cut], dst.at[at], sem.at[len(copies)]))
    for copy in copies:
        copy.start()
    for copy in copies:
        copy.wait()


def rows_kernel(lat, state, depth, rotation, diff, mask, rows, edge, land, sem):
    upper = lat[0] == 0
    cut = (pl.ds(pl.multiple_of(jnp.where(upper, ROWS - 8, 0), 8), 8), slice(None))
    fetch(sources(state, depth, rotation, diff, mask), mask, [(edge, cut)], land, cut, sem)
    edge[FIELDS - 1] = land[...].astype(F32)
    mine = (iota((8, COLS), 0) >= 4) == upper
    for k in range(FIELDS):
        slot, flip = row_slot(k)
        if not flip:
            pair = k + (8 if k < CH else 4)
            rows[8 * slot : 8 * slot + 8, :] = jnp.where(mine, edge[k], pltpu.roll(edge[pair], 4, 0))


def put(k, a, b, w, e):
    lane = iota(w.shape, 1)
    own = (lane >= HALO * k) & (lane < HALO * k + HALO)
    w = jnp.where(own, pltpu.roll(a, HALO * k, 1) if k else a, w)
    return w, jnp.where(own, pltpu.roll(b, HALO * k + HALO, 1), e)


LEFT, RIGHT = slice(0, 128), slice(COLS - 128, COLS)


def strips_kernel(state, depth, rotation, diff, mask, west, east, lo, hi, land, sem):
    full = slice(None)
    cuts = [(lo, (full, LEFT)), (hi, (full, RIGHT))]
    fetch(sources(state, depth, rotation, diff, mask), mask, cuts, land, (full, full), sem)
    lo[FIELDS - 1] = land[:, LEFT].astype(F32)
    hi[FIELDS - 1] = land[:, RIGHT].astype(F32)
    w = e = jnp.zeros((ROWS, 128), F32)
    for k in range(FIELDS):
        w, e = put(k, lo[k], hi[k], w, e)
    west[...] = w
    east[...] = e


def corners_kernel(lat, rows, west, east, west_out, east_out):
    got = (iota((8, 128), 0) < 4) == (lat[0] == 0)
    w = e = jnp.zeros((8, 128), F32)
    for k in range(FIELDS):
        slot, flip = row_slot(k)
        a, b = rows[8 * slot : 8 * slot + 8, LEFT], rows[8 * slot : 8 * slot + 8, RIGHT]
        if flip:
            a, b = pltpu.roll(a, 4, 0), pltpu.roll(b, 4, 0)
        w, e = put(k, a, b, w, e)
    west_out[0:ROWS, :] = west[...]
    east_out[0:ROWS, :] = east[...]
    west_out[ROWS:ROWS_X, :] = jnp.where(got, w, 0.0)
    east_out[ROWS:ROWS_X, :] = jnp.where(got, e, 0.0)


def exchange(where, state, statics):
    n = lax.axis_size("lon")
    up = [(i, (i + 1) % n) for i in range(n)]
    down = [((i + 1) % n, i) for i in range(n)]

    def shape(*dims):
        return jax.ShapeDtypeStruct(dims, F32)

    rows = call(
        rows_kernel,
        shape(FIELDS * 4, COLS),
        [SMEM] + [HBM] * 5,
        VMEM,
        [pltpu.VMEM((FIELDS, 8, COLS), F32), pltpu.VMEM((8, COLS), jnp.int32), pltpu.SemaphoreType.DMA((5,))],
        mib=62,
    )(where, state, *statics)
    rows = lax.ppermute(rows, "lat", [(0, 1), (1, 0)])
    strip = pltpu.VMEM((FIELDS, ROWS, 128), F32)
    west, east = call(
        strips_kernel,
        [shape(ROWS, 128)] * 2,
        [HBM] * 5,
        [VMEM] * 2,
        [strip, strip, pltpu.VMEM((ROWS, COLS), jnp.int32), pltpu.SemaphoreType.DMA((9,))],
        mib=58,
    )(state, *statics)
    west, east = call(corners_kernel, [shape(ROWS_X, 128)] * 2, [SMEM] + [VMEM] * 3, [VMEM] * 2)(
        where, rows, west, east
    )
    return lax.ppermute(east, "lon", up), lax.ppermute(west, "lon", down), rows


def fill_halo(x, lat, from_west, from_east, rows):
    lane = iota((ROWS_X, 128), 1)
    got = (iota((8, COLS), 0) < 4) == (lat[0] == 0)
    w, e = from_west[...], from_east[...]
    for k in range(FIELDS):
        a = pltpu.roll(e, (128 - HALO * k) % 128, 1) if k else e
        x[k, :, COLS:COLS_X] = jnp.where(lane < 64, a, pltpu.roll(w, (124 - HALO * k) % 128, 1))
        j, flip = row_slot(k)
        tile = rows[8 * j : 8 * j + 8, :]
        if flip:
            tile = pltpu.roll(tile, 4, 0)
        x[k, ROWS:ROWS_X, 0:COLS] = jnp.where(got, tile, 0.0)


def tile_at(t):
    return pl.ds(pl.multiple_of(t * 8, 8), 8)


def step(x, static, ub, vb, h2, store, count, tiles, ready):
    sub = iota((8, COLS_X), 0)

    def around(t):
        return tile_at(jnp.where(t == 0, count - 1, t - 1)), tile_at(t), tile_at(jnp.where(t == count - 1, 0, t + 1))

    def north(cur, nxt):
        return pltpu.roll(jnp.where(sub == 0, nxt, cur), 7, 0)

    def south(cur, prv):
        return pltpu.roll(jnp.where(sub == 7, prv, cur), 1, 0)

    def east(cur):
        return pltpu.roll(cur, COLS_X - 1, 1)

    def west(cur):
        return pltpu.roll(cur, 1, 1)

    def sums(t, _):
        c = tile_at(t)
        u = x[1, c, :]
        v = x[1 + LEV, c, :]
        for l in range(1, LEV):
            u = u + x[1 + l, c, :]
            v = v + x[1 + LEV + l, c, :]
        ub[c, :] = east(u) - west(u)
        vb[c, :] = v
        return 0

    ready(0)
    lax.fori_loop(0, count, sums, 0)

    def surface(t, _):
        p, c, n = around(t)
        v = vb[c, :]
        div = ub[c, :] + (north(v, vb[n, :]) - south(v, vb[p, :]))
        h2[c, :] = static[7, c, :] * (x[0, c, :] - (0.25 / LEV) * static[0, c, :] * div)
        return 0

    ready(1)
    lax.fori_loop(0, count, surface, 0)

    def rest(t, _):
        p, c, n = around(t)
        oc = static[7, c, :]
        rot = static[1, c, :]
        h = h2[c, :]
        store(0, c, h)
        px = 0.25 * (east(h) - west(h))
        py = 0.25 * (north(h, h2[n, :]) - south(h, h2[p, :]))
        for l in range(LEV):
            k = static[2 + l, c, :]

            def near(ch):
                q = x[ch, c, :]
                return q, east(q), west(q), north(q, x[ch, n, :]), south(q, x[ch, p, :])

            q, e, w, a, b = near(1 + 2 * LEV + l)
            cx = e - w
            cy = a - b
            c0 = q + k * ((e + w) + (a + b) - 4.0 * q)
            u, e, w, a, b = near(1 + l)
            lap_u = (e + w) + (a + b) - 4.0 * u
            v, e, w, a, b = near(1 + LEV + l)
            lap_v = (e + w) + (a + b) - 4.0 * v
            u2 = oc * (u + rot * v - px - 0.1 * cx + k * lap_u)
            v2 = oc * (v - rot * u - py - 0.1 * cy + k * lap_v)
            store(1 + l, c, u2)
            store(1 + LEV + l, c, v2)
            store(1 + 2 * LEV + l, c, oc * (c0 - 0.05 * (u2 * cx + v2 * cy)))
        return 0

    ready(2)
    lax.fori_loop(0, tiles, rest, 0)


def two_steps(x, static, y, ub, vb, h2, out, ready=lambda stage: None):
    count = x.shape[1] // 8

    def keep(ch, c, value):
        y[ch, c, :] = value

    def give(ch, c, value):
        out[ch, c, :] = value[:, :COLS]

    step(x, static, ub, vb, h2, keep, count, count, ready)
    step(y, static, ub, vb, h2, give, count, count - 1, lambda stage: None)


def step_scratch(rows):
    return [pltpu.VMEM((CH, rows, COLS_X), F32)] + [pltpu.VMEM((rows, COLS_X), F32)] * 3


def own_kernel(where, state, depth, rotation, diff, mask, fw, fe, rows, gate, out, part, x, land, y, ub, vb, h2, sem):
    main = (slice(0, ROWS), slice(0, COLS))

    def fetch_into(i, src, at):
        copy = pltpu.make_async_copy(src, x.at[(at,) + main], sem.at[i])
        copy.start()
        return copy

    flow, heat = slice(1, 1 + 2 * LEV), slice(1 + 2 * LEV, CH)
    now = [fetch_into(0, state.at[flow], flow)]
    soon = [fetch_into(1, state.at[0], 0), fetch_into(2, depth, CH)]
    soon.append(pltpu.make_async_copy(mask, land, sem.at[3]))
    soon[-1].start()
    late = [
        fetch_into(4, state.at[heat], heat),
        fetch_into(5, rotation, CH + 1),
        fetch_into(6, diff, slice(CH + 2, CH + 2 + LEV)),
    ]
    fill_halo(x, where, fw, fe, rows)

    def ready(stage):
        for copy in (now, soon, late)[stage]:
            copy.wait()
        if stage == 1:
            x[(FIELDS - 1,) + main] = land[...].astype(F32)

    two_steps(x, x.at[CH:FIELDS], y, ub, vb, h2, out, ready)
    first = where[1] == 0
    tiles = HALF // 8
    sub = iota((8, COLS_X), 0)

    def body(t, _):
        c, g = tile_at(t), tile_at(t + jnp.where(first, 0, tiles))
        for j in range(CH, FIELDS):
            part[j - CH, c, :] = x[j, g, :]
        return 0

    lax.fori_loop(0, tiles, body, 0)
    for j in range(CH, FIELDS):
        n = x[j, tile_at(jnp.where(first, tiles, 2 * tiles)), :]
        p = x[j, tile_at(jnp.where(first, 2 * tiles, tiles - 1)), :]
        part[j - CH, HALF:HALF_X, :] = jnp.where(sub < 4, n, p)


def own_steps(where, state, statics, halos, gate):
    return call(
        own_kernel,
        [
            jax.ShapeDtypeStruct((CH, ROWS, COLS), F32),
            jax.ShapeDtypeStruct((FIELDS - CH, HALF_X, COLS_X), F32),
        ],
        [SMEM] + [HBM] * 5 + [VMEM] * 3 + [HBM],
        [VMEM] * 2,
        [pltpu.VMEM((FIELDS, ROWS_X, COLS_X), F32), pltpu.VMEM((ROWS, COLS), jnp.int32)]
        + step_scratch(ROWS_X)
        + [pltpu.SemaphoreType.DMA((7,))],
        flops=1 << 28,
        mib=28,
    )(where, state, *statics, *halos, gate)


def control_halo_kernel(fw, fe, rows, out):
    for k in range(8):
        out[k] = rows[8 * k : 8 * k + 8, :]
    for i in range(18):
        out[8 + i // 3, :, 128 * (i % 3) : 128 * (i % 3) + 128] = jnp.zeros((8, 128), F32)
    lane = iota((8, 128), 1)
    for i in range(17):
        r = slice(8 * i, 8 * i + 8)
        s = jnp.where(lane < 64, fw[r, :], pltpu.roll(fe[r, :], 64, 1))
        out[8 + i // 3, :, 128 * (i % 3) : 128 * (i % 3) + 128] = s
    out[14:16] = jnp.zeros((2, 8, COLS), F32)


def send(value, pairs):
    return lax.ppermute(value, "member", pairs)


CHUNKS = 4


def staged(copies, buffer, sem):
    n = CH // CHUNKS
    both = []
    for i, (src, dst) in enumerate(copies):
        for j in range(CHUNKS):
            ch, s = slice(n * j, n * j + n), CHUNKS * i + j
            one = pltpu.make_async_copy(src.at[ch], buffer.at[i, ch], sem.at[2 * s])
            both.append((one, pltpu.make_async_copy(buffer.at[i, ch], dst.at[ch, 0:HALF_X, :], sem.at[2 * s + 1])))
            one.start()
    for one, two in both:
        one.wait()
        two.start()
    for one, two in both:
        two.wait()


STAGE = [pltpu.VMEM((2, CH, HALF_X, COLS), F32), pltpu.SemaphoreType.DMA((4 * CHUNKS,))]


def cut_kernel(where, state, low, top, buffer, sem):
    @pl.when(where[2] == 0)
    def _():
        staged(
            [(state.at[:, 0:HALF_X, :], top), (state.at[:, ROWS - HALF_X : ROWS, :], low)], buffer, sem
        )


def spread_first(where, state):
    shape = jax.ShapeDtypeStruct((CH, HALF_X, COLS), F32)
    low, top = call(cut_kernel, [shape, shape], [SMEM, HBM], [HBM] * 2, STAGE, mib=62)(where, state)
    return low, top, send(top, [(0, 2)]), send(low, [(0, 7)])


def relay_kernel(where, u, v, p1, m1, gate, u_out, v_out, buffer, sem):
    @pl.when(where[2] == 2)
    def _():
        staged([(p1, u_out)], buffer, sem)

    @pl.when(where[2] == 7)
    def _():
        staged([(m1, v_out), (m1, u_out)], buffer, sem)


def known_kernel(where, own, three, six, out, sem):
    for member, ref in ((0, own), (3, three), (6, six)):

        @pl.when(where[2] == member)
        def _(ref=ref):
            copy = pltpu.make_async_copy(ref, out, sem.at[0])
            copy.start()
            copy.wait()


def spread_rest(where, u, v, p1, m1, halo):
    came = [send(halo, [(0, member)]) for member in (3, 6)]
    known = call(
        known_kernel,
        jax.ShapeDtypeStruct((CH, 8, COLS), F32),
        [SMEM] + [ANY] * 3,
        VMEM,
        [pltpu.SemaphoreType.DMA((1,))],
        mib=8,
    )(where, halo, *came)
    u, v = call(
        relay_kernel, [u, v], [SMEM] + [HBM] * 4 + [ANY], [HBM] * 2, STAGE, mib=40, aliases={1: 0, 2: 1}
    )(where, u, v, p1, m1, known)
    p2 = send(u, [(0, 3), (2, 4), (7, 1)])
    m2 = send(v, [(0, 6), (7, 5)])
    return (v, u, p2, m2), (known, send(known, [(0, 1), (3, 2), (6, 7)]), send(known, [(3, 4), (6, 5)]))


HOLDER = ((0, 7), (2,), (1, 3, 4), (5, 6))
HALO_HOLDER = (0, 1, 1, 0, 2, 2, 0, 1)


def control_kernel(where, *refs):
    arrays, halos, (static, out, x, y, ub, vb, h2, near, halo, strip, sem) = refs[:4], refs[4:7], refs[7:]
    first = where[1] == 0
    m = where[2]
    for array, members in zip(arrays, HOLDER):
        for member in members:
            r0, r1 = (0, HALF) if member % 2 == 0 else (8, 0)

            @pl.when(m == member)
            def _(array=array, r0=r0, r1=r1, source=halos[HALO_HOLDER[member]]):
                one = pltpu.make_async_copy(array.at[:, r0 : r0 + HALF, :], x.at[:, 0:HALF, 0:COLS], sem.at[0])
                two = pltpu.make_async_copy(array.at[:, r1 : r1 + 8, :], near, sem.at[1])
                three = pltpu.make_async_copy(source, halo, sem.at[2])
                one.start()
                two.start()
                three.start()
                one.wait()
                two.wait()
                three.wait()

    for i in range(17):
        strip[8 * i : 8 * i + 8, :] = halo[8 + i // 3, :, 128 * (i % 3) : 128 * (i % 3) + 128]

    def margin(k, s):
        lane = iota(s.shape, 1)
        return jnp.where(
            lane < 64, pltpu.roll(s, 64 - HALO * k, 1), pltpu.roll(s, 124 - HALO * k, 1)
        )

    sub = iota((8, COLS), 0)
    inner = (sub < 4) == first
    got = (sub < 4) == (where[0] == 0)
    s_main = strip[pl.ds(pl.multiple_of(jnp.where(first, 0, HALF), 8), HALF), :]
    s_near = strip[pl.ds(pl.multiple_of(jnp.where(first, HALF, HALF - 8), 8), 8), :]
    s_edge = jnp.where(inner[:, :128], s_near, jnp.where(got[:, :128], strip[ROWS:ROWS_X, :], 0.0))
    for k in range(CH):
        x[k, 0:HALF, COLS:COLS_X] = margin(k, s_main)
        x[k, HALF:HALF_X, COLS:COLS_X] = margin(k, s_edge)
        j, flip = row_slot(k)
        tile = halo[j]
        if flip:
            tile = pltpu.roll(tile, 4, 0)
        x[k, HALF:HALF_X, 0:COLS] = jnp.where(inner, near[k], jnp.where(got, tile, 0.0))
    two_steps(x, static, y, ub, vb, h2, out)


def control_steps(where, arrays, halos, static):
    return call(
        control_kernel,
        jax.ShapeDtypeStruct((CH, HALF, COLS), F32),
        [SMEM] + [HBM] * 4 + [ANY] * 3 + [VMEM],
        VMEM,
        [pltpu.VMEM((CH, HALF_X, COLS_X), F32)]
        + step_scratch(HALF_X)
        + [pltpu.VMEM((CH, 8, COLS), F32)] * 2
        + [pltpu.VMEM((ROWS_X, 128), F32), pltpu.SemaphoreType.DMA((3,))],
        flops=1 << 27,
        mib=16,
    )(where, *arrays, *halos, static)


def sums_kernel(other, where, own, control, mask, region, earlier, out, *copy):
    start = HALF // 8 * (where[1] ^ 1 if other else where[1])

    def body(t, carry):
        c, g = tile_at(t), tile_at(t + start)
        acc = None
        for k in range(CH):
            d = own[k, g, :] - control[k, c, :]
            acc = d * d if acc is None else acc + d * d
        oc = mask[g, :].astype(F32)
        cell = oc * acc
        reg = region[g, :]
        new = []
        for r in range(REGIONS):
            hit = reg == r
            s = jnp.where(hit, cell, 0.0)
            n = jnp.where(hit, oc, 0.0)
            new.append(carry[2 * r] + (s[:, :128] + s[:, 128:256] + s[:, 256:]))
            new.append(carry[2 * r + 1] + (n[:, :128] + n[:, 128:256] + n[:, 256:]))
        return tuple(new)

    zero = jnp.zeros((8, 128), F32)
    total = lax.fori_loop(0, HALF // 8, body, (zero,) * (2 * REGIONS))
    lane = iota((8, 128), 1)
    row = zero
    for r in range(REGIONS):
        for j in range(2):
            s = jnp.sum(jnp.sum(total[2 * r + j], axis=0, keepdims=True), axis=1, keepdims=True)
            row = jnp.where(lane == REGIONS * j + r, s, row)
    if other:
        row = row + earlier[...]
        copies, sem = copy
        for i in range(out.shape[0]):
            copies[i] = row
        move = pltpu.make_async_copy(copies, out, sem.at[0])
        move.start()
        move.wait()
    else:
        out[...] = row + earlier[...]


def half_sums(other, where, own, control, mask, region, earlier):
    shape = (32, 8, 128) if other else (8, 128)
    return call(
        functools.partial(sums_kernel, other),
        jax.ShapeDtypeStruct(shape, F32),
        [SMEM] + [VMEM] * 5,
        HBM if other else VMEM,
        [pltpu.VMEM(shape, F32), pltpu.SemaphoreType.DMA((1,))] if other else (),
        mib=4,
    )(where, own, control, mask, region, earlier)


BLOCK = 4


def final_kernel(where, own, mine, theirs, region, parts, target, out, growth, cell):
    @pl.when(pl.program_id(0) == 0)
    def _():
        total = parts[0]
        for i in range(1, 32):
            total = total + parts[i]
        lane = iota((8, 128), 1)
        counts = jnp.where(lane < REGIONS, pltpu.roll(total, 128 - REGIONS, 1), 1.0)
        squares = jnp.where(lane < REGIONS, total, 1.0)
        g = jnp.sqrt(squares / (counts * CH) + EPSILON)
        growth[...] = g[0:1, 0:REGIONS]
        factor = target[...] / g

        def body(t, _):
            c = tile_at(t)
            for j in range(3):
                lanes = slice(128 * j, 128 * j + 128)
                reg = region[c, lanes]
                cell[c, lanes] = jnp.take_along_axis(factor, reg, axis=1, mode="promise_in_bounds")
            return 0

        lax.fori_loop(0, ROWS // 8, body, 0)

    start = HALF // 8 * where[1]
    lead = pl.program_id(0) * BLOCK
    for ref, s in ((mine, start), (theirs, HALF // 8 - start)):

        def body(t, _):
            c, g = tile_at(t), tile_at(t + s)
            f = cell[g, :]
            for k in range(BLOCK):
                q = ref[lead + k, c, :]
                out[k, g, :] = q + f * (own[lead + k, g, :] - q)
            return 0

        lax.fori_loop(0, HALF // 8, body, 0)


def rescale(where, own, mine, theirs, region, parts, target):
    target = jnp.broadcast_to(jnp.pad(target, (0, 128 - REGIONS), constant_values=1.0), (8, 128))

    cut = pl.BlockSpec((BLOCK, ROWS, COLS), lambda i: (i, 0, 0))
    row = pl.BlockSpec((1, REGIONS), lambda i: (0, 0))
    return pl.pallas_call(
        final_kernel,
        grid=(CH // BLOCK,),
        out_shape=[jax.ShapeDtypeStruct((CH, ROWS, COLS), F32), jax.ShapeDtypeStruct((1, REGIONS), F32)],
        in_specs=[SMEM] + [VMEM] * 6,
        out_specs=[cut, row],
        scratch_shapes=[pltpu.VMEM((ROWS, COLS), F32)],
        compiler_params=pltpu.CompilerParams(vmem_limit_bytes=8 << 20),
        cost_estimate=pl.CostEstimate(flops=1 << 22, bytes_accessed=10 << 20, transcendentals=0),
    )(where, own, mine, theirs, region, parts, target)


def per_device(member_state, depth, rotation, diff, mask, region, target):
    state = member_state[0]
    statics = (depth, rotation, diff, mask)
    m = lax.axis_index("member")
    where = jnp.stack([lax.axis_index("lat"), m % 2, m]).astype(jnp.int32)
    first = spread_first(where, state)
    halos = exchange(where, state, statics)
    halo = call(control_halo_kernel, jax.ShapeDtypeStruct((CH, 8, COLS), F32), [VMEM] * 3, VMEM)(*halos)
    arrays, control_halos = spread_rest(where, *first, halo)
    own, static = own_steps(where, state, statics, halos, arrays[1])
    mine = control_steps(where, arrays, control_halos, static)
    theirs = send(mine, [(i, i ^ 1) for i in range(8)])
    parts = half_sums(False, where, own, mine, mask, region, jnp.zeros((8, 128), F32))
    parts = half_sums(True, where, own, theirs, mask, region, parts)
    parts = lax.all_to_all(parts, ("lon", "lat"), 0, 0)
    bred, growth = rescale(where, own, mine, theirs, region, parts, target)
    return bred[None], growth


def solution(mesh):
    return jax.shard_map(
        per_device,
        mesh=mesh,
        in_specs=(
            P("member", None, "lat", "lon"),
            P("lat", "lon"),
            P("lat", "lon"),
            P(None, "lat", "lon"),
            P("lat", "lon"),
            P("lat", "lon"),
            P(),
        ),
        out_specs=(P("member", None, "lat", "lon"), P("member", None)),
        check_vma=False,
    )
```

```python
import functools
import jax
import jax.numpy as jnp
from jax import lax
from jax.experimental import pallas as pl
from jax.experimental.pallas import tpu as pltpu
from jax.sharding import PartitionSpec as P

LEV = 5
CH = 16
FIELDS = 24
REGIONS = 16
ROWS, COLS = 128, 384
ROWS_X, COLS_X = 136, 512
HALF, HALF_X = 64, 72
HALO = 4
EPSILON = 1e-06
VMEM = pl.BlockSpec(memory_space=pltpu.VMEM)
ANY = pl.BlockSpec(memory_space=pl.ANY)
SMEM = pl.BlockSpec(memory_space=pltpu.SMEM)
HBM = pl.BlockSpec(memory_space=pltpu.HBM)
F32 = jnp.float32


def call(kernel, out, in_specs, out_specs, scratch=(), flops=1 << 22, nbytes=1 << 23, mib=12, aliases=None):
    return pl.pallas_call(
        kernel,
        out_shape=out,
        in_specs=in_specs,
        out_specs=out_specs,
        scratch_shapes=list(scratch),
        input_output_aliases=aliases or {},
        compiler_params=pltpu.CompilerParams(vmem_limit_bytes=mib << 20),
        cost_estimate=pl.CostEstimate(flops=flops, bytes_accessed=nbytes, transcendentals=0),
    )


def iota(shape, dim):
    return lax.broadcasted_iota(jnp.int32, shape, dim)


def row_slot(k):
    return (k % 8, k >= 8) if k < CH else (8 + (k - CH) % 4, k - CH >= 4)


def sources(state, depth, rotation, diff, mask):
    return [(state, slice(0, CH)), (depth, CH), (rotation, CH + 1), (diff, slice(CH + 2, CH + 2 + LEV))]


def fetch(fields, mask, cuts, land, land_cut, sem):
    copies = [pltpu.make_async_copy(mask.at[land_cut], land, sem.at[0])]
    for src, at in fields:
        lead = (slice(None),) if src.shape[:-2] else ()
        for dst, cut in cuts:
            copies.append(pltpu.make_async_copy(src.at[lead + cut], dst.at[at], sem.at[len(copies)]))
    for copy in copies:
        copy.start()
    for copy in copies:
        copy.wait()


def rows_kernel(lat, state, depth, rotation, diff, mask, rows, edge, land, sem):
    upper = lat[0] == 0
    cut = (pl.ds(pl.multiple_of(jnp.where(upper, ROWS - 8, 0), 8), 8), slice(None))
    fetch(sources(state, depth, rotation, diff, mask), mask, [(edge, cut)], land, cut, sem)
    edge[FIELDS - 1] = land[...].astype(F32)
    mine = (iota((8, COLS), 0) >= 4) == upper
    for k in range(FIELDS):
        slot, flip = row_slot(k)
        if not flip:
            pair = k + (8 if k < CH else 4)
            rows[8 * slot : 8 * slot + 8, :] = jnp.where(mine, edge[k], pltpu.roll(edge[pair], 4, 0))


def put(k, a, b, w, e):
    lane = iota(w.shape, 1)
    own = (lane >= HALO * k) & (lane < HALO * k + HALO)
    w = jnp.where(own, pltpu.roll(a, HALO * k, 1) if k else a, w)
    return w, jnp.where(own, pltpu.roll(b, HALO * k + HALO, 1), e)


LEFT, RIGHT = slice(0, 128), slice(COLS - 128, COLS)


def strips_kernel(state, depth, rotation, diff, mask, both, lo, hi, land, sem):
    full = slice(None)
    cuts = [(lo, (full, LEFT)), (hi, (full, RIGHT))]
    fetch(sources(state, depth, rotation, diff, mask), mask, cuts, land, (full, full), sem)
    lo[FIELDS - 1] = land[:, LEFT].astype(F32)
    hi[FIELDS - 1] = land[:, RIGHT].astype(F32)
    w = e = jnp.zeros((ROWS, 128), F32)
    for k in range(FIELDS):
        w, e = put(k, lo[k], hi[k], w, e)
    both[0] = w
    both[1] = e


def corners_kernel(lat, rows, both, west_out, east_out):
    got = (iota((8, 128), 0) < 4) == (lat[0] == 0)
    w = e = jnp.zeros((8, 128), F32)
    for k in range(FIELDS):
        slot, flip = row_slot(k)
        a, b = rows[8 * slot : 8 * slot + 8, LEFT], rows[8 * slot : 8 * slot + 8, RIGHT]
        if flip:
            a, b = pltpu.roll(a, 4, 0), pltpu.roll(b, 4, 0)
        w, e = put(k, a, b, w, e)
    west_out[0:ROWS, :] = both[0]
    east_out[0:ROWS, :] = both[1]
    west_out[ROWS:ROWS_X, :] = jnp.where(got, w, 0.0)
    east_out[ROWS:ROWS_X, :] = jnp.where(got, e, 0.0)


def exchange(where, state, statics):
    n = lax.axis_size("lon")
    up = [(i, (i + 1) % n) for i in range(n)]
    down = [((i + 1) % n, i) for i in range(n)]

    def shape(*dims):
        return jax.ShapeDtypeStruct(dims, F32)

    rows = call(
        rows_kernel,
        shape(FIELDS * 4, COLS),
        [SMEM] + [HBM] * 5,
        VMEM,
        [pltpu.VMEM((FIELDS, 8, COLS), F32), pltpu.VMEM((8, COLS), jnp.int32), pltpu.SemaphoreType.DMA((5,))],
        mib=62,
    )(where, state, *statics)
    rows = lax.ppermute(rows, "lat", [(0, 1), (1, 0)])
    strip = pltpu.VMEM((FIELDS, ROWS, 128), F32)
    both = call(
        strips_kernel,
        shape(2, ROWS, 128),
        [HBM] * 5,
        VMEM,
        [strip, strip, pltpu.VMEM((ROWS, COLS), jnp.int32), pltpu.SemaphoreType.DMA((9,))],
        mib=58,
    )(state, *statics)
    west, east = call(corners_kernel, [shape(ROWS_X, 128)] * 2, [SMEM] + [VMEM] * 2, [VMEM] * 2)(
        where, rows, both
    )
    return lax.ppermute(east, "lon", up), lax.ppermute(west, "lon", down), rows


def fill_halo(x, lat, from_west, from_east, rows):
    lane = iota((ROWS_X, 128), 1)
    got = (iota((8, COLS), 0) < 4) == (lat[0] == 0)
    w, e = from_west[...], from_east[...]
    for k in range(FIELDS):
        a = pltpu.roll(e, (128 - HALO * k) % 128, 1) if k else e
        x[k, :, COLS:COLS_X] = jnp.where(lane < 64, a, pltpu.roll(w, (124 - HALO * k) % 128, 1))
        j, flip = row_slot(k)
        tile = rows[8 * j : 8 * j + 8, :]
        if flip:
            tile = pltpu.roll(tile, 4, 0)
        x[k, ROWS:ROWS_X, 0:COLS] = jnp.where(got, tile, 0.0)


def tile_at(t):
    return pl.ds(pl.multiple_of(t * 8, 8), 8)


def step(x, static, ub, vb, h2, store, count, tiles, ready):
    sub = iota((8, COLS_X), 0)

    def around(t):
        return tile_at(jnp.where(t == 0, count - 1, t - 1)), tile_at(t), tile_at(jnp.where(t == count - 1, 0, t + 1))

    def north(cur, nxt):
        return pltpu.roll(jnp.where(sub == 0, nxt, cur), 7, 0)

    def south(cur, prv):
        return pltpu.roll(jnp.where(sub == 7, prv, cur), 1, 0)

    def east(cur):
        return pltpu.roll(cur, COLS_X - 1, 1)

    def west(cur):
        return pltpu.roll(cur, 1, 1)

    def sums(t, _):
        c = tile_at(t)
        u = x[1, c, :]
        v = x[1 + LEV, c, :]
        for l in range(1, LEV):
            u = u + x[1 + l, c, :]
            v = v + x[1 + LEV + l, c, :]
        ub[c, :] = east(u) - west(u)
        vb[c, :] = v
        return 0

    ready(0)
    lax.fori_loop(0, count, sums, 0)

    def surface(t, _):
        p, c, n = around(t)
        v = vb[c, :]
        div = ub[c, :] + (north(v, vb[n, :]) - south(v, vb[p, :]))
        h2[c, :] = static[7, c, :] * (x[0, c, :] - (0.25 / LEV) * static[0, c, :] * div)
        return 0

    ready(1)
    lax.fori_loop(0, count, surface, 0)

    def rest(t, _):
        p, c, n = around(t)
        oc = static[7, c, :]
        rot = static[1, c, :]
        h = h2[c, :]
        store(0, c, h)
        px = 0.25 * (east(h) - west(h))
        py = 0.25 * (north(h, h2[n, :]) - south(h, h2[p, :]))
        for l in range(LEV):
            k = static[2 + l, c, :]

            def near(ch):
                q = x[ch, c, :]
                return q, east(q), west(q), north(q, x[ch, n, :]), south(q, x[ch, p, :])

            q, e, w, a, b = near(1 + 2 * LEV + l)
            cx = e - w
            cy = a - b
            c0 = q + k * ((e + w) + (a + b) - 4.0 * q)
            u, e, w, a, b = near(1 + l)
            lap_u = (e + w) + (a + b) - 4.0 * u
            v, e, w, a, b = near(1 + LEV + l)
            lap_v = (e + w) + (a + b) - 4.0 * v
            u2 = oc * (u + rot * v - px - 0.1 * cx + k * lap_u)
            v2 = oc * (v - rot * u - py - 0.1 * cy + k * lap_v)
            store(1 + l, c, u2)
            store(1 + LEV + l, c, v2)
            store(1 + 2 * LEV + l, c, oc * (c0 - 0.05 * (u2 * cx + v2 * cy)))
        return 0

    ready(2)
    lax.fori_loop(0, tiles, rest, 0)


def two_steps(x, static, y, ub, vb, h2, out, ready=lambda stage: None):
    count = x.shape[1] // 8

    def keep(ch, c, value):
        y[ch, c, :] = value

    def give(ch, c, value):
        out[ch, c, :] = value[:, :COLS]

    step(x, static, ub, vb, h2, keep, count, count, ready)
    step(y, static, ub, vb, h2, give, count, count - 1, lambda stage: None)


def step_scratch(rows):
    return [pltpu.VMEM((CH, rows, COLS_X), F32)] + [pltpu.VMEM((rows, COLS_X), F32)] * 3


def own_kernel(where, state, depth, rotation, diff, mask, fw, fe, rows, gate, out, part, x, land, y, ub, vb, h2, sem):
    main = (slice(0, ROWS), slice(0, COLS))

    def fetch_into(i, src, at):
        copy = pltpu.make_async_copy(src, x.at[(at,) + main], sem.at[i])
        copy.start()
        return copy

    flow, heat = slice(1, 1 + 2 * LEV), slice(1 + 2 * LEV, CH)
    now = [fetch_into(0, state.at[flow], flow)]
    soon = [fetch_into(1, state.at[0], 0), fetch_into(2, depth, CH)]
    soon.append(pltpu.make_async_copy(mask, land, sem.at[3]))
    soon[-1].start()
    late = [
        fetch_into(4, state.at[heat], heat),
        fetch_into(5, rotation, CH + 1),
        fetch_into(6, diff, slice(CH + 2, CH + 2 + LEV)),
    ]
    fill_halo(x, where, fw, fe, rows)

    def ready(stage):
        for copy in (now, soon, late)[stage]:
            copy.wait()
        if stage == 1:
            x[(FIELDS - 1,) + main] = land[...].astype(F32)

    two_steps(x, x.at[CH:FIELDS], y, ub, vb, h2, out, ready)
    first = where[1] == 0
    tiles = HALF // 8
    sub = iota((8, COLS_X), 0)

    def body(t, _):
        c, g = tile_at(t), tile_at(t + jnp.where(first, 0, tiles))
        for j in range(CH, FIELDS):
            part[j - CH, c, :] = x[j, g, :]
        return 0

    lax.fori_loop(0, tiles, body, 0)
    for j in range(CH, FIELDS):
        n = x[j, tile_at(jnp.where(first, tiles, 2 * tiles)), :]
        p = x[j, tile_at(jnp.where(first, 2 * tiles, tiles - 1)), :]
        part[j - CH, HALF:HALF_X, :] = jnp.where(sub < 4, n, p)


def own_steps(where, state, statics, halos, gate):
    return call(
        own_kernel,
        [
            jax.ShapeDtypeStruct((CH, ROWS, COLS), F32),
            jax.ShapeDtypeStruct((FIELDS - CH, HALF_X, COLS_X), F32),
        ],
        [SMEM] + [HBM] * 5 + [VMEM] * 3 + [HBM],
        [VMEM] * 2,
        [pltpu.VMEM((FIELDS, ROWS_X, COLS_X), F32), pltpu.VMEM((ROWS, COLS), jnp.int32)]
        + step_scratch(ROWS_X)
        + [pltpu.SemaphoreType.DMA((7,))],
        flops=1 << 28,
        mib=28,
    )(where, state, *statics, *halos, gate)


def control_halo_kernel(fw, fe, rows, out):
    for k in range(8):
        out[k] = rows[8 * k : 8 * k + 8, :]
    for i in range(18):
        out[8 + i // 3, :, 128 * (i % 3) : 128 * (i % 3) + 128] = jnp.zeros((8, 128), F32)
    lane = iota((8, 128), 1)
    for i in range(17):
        r = slice(8 * i, 8 * i + 8)
        s = jnp.where(lane < 64, fw[r, :], pltpu.roll(fe[r, :], 64, 1))
        out[8 + i // 3, :, 128 * (i % 3) : 128 * (i % 3) + 128] = s
    out[14:16] = jnp.zeros((2, 8, COLS), F32)


def send(value, pairs):
    return lax.ppermute(value, "member", pairs)


CHUNKS = 4


def staged(copies, buffer, sem):
    n = CH // CHUNKS
    both = []
    for i, (src, dst) in enumerate(copies):
        for j in range(CHUNKS):
            ch, s = slice(n * j, n * j + n), CHUNKS * i + j
            one = pltpu.make_async_copy(src.at[ch], buffer.at[i, ch], sem.at[2 * s])
            both.append((one, pltpu.make_async_copy(buffer.at[i, ch], dst.at[ch, 0:HALF_X, :], sem.at[2 * s + 1])))
            one.start()
    for one, two in both:
        one.wait()
        two.start()
    for one, two in both:
        two.wait()


STAGE = [pltpu.VMEM((2, CH, HALF_X, COLS), F32), pltpu.SemaphoreType.DMA((4 * CHUNKS,))]


def cut_kernel(where, state, low, top, buffer, sem):
    @pl.when(where[2] == 0)
    def _():
        staged(
            [(state.at[:, 0:HALF_X, :], top), (state.at[:, ROWS - HALF_X : ROWS, :], low)], buffer, sem
        )


def spread_first(where, state):
    shape = jax.ShapeDtypeStruct((CH, HALF_X, COLS), F32)
    low, top = call(cut_kernel, [shape, shape], [SMEM, HBM], [HBM] * 2, STAGE, mib=62)(where, state)
    return low, top, send(top, [(0, 2)]), send(low, [(0, 7)])


def relay_kernel(where, u, v, p1, m1, gate, u_out, v_out, buffer, sem):
    @pl.when(where[2] == 2)
    def _():
        staged([(p1, u_out)], buffer, sem)

    @pl.when(where[2] == 7)
    def _():
        staged([(m1, v_out), (m1, u_out)], buffer, sem)


def known_kernel(where, own, three, six, out, sem):
    for member, ref in ((0, own), (3, three), (6, six)):

        @pl.when(where[2] == member)
        def _(ref=ref):
            copy = pltpu.make_async_copy(ref, out, sem.at[0])
            copy.start()
            copy.wait()


def spread_rest(where, u, v, p1, m1, halo):
    came = [send(halo, [(0, member)]) for member in (3, 6)]
    known = call(
        known_kernel,
        jax.ShapeDtypeStruct((CH, 8, COLS), F32),
        [SMEM] + [ANY] * 3,
        VMEM,
        [pltpu.SemaphoreType.DMA((1,))],
        mib=8,
    )(where, halo, *came)
    u, v = call(
        relay_kernel, [u, v], [SMEM] + [HBM] * 4 + [ANY], [HBM] * 2, STAGE, mib=40, aliases={1: 0, 2: 1}
    )(where, u, v, p1, m1, known)
    p2 = send(u, [(0, 3), (2, 4), (7, 1)])
    m2 = send(v, [(0, 6), (7, 5)])
    return (v, u, p2, m2), (known, send(known, [(0, 1), (3, 2), (6, 7)]), send(known, [(3, 4), (6, 5)]))


HOLDER = ((0, 7), (2,), (1, 3, 4), (5, 6))
HALO_HOLDER = (0, 1, 1, 0, 2, 2, 0, 1)


def control_kernel(where, *refs):
    arrays, halos, (static, out, x, y, ub, vb, h2, near, halo, strip, sem) = refs[:4], refs[4:7], refs[7:]
    first = where[1] == 0
    m = where[2]
    for array, members in zip(arrays, HOLDER):
        for member in members:
            r0, r1 = (0, HALF) if member % 2 == 0 else (8, 0)

            @pl.when(m == member)
            def _(array=array, r0=r0, r1=r1, source=halos[HALO_HOLDER[member]]):
                one = pltpu.make_async_copy(array.at[:, r0 : r0 + HALF, :], x.at[:, 0:HALF, 0:COLS], sem.at[0])
                two = pltpu.make_async_copy(array.at[:, r1 : r1 + 8, :], near, sem.at[1])
                three = pltpu.make_async_copy(source, halo, sem.at[2])
                one.start()
                two.start()
                three.start()
                one.wait()
                two.wait()
                three.wait()

    for i in range(17):
        strip[8 * i : 8 * i + 8, :] = halo[8 + i // 3, :, 128 * (i % 3) : 128 * (i % 3) + 128]

    def margin(k, s):
        lane = iota(s.shape, 1)
        return jnp.where(
            lane < 64, pltpu.roll(s, 64 - HALO * k, 1), pltpu.roll(s, 124 - HALO * k, 1)
        )

    sub = iota((8, COLS), 0)
    inner = (sub < 4) == first
    got = (sub < 4) == (where[0] == 0)
    s_main = strip[pl.ds(pl.multiple_of(jnp.where(first, 0, HALF), 8), HALF), :]
    s_near = strip[pl.ds(pl.multiple_of(jnp.where(first, HALF, HALF - 8), 8), 8), :]
    s_edge = jnp.where(inner[:, :128], s_near, jnp.where(got[:, :128], strip[ROWS:ROWS_X, :], 0.0))
    for k in range(CH):
        x[k, 0:HALF, COLS:COLS_X] = margin(k, s_main)
        x[k, HALF:HALF_X, COLS:COLS_X] = margin(k, s_edge)
        j, flip = row_slot(k)
        tile = halo[j]
        if flip:
            tile = pltpu.roll(tile, 4, 0)
        x[k, HALF:HALF_X, 0:COLS] = jnp.where(inner, near[k], jnp.where(got, tile, 0.0))
    two_steps(x, static, y, ub, vb, h2, out)


def control_steps(where, arrays, halos, static):
    return call(
        control_kernel,
        jax.ShapeDtypeStruct((CH, HALF, COLS), F32),
        [SMEM] + [HBM] * 4 + [ANY] * 3 + [VMEM],
        VMEM,
        [pltpu.VMEM((CH, HALF_X, COLS_X), F32)]
        + step_scratch(HALF_X)
        + [pltpu.VMEM((CH, 8, COLS), F32)] * 2
        + [pltpu.VMEM((ROWS_X, 128), F32), pltpu.SemaphoreType.DMA((3,))],
        flops=1 << 27,
        mib=16,
    )(where, *arrays, *halos, static)


def sums_kernel(other, where, own, control, mask, region, earlier, out, *copy):
    start = HALF // 8 * (where[1] ^ 1 if other else where[1])

    def body(t, carry):
        c, g = tile_at(t), tile_at(t + start)
        acc = None
        for k in range(CH):
            d = own[k, g, :] - control[k, c, :]
            acc = d * d if acc is None else acc + d * d
        oc = mask[g, :].astype(F32)
        cell = oc * acc
        reg = region[g, :]
        new = []
        for r in range(REGIONS):
            hit = reg == r
            s = jnp.where(hit, cell, 0.0)
            n = jnp.where(hit, oc, 0.0)
            new.append(carry[2 * r] + (s[:, :128] + s[:, 128:256] + s[:, 256:]))
            new.append(carry[2 * r + 1] + (n[:, :128] + n[:, 128:256] + n[:, 256:]))
        return tuple(new)

    zero = jnp.zeros((8, 128), F32)
    total = lax.fori_loop(0, HALF // 8, body, (zero,) * (2 * REGIONS))
    lane = iota((8, 128), 1)
    row = zero
    for r in range(REGIONS):
        for j in range(2):
            s = jnp.sum(jnp.sum(total[2 * r + j], axis=0, keepdims=True), axis=1, keepdims=True)
            row = jnp.where(lane == REGIONS * j + r, s, row)
    if other:
        row = row + earlier[...]
        copies, sem = copy
        for i in range(out.shape[0]):
            copies[i] = row
        move = pltpu.make_async_copy(copies, out, sem.at[0])
        move.start()
        move.wait()
    else:
        out[...] = row + earlier[...]


def half_sums(other, where, own, control, mask, region, earlier):
    shape = (32, 8, 128) if other else (8, 128)
    return call(
        functools.partial(sums_kernel, other),
        jax.ShapeDtypeStruct(shape, F32),
        [SMEM] + [VMEM] * 5,
        HBM if other else VMEM,
        [pltpu.VMEM(shape, F32), pltpu.SemaphoreType.DMA((1,))] if other else (),
        mib=4,
    )(where, own, control, mask, region, earlier)


BLOCK = 2


def final_kernel(where, own, mine, theirs, region, parts, target, out, growth, cell):
    @pl.when(pl.program_id(0) == 0)
    def _():
        total = parts[0]
        for i in range(1, 32):
            total = total + parts[i]
        lane = iota((8, 128), 1)
        counts = jnp.where(lane < REGIONS, pltpu.roll(total, 128 - REGIONS, 1), 1.0)
        squares = jnp.where(lane < REGIONS, total, 1.0)
        g = jnp.sqrt(squares / (counts * CH) + EPSILON)
        growth[...] = g[0:1, 0:REGIONS]
        factor = target[...] / g

        def body(t, _):
            c = tile_at(t)
            for j in range(3):
                lanes = slice(128 * j, 128 * j + 128)
                reg = region[c, lanes]
                cell[c, lanes] = jnp.take_along_axis(factor, reg, axis=1, mode="promise_in_bounds")
            return 0

        lax.fori_loop(0, ROWS // 8, body, 0)

    start = HALF // 8 * where[1]
    lead = pl.program_id(0) * BLOCK
    for ref, s in ((mine, start), (theirs, HALF // 8 - start)):

        def body(t, _):
            c, g = tile_at(t), tile_at(t + s)
            f = cell[g, :]
            for k in range(BLOCK):
                q = ref[lead + k, c, :]
                out[k, g, :] = q + f * (own[lead + k, g, :] - q)
            return 0

        lax.fori_loop(0, HALF // 8, body, 0)


def rescale(where, own, mine, theirs, region, parts, target):
    target = jnp.broadcast_to(jnp.pad(target, (0, 128 - REGIONS), constant_values=1.0), (8, 128))

    cut = pl.BlockSpec((BLOCK, ROWS, COLS), lambda i: (i, 0, 0))
    row = pl.BlockSpec((1, REGIONS), lambda i: (0, 0))
    return pl.pallas_call(
        final_kernel,
        grid=(CH // BLOCK,),
        out_shape=[jax.ShapeDtypeStruct((CH, ROWS, COLS), F32), jax.ShapeDtypeStruct((1, REGIONS), F32)],
        in_specs=[SMEM] + [VMEM] * 6,
        out_specs=[cut, row],
        scratch_shapes=[pltpu.VMEM((ROWS, COLS), F32)],
        compiler_params=pltpu.CompilerParams(vmem_limit_bytes=8 << 20),
        cost_estimate=pl.CostEstimate(flops=1 << 22, bytes_accessed=10 << 20, transcendentals=0),
    )(where, own, mine, theirs, region, parts, target)


def per_device(member_state, depth, rotation, diff, mask, region, target):
    state = member_state[0]
    statics = (depth, rotation, diff, mask)
    m = lax.axis_index("member")
    where = jnp.stack([lax.axis_index("lat"), m % 2, m]).astype(jnp.int32)
    first = spread_first(where, state)
    halos = exchange(where, state, statics)
    halo = call(control_halo_kernel, jax.ShapeDtypeStruct((CH, 8, COLS), F32), [VMEM] * 3, VMEM)(*halos)
    arrays, control_halos = spread_rest(where, *first, halo)
    own, static = own_steps(where, state, statics, halos, arrays[1])
    mine = control_steps(where, arrays, control_halos, static)
    theirs = send(mine, [(i, i ^ 1) for i in range(8)])
    parts = half_sums(False, where, own, mine, mask, region, jnp.zeros((8, 128), F32))
    parts = half_sums(True, where, own, theirs, mask, region, parts)
    parts = lax.all_to_all(parts, ("lon", "lat"), 0, 0)
    bred, growth = rescale(where, own, mine, theirs, region, parts, target)
    return bred[None], growth


def solution(mesh):
    return jax.shard_map(
        per_device,
        mesh=mesh,
        in_specs=(
            P("member", None, "lat", "lon"),
            P("lat", "lon"),
            P("lat", "lon"),
            P(None, "lat", "lon"),
            P("lat", "lon"),
            P("lat", "lon"),
            P(),
        ),
        out_specs=(P("member", None, "lat", "lon"), P("member", None)),
        check_vma=False,
    )
```
